32 devices in a mesh: dp: 16 (over z, y, x), expert: 2 (over core).
Axes of the slice: x: 2, y: 2, z: 4, core: 2. Of those that a mesh axis runs over, the one named last changes fastest.
Arguments:
- tokens: bfloat16 [6144, 4096], P('dp'), may hold values from -8 to 8, as said below
- centroids: bfloat16 [512, 4096], P('expert'), may hold values from -8 to 8, as said below
- prices: float32 [512], P('expert'), may hold values from 0 to 259.9922, as said below
- epsilon: float32 [1], replicated, may hold values from 0.125 to 1, as said below
Outputs:
- final_prices: float32 [512], P('expert')
- best_expert: int32 [6144], P('dp')
- holder: int32 [512], P('expert')
- refreshed: bfloat16 [512, 4096], P('expert')
The draws below stay inside these ranges and needn't reach their ends.
Inputs may be any that keep to these rules, and one draw needn't show every extreme that they name: `tokens`: every entry is a whole number. `centroids`: every entry is a whole number. `prices`: distinct multiples of 1/128. `epsilon`: A multiple of 1/8.
All inputs are finite; a program needn't handle non-finite values.
Results may differ from the reference program's by a relative error of at most 0.001.
Values may be sent and summed in bfloat16 or wider, within the bound.
No kernel may reach another device: no remote copies, remote signals or barrier semaphores. Data moves between devices by JAX's collectives and lax.ppermute only.
A program may use at most 64 MiB of HBM per device.

```python
import jax
import jax.numpy as jnp
from jax import lax

D = 4096
E = 512
ROUNDS = 3
TOKENS = 6144


def draw_tokens(key, part):
    token_key = jax.random.fold_in(key, 3)
    return jax.random.randint(token_key, (TOKENS, D), -4, 5).astype(jnp.bfloat16)


def draw_centroids(key, part):
    centre_key = jax.random.fold_in(key, 5)
    return jax.random.randint(centre_key, (E, D), -4, 5).astype(jnp.bfloat16)


def draw_prices(key, part):
    ranks = jax.random.permutation(jax.random.fold_in(key, 7), E)
    reserved = (ranks >= E - E // 16).astype(jnp.float32)
    return ranks.astype(jnp.float32) * 0.0078125 + 256.0 * reserved


def draw_epsilon(key, part):
    return jax.random.randint(jax.random.fold_in(key, 11), (1,), 1, 9).astype(jnp.float32) * 0.125


def setup_inputs(seed: int = 0) -> dict:
    splits = jax.random.split(jax.random.key(seed), 5)
    tokens = draw_tokens(jax.random.fold_in(splits[4], 71), 0)
    centroids = draw_centroids(jax.random.fold_in(splits[4], 71), 0)
    prices = draw_prices(jax.random.fold_in(splits[4], 71), 0)
    epsilon = draw_epsilon(jax.random.fold_in(splits[4], 71), 0)
    return {"tokens": tokens, "centroids": centroids, "prices": prices, "epsilon": epsilon}


lowest = -1e30
far_index = 1 << 30


def top_two(values, expert_ids):
    best_value = jnp.max(values, axis=0)
    best_index = jnp.min(jnp.where(values == best_value[None, :], expert_ids[:, None], far_index), axis=0)
    second_value = jnp.max(jnp.where(expert_ids[:, None] == best_index[None, :], lowest, values), axis=0)
    return best_value, best_index, second_value


def reference(tokens, centroids, prices, epsilon):
    scores = lax.dot_general(centroids, tokens, (((1,), (1,)), ((), ())), preferred_element_type=jnp.float32) * 0.015625
    expert_ids = jnp.arange(E, dtype=jnp.int32)
    token_ids = jnp.arange(TOKENS, dtype=jnp.int32)
    current = prices
    for auction_step in range(ROUNDS):
        values = scores - current[:, None]
        best_value, best_index, second_value = top_two(values, expert_ids)
        bids_now = best_value - second_value + epsilon[0]
        claims = expert_ids[:, None] == best_index[None, :]
        top_bid = jnp.max(jnp.where(claims, bids_now[None, :], -1.0), axis=1)
        first_token = jnp.min(jnp.where(claims & (bids_now[None, :] == top_bid[:, None]), token_ids[None, :], far_index), axis=1)
        current = current + jnp.maximum(top_bid, 0.0)
        holder = jnp.where(top_bid > 0, first_token, -1).astype(jnp.int32)
    counts = jnp.sum(claims, axis=1).astype(jnp.float32)
    feature_sums = jnp.dot(claims.astype(jnp.bfloat16), tokens, preferred_element_type=jnp.float32)
    refreshed = (0.5 * centroids.astype(jnp.float32) + 0.5 * feature_sums / jnp.maximum(counts, 1.0)[:, None]).astype(jnp.bfloat16)
    return current, best_index, holder, refreshed
```

```python
import functools

import jax
import jax.numpy as jnp
from jax import lax
from jax.experimental import pallas as pl
from jax.experimental.pallas import tpu as pltpu
from jax.sharding import PartitionSpec as P

ROUNDS = 3

lowest = -1e30
far = 1073741824.0
VMEM = pl.BlockSpec(memory_space=pltpu.VMEM)
SMEM = pl.BlockSpec(memory_space=pltpu.SMEM)
ANY = pl.BlockSpec(memory_space=pl.ANY)


def choose(scores, current, eps):
    values = scores - current
    ids = lax.broadcasted_iota(jnp.int32, values.shape, 1).astype(jnp.float32)
    top = jnp.max(values, axis=1, keepdims=True)
    choice = jnp.min(jnp.where(values == top, ids, far), axis=1, keepdims=True)
    claims = ids == choice
    second = jnp.max(jnp.where(claims, lowest, values), axis=1, keepdims=True)
    bid = top - second + eps
    bids = jnp.where(claims, bid, -1.0)
    return choice, claims, bid, bids, jnp.max(bids, axis=0, keepdims=True)


def first_round(scores, prices, epsilon, out):
    raised = choose(scores[...], prices[...], epsilon[0])[4]
    out[...] = jnp.broadcast_to(raised[None], out.shape)


def next_round(scores, prices, epsilon, bids, out, new_prices):
    top_bid = jnp.max(bids[...], axis=0)
    current = prices[...] + jnp.maximum(top_bid, 0.0)
    new_prices[...] = current
    raised = choose(scores[...], current, epsilon[0])[4]
    out[...] = jnp.broadcast_to(raised[None], out.shape)


def last_round(scores, prices, epsilon, bids, base, out, new_prices):
    experts = prices.shape[1]
    rows = scores.shape[0]
    top_bid = jnp.max(bids[...], axis=0)
    current = prices[...] + jnp.maximum(top_bid, 0.0)
    new_prices[...] = current
    choice, claims, bid, spread, raised = choose(scores[...], current, epsilon[0])
    token = (base[0] + lax.broadcasted_iota(jnp.int32, (rows, experts), 0)).astype(jnp.float32)
    first = jnp.min(jnp.where(claims & (spread == raised), token, far), axis=0, keepdims=True)
    count = jnp.sum(claims.astype(jnp.float32), axis=0, keepdims=True)
    wide = out.shape[2] - 3 * experts
    lane = lax.broadcasted_iota(jnp.int32, (rows, wide), 1)
    row = lax.broadcasted_iota(jnp.int32, (rows, wide), 0)
    turned = jnp.sum(jnp.where(lane == row, choice, 0.0), axis=0, keepdims=True)
    line = jnp.concatenate([raised, first, count, turned], axis=1)
    out[...] = jnp.broadcast_to(line[None], out.shape)


def finish(rows, swap, info, place, prices, centroids, *refs):
    columns, (final, holder, block) = refs[:-3], refs[-3:]
    devices = info.shape[0]
    experts = prices.shape[1]
    own = centroids.shape[0]
    raised = info[:, :, :experts]
    top_bid = jnp.max(raised, axis=0)
    final[...] = prices[...] + jnp.maximum(top_bid, 0.0)
    firsts = jnp.where(raised == top_bid[None], info[:, :, experts : 2 * experts], far)
    first = jnp.min(firsts, axis=0)
    holder[...] = jnp.where(top_bid > 0, first, -1.0).astype(jnp.int32)
    counts = jnp.sum(info[:, :, 2 * experts : 3 * experts], axis=0)
    ids = (place[0] + lax.broadcasted_iota(jnp.int32, (own, rows), 0)).astype(jnp.float32)
    total = jnp.zeros((own, sum(c.shape[2] for c in columns)), jnp.float32)
    for n in range(devices):
        hot = jnp.where(ids == info[n, :, 3 * experts : 3 * experts + rows], 1.0, 0.0)
        features = [c[n] for c in columns]
        features = features[0] if len(features) == 1 else jnp.concatenate(features, axis=1)
        total += jnp.dot(
            hot.astype(jnp.bfloat16), features, preferred_element_type=jnp.float32
        )
    if swap:
        half = total.shape[1] // 2
        left, right = total[:, :half], total[:, half:]
        total = jnp.concatenate(
            [jnp.where(place[2] == 0, left, right), jnp.where(place[2] == 0, right, left)], axis=1
        )
    expert_row = (place[0] + lax.broadcasted_iota(jnp.int32, (own, experts), 0))
    lane = lax.broadcasted_iota(jnp.int32, (own, experts), 1)
    mine = jnp.sum(jnp.where(expert_row == lane, counts, 0.0), axis=1, keepdims=True)
    fresh = 0.5 * centroids[...].astype(jnp.float32) + 0.5 * total / jnp.maximum(mine, 1.0)
    fresh = fresh.astype(jnp.bfloat16)
    half = own // 2
    block[0] = fresh[:half]
    block[1] = fresh[half:]


def assemble(plan, base, *refs):
    pieces, out, sem = refs[:-2], refs[-2], refs[-1]
    half, cols = pieces[0].shape[1:]
    copies = []
    for piece, slots in zip(pieces, plan):
        for i, (part, slot) in enumerate(slots):
            col = pl.multiple_of(base[slot] * cols, cols)
            copies.append(
                pltpu.make_async_copy(
                    piece.at[i], out.at[pl.ds(part * half, half), pl.ds(col, cols)], sem.at[len(copies)]
                )
            )
    for copy in copies:
        copy.start()
    for copy in copies:
        copy.wait()


def gather_columns(block, n):
    if n % 4 or block.shape[2] % 128:
        return lax.all_gather(block.reshape(-1, block.shape[2]), "dp", axis=1, tiled=True)
    line = n // 4
    me = lax.axis_index("dp")

    def move(value, step, flip):
        def to(i):
            return (i // 4 + step) % line * 4 + (i % 4 ^ flip)

        return lax.ppermute(value, "dp", [(i, to(i)) for i in range(n)])

    up, down = {0: block}, {0: block}
    got = [(block, [(0, (0, 0)), (1, (0, 0))])]
    one, two = block[0:1], block[1:2]
    near = {0: (one, two)}
    steps = (line - 1) // 2
    for s in range(1, steps + 1):
        up[s] = move(up[s - 1], 1, 0)
        down[s] = move(down[s - 1], -1, 0)
        got.append((up[s], [(0, (-s, 0)), (1, (-s, 0))]))
        got.append((down[s], [(0, (s, 0)), (1, (s, 0))]))
        near[-s] = (up[s][0:1], up[s][1:2])
        near[s] = (down[s][0:1], down[s][1:2])
    if line % 2 == 0:
        s = line // 2
        a = move(near[-(s - 1)][0], 1, 0)
        b = move(near[s - 1][1], -1, 0)
        got.append((a, [(0, (s, 0))]))
        got.append((b, [(1, (s, 0))]))
        near[s] = (a, b)

    def plane(offsets):
        ones = jnp.concatenate([near[o][0] for o in offsets]) if len(offsets) > 1 else near[offsets[0]][0]
        twos = jnp.concatenate([near[o][1] for o in offsets]) if len(offsets) > 1 else near[offsets[0]][1]
        ax, ay = move(ones, 0, 1), move(ones, 0, 2)
        bx, by = move(twos, 0, 1), move(twos, 0, 2)
        ad = move(ax, 0, 2)
        bd = move(by, 0, 1)
        for value, part, flip in ((ax, 0, 1), (ay, 0, 2), (bx, 1, 1), (by, 1, 2), (ad, 0, 3), (bd, 1, 3)):
            got.append((value, [(part, (o, flip)) for o in offsets]))

    plane([0])
    if line > 1:
        plane([o for o in near if o])
    slots = sorted({slot for _, entry in got for _, slot in entry})
    base = jnp.stack([(me // 4 + o) % line * 4 + (me % 4 ^ f) for o, f in slots]).astype(jnp.int32)
    plan = [[(part, slots.index(slot)) for part, slot in entry] for _, entry in got]
    half, cols = block.shape[1:]
    return pl.pallas_call(
        functools.partial(assemble, plan),
        out_shape=jax.ShapeDtypeStruct((2 * half, n * cols), block.dtype),
        in_specs=[SMEM] + [ANY] * len(got),
        out_specs=ANY,
        scratch_shapes=[pltpu.SemaphoreType.DMA((sum(map(len, plan)),))],
        name="assemble",
    )(base, *[value for value, _ in got])


def body(dp, ne, tokens, centroids, prices, epsilon):
    f32 = jnp.float32
    local_tokens, width = tokens.shape
    own = centroids.shape[0]
    experts = own * ne
    devices = dp * ne
    rows = local_tokens // ne
    cols = width // dp
    dp_at, expert_at = lax.axis_index("dp"), lax.axis_index("expert")
    everywhere = ("dp", "expert")

    paired = ne == 2 and (cols // 2) % 128 == 0
    if paired:
        sub = cols // 2
        mine = lax.dynamic_slice_in_dim(tokens, expert_at * rows, rows, 0)
        parcels = mine.reshape(rows, devices, sub).transpose(1, 0, 2)
        columns = lax.all_to_all(parcels, everywhere, 0, 0, tiled=True)
        columns = [columns, lax.ppermute(columns, "expert", [(0, 1), (1, 0)])]
    else:
        parcels = tokens.reshape(local_tokens, dp, cols).transpose(1, 0, 2)
        columns = lax.all_to_all(parcels, "dp", 0, 0, tiled=True)
        columns = [columns.reshape(devices, rows, cols)]

    part = lax.dot_general(
        tokens, centroids, (((1,), (1,)), ((), ())), preferred_element_type=f32
    ) * 0.015625
    if ne == 2:
        theirs = lax.dynamic_slice_in_dim(part, (1 - expert_at) * rows, rows, 0)
        kept = lax.dynamic_slice_in_dim(part, expert_at * rows, rows, 0)
        theirs = lax.ppermute(theirs, "expert", [(0, 1), (1, 0)])
        scores = jnp.concatenate(
            [jnp.where(expert_at == 0, kept, theirs), jnp.where(expert_at == 0, theirs, kept)], axis=1
        )
    else:
        scores = lax.all_to_all(part, "expert", 0, 1, tiled=True)
    current = lax.all_gather(prices, "expert", tiled=True).reshape(1, experts)

    line = jax.ShapeDtypeStruct((1, experts), f32)
    spread = jax.ShapeDtypeStruct((devices, 1, experts), f32)
    bids = pl.pallas_call(
        first_round, out_shape=spread, in_specs=[VMEM, VMEM, SMEM], out_specs=VMEM, name="first_round"
    )(scores, current, epsilon)
    for _ in range(ROUNDS - 2):
        bids = lax.all_to_all(bids, everywhere, 0, 0, tiled=True)
        bids, current = pl.pallas_call(
            next_round,
            out_shape=(spread, line),
            in_specs=[VMEM, VMEM, SMEM, VMEM],
            out_specs=(VMEM, VMEM),
            name="next_round",
        )(scores, current, epsilon, bids)
    bids = lax.all_to_all(bids, everywhere, 0, 0, tiled=True)
    wide = -(-rows // 128) * 128
    base = (dp_at * local_tokens + expert_at * rows).astype(jnp.int32).reshape(1)
    info, current = pl.pallas_call(
        last_round,
        out_shape=(jax.ShapeDtypeStruct((devices, 1, 3 * experts + wide), f32), line),
        in_specs=[VMEM, VMEM, SMEM, VMEM, SMEM],
        out_specs=(VMEM, VMEM),
        name="last_round",
    )(scores, current, epsilon, bids, base)
    info = lax.all_to_all(info, everywhere, 0, 0, tiled=True)

    place = jnp.stack([expert_at * own, dp_at, expert_at]).astype(jnp.int32)
    my_centroids = lax.dynamic_slice_in_dim(centroids, dp_at * cols, cols, 1)
    final, holder, block = pl.pallas_call(
        functools.partial(finish, rows, paired),
        out_shape=(
            line,
            jax.ShapeDtypeStruct((1, experts), jnp.int32),
            jax.ShapeDtypeStruct((2, own // 2, cols), jnp.bfloat16),
        ),
        in_specs=[VMEM, SMEM, VMEM, VMEM] + [VMEM] * len(columns),
        out_specs=(VMEM, VMEM, VMEM),
        name="finish",
        compiler_params=pltpu.CompilerParams(vmem_limit_bytes=40 * 1024 * 1024),
    )(info, place, current, my_centroids, *columns)
    refreshed = gather_columns(block, dp)
    best = lax.dynamic_slice_in_dim(info, dp_at * ne, ne, 0)[:, 0, 3 * experts : 3 * experts + rows]
    best = best.reshape(local_tokens).astype(jnp.int32)
    final = lax.dynamic_slice_in_dim(final[0], expert_at * own, own, 0)
    holder = lax.dynamic_slice_in_dim(holder[0], expert_at * own, own, 0)
    return final, best, holder, refreshed


def solution(mesh):
    placed = (P("dp", None), P("expert", None), P("expert"), P())
    return jax.shard_map(
        functools.partial(body, mesh.shape["dp"], mesh.shape["expert"]),
        mesh=mesh,
        in_specs=placed,
        out_specs=(P("expert"), P("dp"), P("expert"), P("expert", None)),
        check_vma=False,
    )
```

```python
import functools

import jax
import jax.numpy as jnp
from jax import lax
from jax.experimental import pallas as pl
from jax.experimental.pallas import tpu as pltpu
from jax.sharding import PartitionSpec as P

ROUNDS = 3

lowest = -1e30
far = 1073741824.0
VMEM = pl.BlockSpec(memory_space=pltpu.VMEM)
SMEM = pl.BlockSpec(memory_space=pltpu.SMEM)
ANY = pl.BlockSpec(memory_space=pl.ANY)
ROOM = pltpu.CompilerParams(vmem_limit_bytes=32 * 1024 * 1024)


def scored(tokens, centroids, prices):
    scores = lax.dot_general(
        tokens, centroids, (((1,), (1,)), ((), ())), preferred_element_type=jnp.float32
    )
    return scores * 0.015625 - prices


def opening(place, tokens, centroids, prices, kept, sent, mine, *parcels):
    rows, cols = kept.shape[0], mine.shape[1]
    for out, at in ((sent, 1), (kept, 0)):
        row = pl.multiple_of(place[at] * rows, rows)
        out[...] = scored(tokens[pl.ds(row, rows), :], centroids[...], prices[...])
    mine[...] = centroids[:, pl.ds(pl.multiple_of(place[2] * cols, cols), cols)]
    for k, parcel in enumerate(parcels):
        parcel[...] = tokens[:, pl.ds(pl.multiple_of(place[3 + k] * cols, cols), cols)]


def choose(values, eps):
    ids = lax.broadcasted_iota(jnp.int32, values.shape, 1).astype(jnp.float32)
    top = jnp.max(values, axis=1, keepdims=True)
    choice = jnp.min(jnp.where(values == top, ids, far), axis=1, keepdims=True)
    claims = ids == choice
    second = jnp.max(jnp.where(claims, lowest, values), axis=1, keepdims=True)
    bids = jnp.where(claims, top - second + eps, -1.0)
    return choice, claims, bids, jnp.max(bids, axis=0, keepdims=True)


def first_round(place, kept, theirs, epsilon, values, out):
    if theirs is None:
        values[...] = kept[...]
    else:
        own = kept.shape[1]
        swapped = place[0] != 0
        values[:, :own] = jnp.where(swapped, theirs[...], kept[...])
        values[:, own:] = jnp.where(swapped, kept[...], theirs[...])
    raised = choose(values[...], epsilon[0])[-1]
    out[...] = jnp.broadcast_to(raised[None], out.shape)


def first_round_whole(place, kept, epsilon, values, out):
    first_round(place, kept, None, epsilon, values, out)


def next_round(values, before, epsilon, bids, out, after):
    total = before[...] + jnp.maximum(jnp.max(bids[...], axis=0), 0.0)
    after[...] = total
    raised = choose(values[...] - total, epsilon[0])[-1]
    out[...] = jnp.broadcast_to(raised[None], out.shape)


def last_round(values, before, epsilon, bids, base, out, after):
    rows, experts = values.shape
    total = before[...] + jnp.maximum(jnp.max(bids[...], axis=0), 0.0)
    after[...] = total
    choice, claims, spread, raised = choose(values[...] - total, epsilon[0])
    token = (base[0] + lax.broadcasted_iota(jnp.int32, (rows, experts), 0)).astype(jnp.float32)
    first = jnp.min(jnp.where(claims & (spread == raised), token, far), axis=0, keepdims=True)
    count = jnp.sum(claims.astype(jnp.float32), axis=0, keepdims=True)
    wide = out.shape[2] - 3 * experts
    lane = lax.broadcasted_iota(jnp.int32, (rows, wide), 1)
    row = lax.broadcasted_iota(jnp.int32, (rows, wide), 0)
    turned = jnp.sum(jnp.where(lane == row, choice, 0.0), axis=0, keepdims=True)
    line = jnp.concatenate([raised, first, count, turned], axis=1)
    out[...] = jnp.broadcast_to(line[None], out.shape)


def finish(ne, rows, place, info, before, prices, centroids, *refs):
    columns, (final, holder, best, block) = refs[:-4], refs[-4:]
    experts = before.shape[1]
    own = centroids.shape[0]
    start = place[0]
    if own % 128 == 0:
        start = pl.multiple_of(start, 128)
        raised = info[:, :, pl.ds(start, own)]
        firsts = info[:, :, pl.ds(pl.multiple_of(experts + start, 128), own)]
        earlier = before[:, pl.ds(start, own)]
        top_bid = jnp.max(raised, axis=0)
        first = jnp.min(jnp.where(raised == top_bid[None], firsts, far), axis=0)
        final[...] = prices[...] + earlier + jnp.maximum(top_bid, 0.0)
        holder[...] = jnp.where(top_bid > 0, first, -1.0).astype(jnp.int32)
    else:
        raised = info[:, :, :experts]
        top_bid = jnp.max(raised, axis=0)
        firsts = jnp.where(raised == top_bid[None], info[:, :, experts : 2 * experts], far)
        final[...] = before[...] + jnp.maximum(top_bid, 0.0)
        holder[...] = jnp.where(top_bid > 0, jnp.min(firsts, axis=0), -1.0).astype(jnp.int32)
    for c in range(ne):
        best[c] = info[place[1] * ne + c, :, 3 * experts : 3 * experts + rows].astype(jnp.int32)
    ids = (start + lax.broadcasted_iota(jnp.int32, (own, rows), 0)).astype(jnp.float32)
    total = jnp.zeros(block.shape, jnp.float32)
    for k, features in enumerate(columns):
        for c in range(ne):
            chosen = info[place[2 + k] * ne + c, :, 3 * experts : 3 * experts + rows]
            hot = jnp.where(ids == chosen, 1.0, 0.0).astype(jnp.bfloat16)
            total += jnp.dot(
                hot, features[c * rows : (c + 1) * rows, :], preferred_element_type=jnp.float32
            )
    counts = jnp.sum(info[:, :, 2 * experts : 3 * experts], axis=0)
    expert_row = place[0] + lax.broadcasted_iota(jnp.int32, (own, experts), 0)
    lane = lax.broadcasted_iota(jnp.int32, (own, experts), 1)
    counts = jnp.sum(jnp.where(expert_row == lane, counts, 0.0), axis=1, keepdims=True)
    fresh = 0.5 * centroids[...].astype(jnp.float32) + 0.5 * total / jnp.maximum(counts, 1.0)
    block[...] = fresh.astype(block.dtype)


def assemble(plan, base, *refs):
    pieces, out, sem = refs[:-2], refs[-2], refs[-1]
    cols = pieces[0].shape[-1]
    copies = []
    for piece, slots in zip(pieces, plan):
        for i, slot in enumerate(slots):
            col = pl.multiple_of(base[slot] * cols, cols)
            source = piece if len(piece.shape) == 2 else piece.at[i]
            copies.append(
                pltpu.make_async_copy(source, out.at[:, pl.ds(col, cols)], sem.at[len(copies)])
            )
    for copy in copies:
        copy.start()
    for copy in copies:
        copy.wait()


def gather_columns(block, n, ne):
    if ne != 2 or n % 4 or block.shape[1] % 128:
        return lax.all_gather(block, "dp", axis=1, tiled=True)
    line = n // 4
    me, core = lax.axis_index("dp"), lax.axis_index("expert")

    def move(value, steps, flips):
        pairs = []
        for i in range(n):
            for c in range(2):
                to = (i // 4 + steps[c]) % line * 4 + (i % 4 ^ flips[c])
                pairs.append((i * 2 + c, to * 2 + c))
        return lax.ppermute(value, ("dp", "expert"), pairs)

    across, along = (1, 2), (2, 1)
    got, held = [(block, [(0, 0)])], [("a", None)]

    def stack(values):
        values = [v if v.ndim == 3 else v[None] for v in values]
        return values[0] if len(values) == 1 else jnp.concatenate(values)

    def flip(offsets, kinds):
        return [(o, k) for o, k in zip(offsets, kinds)]

    def first_flip(values, offsets):
        value = move(stack(values), (0, 0), across)
        got.append((value, [(o, 1) for o in offsets]))
        return value

    def second_flip(values, slots):
        value = move(stack(values), (0, 0), along)
        got.append((value, [(o, code + 2) for o, code in slots]))

    up, down = move(block, (1, 1), (0, 0)), move(block, (-1, -1), (0, 0))
    plane = first_flip([block], [0])
    second_flip([block, plane], [(0, 0), (0, 1)])
    if line >= 3:
        for s in range(1, (line - 1) // 2 + 1):
            if s > 1:
                up, down = move(up, (1, 1), (0, 0)), move(down, (-1, -1), (0, 0))
            got += [(up, [(-s, 0)]), (down, [(s, 0)])]
            plane = first_flip([up, down], [-s, s])
            second_flip([up, down, plane], [(-s, 0), (s, 0), (-s, 1), (s, 1)])
    if line % 2 == 0:
        s = line // 2
        lasting = move(jnp.where(core == 0, up, down), (1, -1), (0, 0)) if line > 2 else up
        got.append((lasting, [(s, 0)]))
        plane = first_flip([lasting], [s])
        second_flip([lasting, plane], [(s, 0), (s, 1)])

    slots = sorted({slot for _, entry in got for slot in entry})
    one, two = 1 + core, 2 - core
    codes = [0, one, two, 3]
    base = jnp.stack([(me // 4 + o) % line * 4 + (me % 4 ^ codes[f]) for o, f in slots]).astype(jnp.int32)
    plan = [[slots.index(slot) for slot in entry] for _, entry in got]
    own, cols = block.shape
    return pl.pallas_call(
        functools.partial(assemble, plan),
        out_shape=jax.ShapeDtypeStruct((own, n * cols), block.dtype),
        in_specs=[SMEM] + [VMEM] * len(got),
        out_specs=ANY,
        scratch_shapes=[pltpu.SemaphoreType.DMA((sum(map(len, plan)),))],
        compiler_params=ROOM,
        name="assemble",
    )(base, *[value for value, _ in got])


def body(dp, ne, tokens, centroids, prices, epsilon):
    f32 = jnp.float32
    local_tokens, width = tokens.shape
    own = centroids.shape[0]
    experts = own * ne
    devices = dp * ne
    rows = local_tokens // ne
    cols = width // dp
    dp_at, expert_at = lax.axis_index("dp"), lax.axis_index("expert")
    everywhere = ("dp", "expert")
    paired = ne == 2 and dp & (dp - 1) == 0 and dp > 1 and cols % 128 == 0
    swap = [(0, 1), (1, 0)]

    def shape(*sizes, dtype=f32):
        return jax.ShapeDtypeStruct(sizes, dtype)

    line, spread = shape(1, experts), shape(devices, 1, experts)
    at = jnp.stack([expert_at]).astype(jnp.int32)
    if paired:
        half = dp // 2
        theirs = [dp_at ^ (2 * k + expert_at) for k in range(half)]
        place = jnp.stack([expert_at, 1 - expert_at, dp_at] + theirs).astype(jnp.int32)
        kept, sent, mine, *parcels = pl.pallas_call(
            opening,
            out_shape=[shape(rows, own)] * 2
            + [shape(own, cols, dtype=centroids.dtype)]
            + [shape(local_tokens, cols, dtype=tokens.dtype)] * half,
            in_specs=[SMEM, VMEM, VMEM, VMEM],
            out_specs=[VMEM] * (3 + half),
            compiler_params=ROOM,
            name="opening",
        )(place, tokens, centroids, prices.reshape(1, own))
        received = lax.ppermute(sent, "expert", swap)
        values, bids = pl.pallas_call(
            first_round,
            out_shape=(shape(rows, experts), spread),
            in_specs=[SMEM, VMEM, VMEM, SMEM],
            out_specs=(VMEM, VMEM),
            name="first_round",
        )(at, kept, received, epsilon)
        columns = []
        for k, parcel in enumerate(parcels):
            pairs = [
                (i * 2 + c, (i ^ (2 * k + c)) * 2 + c) for i in range(dp) for c in range(2)
            ]
            columns.append(lax.ppermute(parcel, everywhere, pairs))
        columns += [lax.ppermute(c, "expert", swap) for c in columns]
        sources = theirs + [dp_at ^ (2 * k + 1 - expert_at) for k in range(half)]
    else:
        parcels = tokens.reshape(local_tokens, dp, cols).transpose(1, 0, 2)
        columns = lax.all_to_all(parcels, "dp", 0, 0, tiled=True)
        columns = [columns.reshape(dp * local_tokens, cols)[i * local_tokens :][:local_tokens] for i in range(dp)]
        sources = list(range(dp))
        mine = lax.dynamic_slice_in_dim(centroids, dp_at * cols, cols, 1)
        part = lax.dot_general(
            tokens, centroids, (((1,), (1,)), ((), ())), preferred_element_type=f32
        ) * 0.015625 - prices
        part = lax.all_to_all(part, "expert", 0, 1, tiled=True)
        values, bids = pl.pallas_call(
            first_round_whole,
            out_shape=(shape(rows, experts), spread),
            in_specs=[SMEM, VMEM, SMEM],
            out_specs=(VMEM, VMEM),
            name="first_round",
        )(at, part, epsilon)

    total = jnp.zeros((1, experts), f32)
    for _ in range(ROUNDS - 2):
        bids = lax.all_to_all(bids, everywhere, 0, 0, tiled=True)
        bids, total = pl.pallas_call(
            next_round,
            out_shape=(spread, line),
            in_specs=[VMEM, VMEM, SMEM, VMEM],
            out_specs=(VMEM, VMEM),
            name="next_round",
        )(values, total, epsilon, bids)
    bids = lax.all_to_all(bids, everywhere, 0, 0, tiled=True)
    wide = -(-rows // 128) * 128
    base = (dp_at * local_tokens + expert_at * rows).astype(jnp.int32).reshape(1)
    info, total = pl.pallas_call(
        last_round,
        out_shape=(shape(devices, 1, 3 * experts + wide), line),
        in_specs=[VMEM, VMEM, SMEM, VMEM, SMEM],
        out_specs=(VMEM, VMEM),
        name="last_round",
    )(values, total, epsilon, bids, base)
    info = lax.all_to_all(info, everywhere, 0, 0, tiled=True)

    place = jnp.stack([expert_at * own, dp_at] + sources).astype(jnp.int32)
    direct = own % 128 == 0
    listed = own if direct else experts
    final, holder, best, block = pl.pallas_call(
        functools.partial(finish, ne, rows),
        out_shape=(
            shape(1, listed),
            shape(1, listed, dtype=jnp.int32),
            shape(ne, 1, rows, dtype=jnp.int32),
            shape(own, cols, dtype=centroids.dtype),
        ),
        in_specs=[SMEM] + [VMEM] * (4 + len(columns)),
        out_specs=(VMEM, VMEM, VMEM, VMEM),
        compiler_params=ROOM,
        name="finish",
    )(place, info, total, prices.reshape(1, own), mine, *columns)
    refreshed = gather_columns(block, dp, ne)
    if direct:
        final, holder = final[0], holder[0]
    else:
        final = prices + lax.dynamic_slice_in_dim(final[0], expert_at * own, own, 0)
        holder = lax.dynamic_slice_in_dim(holder[0], expert_at * own, own, 0)
    return final, best.reshape(local_tokens), holder, refreshed


def solution(mesh):
    placed = (P("dp", None), P("expert", None), P("expert"), P())
    return jax.shard_map(
        functools.partial(body, mesh.shape["dp"], mesh.shape["expert"]),
        mesh=mesh,
        in_specs=placed,
        out_specs=(P("expert"), P("dp"), P("expert"), P("expert", None)),
        check_vma=False,
    )
```

```python
import functools

import jax
import jax.numpy as jnp
from jax import lax
from jax.experimental import pallas as pl
from jax.experimental.pallas import tpu as pltpu
from jax.sharding import PartitionSpec as P

ROUNDS = 3

lowest = -1e30
far = 1073741824.0
VMEM = pl.BlockSpec(memory_space=pltpu.VMEM)
SMEM = pl.BlockSpec(memory_space=pltpu.SMEM)
ANY = pl.BlockSpec(memory_space=pl.ANY)


def room(mebibytes):
    return pltpu.CompilerParams(vmem_limit_bytes=mebibytes * 1024 * 1024)


def opening(chunks, place, tokens, centroids, prices, kept, sent, mine, *refs):
    parcels, (tok, cen, acc, sem) = refs[:-4], refs[-4:]
    rows, cols = kept.shape[0], mine.shape[1]
    step = tok.shape[1] // chunks
    copies = []
    for i in range(chunks):
        part = pl.ds(i * step, step)
        copies.append((
            pltpu.make_async_copy(tokens.at[:, part], tok.at[:, part], sem.at[0, i]),
            pltpu.make_async_copy(centroids.at[:, part], cen.at[:, part], sem.at[1, i]),
        ))
    for pair in copies:
        pair[0].start()
        pair[1].start()
    for i, pair in enumerate(copies):
        pair[0].wait()
        pair[1].wait()
        part = slice(i * step, (i + 1) * step)
        product = lax.dot_general(
            tok[:, part], cen[:, part], (((1,), (1,)), ((), ())), preferred_element_type=jnp.float32
        )
        if i:
            acc[...] += product
        else:
            acc[...] = product
    for out, at in ((sent, 1), (kept, 0)):
        row = pl.multiple_of(place[at] * rows, rows)
        out[...] = acc[pl.ds(row, rows), :] * 0.015625 - prices[...]
    mine[...] = cen[:, pl.ds(pl.multiple_of(place[2] * cols, cols), cols)]
    for k, parcel in enumerate(parcels):
        parcel[...] = tok[:, pl.ds(pl.multiple_of(place[3 + k] * cols, cols), cols)]


def choose(values, eps):
    ids = lax.broadcasted_iota(jnp.int32, values.shape, 1).astype(jnp.float32)
    top = jnp.max(values, axis=1, keepdims=True)
    choice = jnp.min(jnp.where(values == top, ids, far), axis=1, keepdims=True)
    claims = ids == choice
    second = jnp.max(jnp.where(claims, lowest, values), axis=1, keepdims=True)
    bids = jnp.where(claims, top - second + eps, -1.0)
    return choice, claims, bids, jnp.max(bids, axis=0, keepdims=True)


def first_round(place, kept, theirs, epsilon, values, out):
    if theirs is None:
        values[...] = kept[...]
    else:
        own = kept.shape[1]
        swapped = place[0] != 0
        values[:, :own] = jnp.where(swapped, theirs[...], kept[...])
        values[:, own:] = jnp.where(swapped, kept[...], theirs[...])
    raised = choose(values[...], epsilon[0])[-1]
    out[...] = jnp.broadcast_to(raised[None], out.shape)


def first_round_whole(place, kept, epsilon, values, out):
    first_round(place, kept, None, epsilon, values, out)


def next_round(values, before, epsilon, bids, out, after):
    total = before[...] + jnp.maximum(jnp.max(bids[...], axis=0), 0.0)
    after[...] = total
    raised = choose(values[...] - total, epsilon[0])[-1]
    out[...] = jnp.broadcast_to(raised[None], out.shape)


def last_round(values, before, epsilon, bids, base, largest, out, after):
    rows, experts = values.shape
    total = before[...] + jnp.maximum(jnp.max(bids[...], axis=0), 0.0)
    after[...] = total
    choice, claims, spread, raised = choose(values[...] - total, epsilon[0])
    token = (base[0] + lax.broadcasted_iota(jnp.int32, (rows, experts), 0)).astype(jnp.float32)
    first = jnp.min(jnp.where(claims & (spread == raised), token, far), axis=0, keepdims=True)
    count = jnp.sum(claims.astype(jnp.float32), axis=0, keepdims=True)
    wide = out.shape[2] - 3 * experts
    lane = lax.broadcasted_iota(jnp.int32, (rows, wide), 1)
    row = lax.broadcasted_iota(jnp.int32, (rows, wide), 0)
    turned = jnp.sum(jnp.where(lane == row, choice, 0.0), axis=0, keepdims=True)
    turned = jnp.where(lane[:1] == rows, largest[0], turned)
    line = jnp.concatenate([raised, first, count, turned], axis=1)
    out[...] = jnp.broadcast_to(line[None], out.shape)


def finish(ne, rows, outer, place, info, before, prices, *refs):
    columns, (final, holder, best, counts_out, fits, *sums) = refs[: -5 - 2], refs[-5 - 2 :]
    experts = before.shape[1]
    own = prices.shape[1]
    start = place[0]
    if own % 128 == 0:
        start = pl.multiple_of(start, 128)
        raised = info[:, :, pl.ds(start, own)]
        firsts = info[:, :, pl.ds(pl.multiple_of(experts + start, 128), own)]
        earlier = before[:, pl.ds(start, own)]
        top_bid = jnp.max(raised, axis=0)
        first = jnp.min(jnp.where(raised == top_bid[None], firsts, far), axis=0)
        final[...] = prices[...] + earlier + jnp.maximum(top_bid, 0.0)
        holder[...] = jnp.where(top_bid > 0, first, -1.0).astype(jnp.int32)
    else:
        raised = info[:, :, :experts]
        top_bid = jnp.max(raised, axis=0)
        firsts = jnp.where(raised == top_bid[None], info[:, :, experts : 2 * experts], far)
        final[...] = before[...] + jnp.maximum(top_bid, 0.0)
        holder[...] = jnp.where(top_bid > 0, jnp.min(firsts, axis=0), -1.0).astype(jnp.int32)
    at = 3 * experts
    for c in range(ne):
        best[c] = info[place[1] * ne + c, :, at : at + rows].astype(jnp.int32)
    ids = (start + lax.broadcasted_iota(jnp.int32, (own, rows), 0)).astype(jnp.float32)
    total = jnp.zeros((own, sums[0].shape[1]), jnp.float32)
    for k, features in enumerate(columns):
        for c in range(ne):
            chosen = info[place[2 + k] * ne + c, :, at : at + rows]
            hot = jnp.where(ids == chosen, 1.0, 0.0).astype(jnp.bfloat16)
            total += jnp.dot(
                hot, features[c * rows : (c + 1) * rows, :], preferred_element_type=jnp.float32
            )
    part = own // len(sums)
    for i, out in enumerate(sums):
        out[...] = total[i * part : (i + 1) * part]
    share = info.shape[0] // outer
    parts = [
        jnp.sum(info[i * share : (i + 1) * share, :, 2 * experts : at], axis=0) for i in range(outer)
    ]
    largest = jnp.max(info[:, :, at + rows : at + rows + 1])
    fullest = jnp.max(functools.reduce(jnp.maximum, parts))
    fits[0] = jnp.where(fullest * largest <= 256.0, 1, 0)
    counts = functools.reduce(jnp.add, parts)
    expert_row = place[0] + lax.broadcasted_iota(jnp.int32, (own, experts), 0)
    lane = lax.broadcasted_iota(jnp.int32, (own, experts), 1)
    counts = jnp.sum(jnp.where(expert_row == lane, counts, 0.0), axis=1, keepdims=True)
    counts_out[...] = jnp.broadcast_to(jnp.maximum(counts, 1.0), counts_out.shape)


def blend(row, centroids, counts, *refs):
    sums, out = refs[:-1], refs[-1]
    rows, cols = out.shape
    total = functools.reduce(jnp.add, [s[...].astype(jnp.float32) for s in sums])
    old = centroids[row : row + rows, :].astype(jnp.float32)
    share = counts[row : row + rows, :1]
    out[...] = (0.5 * old + 0.5 * total / share).astype(out.dtype)


def assemble(plan, base, *refs):
    pieces, out, sem = refs[:-2], refs[-2], refs[-1]
    rows, cols = pieces[0].shape[-2:]
    copies = []
    for piece, (row, slots) in zip(pieces, plan):
        for i, slot in enumerate(slots):
            col = pl.multiple_of(base[slot] * cols, cols)
            source = piece if len(piece.shape) == 2 else piece.at[i]
            copies.append(
                pltpu.make_async_copy(
                    source, out.at[pl.ds(row, rows), pl.ds(col, cols)], sem.at[len(copies)]
                )
            )
    for copy in copies:
        copy.start()
    for copy in copies:
        copy.wait()


TURNS = ((0, 1), (2, 1))


def spread_out(dp, inner, wide, sums, mine, counts):
    bits = inner.bit_length() - 1
    member = lax.axis_index("dp") % inner
    core = lax.axis_index("expert")

    def move(value, masks):
        pairs = [(i * 2 + c, (i ^ masks[c]) * 2 + c) for i in range(dp) for c in range(2)]
        return lax.ppermute(value, ("dp", "expert"), pairs)

    parts = len(sums)
    rows, cols = sums[0].shape
    sent = [s if wide else s.astype(jnp.bfloat16) for s in sums]
    other = [move(s, (inner, inner)) for s in sent] if inner < dp else None
    held, pieces, plan, slots = [], [], [], []
    for p in range(parts):
        terms = [sums[p], other[p]] if other else [sums[p]]
        fresh = pl.pallas_call(
            functools.partial(blend, p * rows),
            out_shape=jax.ShapeDtypeStruct((rows, cols), mine.dtype),
            in_specs=[VMEM] * (2 + len(terms)),
            out_specs=VMEM,
            compiler_params=room(4),
            name="blend",
        )(mine, counts, *terms)
        held.append([(fresh[None], [(0, 0)])])
    for stage in range(bits):
        for p in range(parts):
            turns = [(stage + t) % bits for t in TURNS[p]]
            masks = [1 << t for t in turns]
            values = [v for v, _ in held[p]]
            where = [m for _, ms in held[p] for m in ms]
            value = values[0] if len(values) == 1 else jnp.concatenate(values)
            held[p].append((move(value, masks), [(a ^ masks[0], b ^ masks[1]) for a, b in where]))
    for p in range(parts):
        for value, where in held[p]:
            pieces.append(value)
            plan.append((p * rows, [len(slots) + i for i in range(len(where))]))
            slots += where
    base = jnp.stack([member ^ jnp.where(core == 0, a, b) for a, b in slots]).astype(jnp.int32)
    return pl.pallas_call(
        functools.partial(assemble, plan),
        out_shape=jax.ShapeDtypeStruct((parts * rows, inner * cols), mine.dtype),
        in_specs=[SMEM] + [VMEM] * len(pieces),
        out_specs=ANY,
        scratch_shapes=[pltpu.SemaphoreType.DMA((len(slots),))],
        compiler_params=room(16),
        name="assemble",
    )(base, *pieces)


def body(dp, ne, tokens, centroids, prices, epsilon):
    f32 = jnp.float32
    local_tokens, width = tokens.shape
    own = centroids.shape[0]
    experts = own * ne
    devices = dp * ne
    rows = local_tokens // ne
    cols = width // dp
    dp_at, expert_at = lax.axis_index("dp"), lax.axis_index("expert")
    everywhere = ("dp", "expert")
    outer = 2 if ne == 2 and dp % 16 == 0 and dp & (dp - 1) == 0 else 1
    inner = dp // outer
    cols = width // inner
    paired = outer == 2 and cols % 128 == 0 and own % 32 == 0
    swap = [(0, 1), (1, 0)]

    def shape(*sizes, dtype=f32):
        return jax.ShapeDtypeStruct(sizes, dtype)

    line, spread = shape(1, experts), shape(devices, 1, experts)
    at = jnp.stack([expert_at]).astype(jnp.int32)
    if paired:
        half = inner // 2
        chunks = 4
        theirs = [dp_at ^ (2 * k + expert_at) for k in range(half)]
        place = [expert_at, 1 - expert_at, dp_at % inner] + [t % inner for t in theirs]
        place = jnp.stack(place).astype(jnp.int32)
        kept, sent, mine, *parcels = pl.pallas_call(
            functools.partial(opening, chunks),
            out_shape=[shape(rows, own)] * 2
            + [shape(own, cols, dtype=centroids.dtype)]
            + [shape(local_tokens, cols, dtype=tokens.dtype)] * half,
            in_specs=[SMEM, ANY, ANY, VMEM],
            out_specs=[VMEM] * (3 + half),
            scratch_shapes=[
                pltpu.VMEM(tokens.shape, tokens.dtype),
                pltpu.VMEM(centroids.shape, centroids.dtype),
                pltpu.VMEM((local_tokens, own), f32),
                pltpu.SemaphoreType.DMA((2, chunks)),
            ],
            compiler_params=room(48),
            name="opening",
        )(place, tokens, centroids, prices.reshape(1, own))
        received = lax.ppermute(sent, "expert", swap)
        values, bids = pl.pallas_call(
            first_round,
            out_shape=(shape(rows, experts), spread),
            in_specs=[SMEM, VMEM, VMEM, SMEM],
            out_specs=(VMEM, VMEM),
            compiler_params=room(4),
            name="first_round",
        )(at, kept, received, epsilon)
        columns = []
        for k, parcel in enumerate(parcels):
            pairs = [
                (i * 2 + c, (i ^ (2 * k + c)) * 2 + c) for i in range(dp) for c in range(2)
            ]
            columns.append(lax.ppermute(parcel, everywhere, pairs))
        columns += [lax.ppermute(c, "expert", swap) for c in columns]
        sources = theirs + [dp_at ^ (2 * k + 1 - expert_at) for k in range(half)]
    else:
        parcels = tokens.reshape(local_tokens, dp, cols).transpose(1, 0, 2)
        columns = lax.all_to_all(parcels, "dp", 0, 0, tiled=True)
        columns = [columns.reshape(dp * local_tokens, cols)[i * local_tokens :][:local_tokens] for i in range(dp)]
        sources = list(range(dp))
        mine = lax.dynamic_slice_in_dim(centroids, dp_at * cols, cols, 1)
        part = lax.dot_general(
            tokens, centroids, (((1,), (1,)), ((), ())), preferred_element_type=f32
        ) * 0.015625 - prices
        part = lax.all_to_all(part, "expert", 0, 1, tiled=True)
        values, bids = pl.pallas_call(
            first_round_whole,
            out_shape=(shape(rows, experts), spread),
            in_specs=[SMEM, VMEM, SMEM],
            out_specs=(VMEM, VMEM),
            compiler_params=room(4),
            name="first_round",
        )(at, part, epsilon)

    total = jnp.zeros((1, experts), f32)
    for _ in range(ROUNDS - 2):
        bids = lax.all_to_all(bids, everywhere, 0, 0, tiled=True)
        bids, total = pl.pallas_call(
            next_round,
            out_shape=(spread, line),
            in_specs=[VMEM, VMEM, SMEM, VMEM],
            out_specs=(VMEM, VMEM),
            compiler_params=room(4),
            name="next_round",
        )(values, total, epsilon, bids)
    bids = lax.all_to_all(bids, everywhere, 0, 0, tiled=True)
    wide = (rows // 128 + 1) * 128
    largest = jnp.max(jnp.abs(tokens)).astype(f32).reshape(1)
    base = (dp_at * local_tokens + expert_at * rows).astype(jnp.int32).reshape(1)
    info, total = pl.pallas_call(
        last_round,
        out_shape=(shape(devices, 1, 3 * experts + wide), line),
        in_specs=[VMEM, VMEM, SMEM, VMEM, SMEM, SMEM],
        out_specs=(VMEM, VMEM),
        compiler_params=room(8),
        name="last_round",
    )(values, total, epsilon, bids, base, largest)
    info = lax.all_to_all(info, everywhere, 0, 0, tiled=True)

    place = jnp.stack([expert_at * own, dp_at] + sources).astype(jnp.int32)
    direct = own % 128 == 0
    listed = own if direct else experts
    final, holder, best, counts, fits, *sums = pl.pallas_call(
        functools.partial(finish, ne, rows, outer),
        out_shape=(
            shape(1, listed),
            shape(1, listed, dtype=jnp.int32),
            shape(ne, 1, rows, dtype=jnp.int32),
            shape(own, 128),
            shape(1, dtype=jnp.int32),
        )
        + (shape(own // 2, cols),) * 2,
        in_specs=[SMEM] + [VMEM] * (3 + len(columns)),
        out_specs=(VMEM, VMEM, VMEM, VMEM, SMEM, VMEM, VMEM),
        compiler_params=room(16),
        name="finish",
    )(place, info, total, prices.reshape(1, own), *columns)
    if paired:
        spread_as = [functools.partial(spread_out, dp, inner, wide) for wide in (True, False)]
        refreshed = lax.cond(fits[0] > 0, spread_as[1], spread_as[0], sums, mine, counts)
    else:
        sums = jnp.concatenate(sums)
        fresh = 0.5 * mine.astype(f32) + 0.5 * sums / counts[:, :1]
        refreshed = lax.all_gather(fresh.astype(centroids.dtype), "dp", axis=1, tiled=True)
    if direct:
        final, holder = final[0], holder[0]
    else:
        final = prices + lax.dynamic_slice_in_dim(final[0], expert_at * own, own, 0)
        holder = lax.dynamic_slice_in_dim(holder[0], expert_at * own, own, 0)
    return final, best.reshape(local_tokens), holder, refreshed


def solution(mesh):
    placed = (P("dp", None), P("expert", None), P("expert"), P())
    return jax.shard_map(
        functools.partial(body, mesh.shape["dp"], mesh.shape["expert"]),
        mesh=mesh,
        in_specs=placed,
        out_specs=(P("expert"), P("dp"), P("expert"), P("expert", None)),
        check_vma=False,
    )
```

```python
import functools

import jax
import jax.numpy as jnp
from jax import lax
from jax.experimental import pallas as pl
from jax.experimental.pallas import tpu as pltpu
from jax.sharding import PartitionSpec as P

ROUNDS = 3

lowest = -1e30
far = 1073741824.0
VMEM = pl.BlockSpec(memory_space=pltpu.VMEM)
SMEM = pl.BlockSpec(memory_space=pltpu.SMEM)
ANY = pl.BlockSpec(memory_space=pl.ANY)


def room(mebibytes):
    return pltpu.CompilerParams(vmem_limit_bytes=mebibytes * 1024 * 1024)


def opening(chunks, place, tokens, centroids, prices, kept, sent, mine, *refs):
    parcels, (tok, cen, cost, acc, sem) = refs[:-5], refs[-5:]
    rows, cols = kept.shape[0], mine.shape[1]

    def pieces(source, target, which):
        step = source.shape[0] // chunks
        return [
            pltpu.make_async_copy(
                source.at[pl.ds(i * step, step)], target.at[pl.ds(i * step, step)], sem.at[which, i]
            )
            for i in range(chunks)
        ]

    first = pieces(centroids, cen, 0)
    second = pieces(tokens, tok, 1)
    third = pltpu.make_async_copy(prices, cost, sem.at[2, 0])
    for copy in first + second + [third]:
        copy.start()
    for copy in first:
        copy.wait()
    step = tok.shape[0] // chunks
    for i, copy in enumerate(second):
        copy.wait()
        part = slice(i * step, (i + 1) * step)
        acc[part, :] = lax.dot_general(
            tok[part, :], cen[...], (((1,), (1,)), ((), ())), preferred_element_type=jnp.float32
        )
    third.wait()
    for out, at in ((sent, 1), (kept, 0)):
        row = pl.multiple_of(place[at] * rows, rows)
        out[...] = acc[pl.ds(row, rows), :] * 0.015625 - cost[...]
    mine[...] = cen[:, pl.ds(pl.multiple_of(place[2] * cols, cols), cols)]
    for k, parcel in enumerate(parcels):
        parcel[...] = tok[:, pl.ds(pl.multiple_of(place[3 + k] * cols, cols), cols)]


def choose(values, eps):
    ids = lax.broadcasted_iota(jnp.int32, values.shape, 1).astype(jnp.float32)
    top = jnp.max(values, axis=1, keepdims=True)
    choice = jnp.min(jnp.where(values == top, ids, far), axis=1, keepdims=True)
    claims = ids == choice
    second = jnp.max(jnp.where(claims, lowest, values), axis=1, keepdims=True)
    bids = jnp.where(claims, top - second + eps, -1.0)
    return choice, claims, bids, jnp.max(bids, axis=0, keepdims=True)


def first_round(place, kept, theirs, epsilon, values, out):
    if theirs is None:
        values[...] = kept[...]
    else:
        own = kept.shape[1]
        swapped = place[0] != 0
        values[:, :own] = jnp.where(swapped, theirs[...], kept[...])
        values[:, own:] = jnp.where(swapped, kept[...], theirs[...])
    raised = choose(values[...], epsilon[0])[-1]
    out[...] = jnp.broadcast_to(raised[None], out.shape)


def first_round_whole(place, kept, epsilon, values, out):
    first_round(place, kept, None, epsilon, values, out)


def next_round(values, before, epsilon, bids, out, after):
    total = before[...] + jnp.maximum(jnp.max(bids[...], axis=0), 0.0)
    after[...] = total
    raised = choose(values[...] - total, epsilon[0])[-1]
    out[...] = jnp.broadcast_to(raised[None], out.shape)


def last_round(values, before, epsilon, bids, base, largest, out, after):
    rows, experts = values.shape
    total = before[...] + jnp.maximum(jnp.max(bids[...], axis=0), 0.0)
    after[...] = total
    choice, claims, spread, raised = choose(values[...] - total, epsilon[0])
    token = (base[0] + lax.broadcasted_iota(jnp.int32, (rows, experts), 0)).astype(jnp.float32)
    first = jnp.min(jnp.where(claims & (spread == raised), token, far), axis=0, keepdims=True)
    count = jnp.sum(claims.astype(jnp.float32), axis=0, keepdims=True)
    wide = out.shape[2] - 3 * experts
    lane = lax.broadcasted_iota(jnp.int32, (rows, wide), 1)
    row = lax.broadcasted_iota(jnp.int32, (rows, wide), 0)
    turned = jnp.sum(jnp.where(lane == row, choice, 0.0), axis=0, keepdims=True)
    turned = jnp.where(lane[:1] == rows, largest[0], turned)
    line = jnp.concatenate([raised, first, count, turned], axis=1)
    out[...] = jnp.broadcast_to(line[None], out.shape)


def finish(ne, rows, outer, place, info, before, prices, *refs):
    columns, (final, holder, best, counts_out, fits, *sums) = refs[: -5 - 4], refs[-5 - 4 :]
    sums, short = sums[:2], sums[2:]
    experts = before.shape[1]
    own = prices.shape[1]
    start = place[0]
    if own % 128 == 0:
        start = pl.multiple_of(start, 128)
        raised = info[:, :, pl.ds(start, own)]
        firsts = info[:, :, pl.ds(pl.multiple_of(experts + start, 128), own)]
        earlier = before[:, pl.ds(start, own)]
        top_bid = jnp.max(raised, axis=0)
        first = jnp.min(jnp.where(raised == top_bid[None], firsts, far), axis=0)
        final[...] = prices[...] + earlier + jnp.maximum(top_bid, 0.0)
        holder[...] = jnp.where(top_bid > 0, first, -1.0).astype(jnp.int32)
    else:
        raised = info[:, :, :experts]
        top_bid = jnp.max(raised, axis=0)
        firsts = jnp.where(raised == top_bid[None], info[:, :, experts : 2 * experts], far)
        final[...] = before[...] + jnp.maximum(top_bid, 0.0)
        holder[...] = jnp.where(top_bid > 0, jnp.min(firsts, axis=0), -1.0).astype(jnp.int32)
    at = 3 * experts
    for c in range(ne):
        mark = info[place[1] * ne + c, :, at : at + rows]
        best[:, c * rows : (c + 1) * rows] = mark.astype(jnp.int32)
    ids = (start + lax.broadcasted_iota(jnp.int32, (own, rows), 0)).astype(jnp.float32)
    total = jnp.zeros((own, sums[0].shape[1]), jnp.float32)
    for k, features in enumerate(columns):
        for c in range(ne):
            chosen = info[place[2 + k] * ne + c, :, at : at + rows]
            hot = jnp.where(ids == chosen, 1.0, 0.0).astype(jnp.bfloat16)
            total += jnp.dot(
                hot, features[c * rows : (c + 1) * rows, :], preferred_element_type=jnp.float32
            )
    part = own // len(sums)
    for i, (out, brief) in enumerate(zip(sums, short)):
        out[...] = total[i * part : (i + 1) * part]
        brief[...] = total[i * part : (i + 1) * part].astype(brief.dtype)
    share = info.shape[0] // outer
    parts = [
        jnp.sum(info[i * share : (i + 1) * share, :, 2 * experts : at], axis=0) for i in range(outer)
    ]
    largest = jnp.max(info[:, :, at + rows : at + rows + 1])
    fullest = jnp.max(functools.reduce(jnp.maximum, parts))
    fits[0] = jnp.where(fullest * largest <= 256.0, 1, 0)
    counts = functools.reduce(jnp.add, parts)
    expert_row = place[0] + lax.broadcasted_iota(jnp.int32, (own, experts), 0)
    lane = lax.broadcasted_iota(jnp.int32, (own, experts), 1)
    counts = jnp.sum(jnp.where(expert_row == lane, counts, 0.0), axis=1, keepdims=True)
    counts_out[...] = jnp.broadcast_to(jnp.maximum(counts, 1.0), counts_out.shape)


def blend(row, centroids, counts, *refs):
    sums, out = refs[:-1], refs[-1]
    rows, cols = out.shape
    total = functools.reduce(jnp.add, [s[...].astype(jnp.float32) for s in sums])
    old = centroids[row : row + rows, :].astype(jnp.float32)
    share = counts[row : row + rows, :1]
    out[...] = (0.5 * old + 0.5 * total / share).astype(out.dtype)


def assemble(plan, base, *refs):
    pieces, out, sem = refs[: len(plan)], refs[-2], refs[-1]
    rows, cols = pieces[0].shape[-2:]
    copies = []
    for piece, (row, slots) in zip(pieces, plan):
        for i, slot in enumerate(slots):
            col = pl.multiple_of(base[slot] * cols, cols)
            copies.append(
                pltpu.make_async_copy(
                    piece.at[i], out.at[pl.ds(row, rows), pl.ds(col, cols)], sem.at[len(copies)]
                )
            )
    for copy in copies:
        copy.start()
    for copy in copies:
        copy.wait()


TURNS = ((0, 1), (2, 1))


def spread_out(dp, inner, wide, sums, short, mine, counts):
    bits = inner.bit_length() - 1
    member = lax.axis_index("dp") % inner
    core = lax.axis_index("expert")

    def move(value, masks):
        pairs = [(i * 2 + c, (i ^ masks[c]) * 2 + c) for i in range(dp) for c in range(2)]
        return lax.ppermute(value, ("dp", "expert"), pairs)

    parts = len(sums)
    rows, cols = sums[0].shape
    sent = sums if wide else short
    other = [move(s, (inner, inner)) for s in sent] if inner < dp else None
    held = []
    for p in range(parts):
        terms = [sums[p], other[p]] if other else [sums[p]]
        fresh = pl.pallas_call(
            functools.partial(blend, p * rows),
            out_shape=jax.ShapeDtypeStruct((rows, cols), mine.dtype),
            in_specs=[VMEM] * (2 + len(terms)),
            out_specs=VMEM,
            compiler_params=room(4),
            name="blend",
        )(mine, counts, *terms)
        held.append([(fresh[None], [(0, 0)])])

    def join(values):
        return values[0] if len(values) == 1 else jnp.concatenate(values)

    late = [[] for _ in range(parts)]
    for stage in range(bits):
        for p in range(parts):
            masks = [1 << (stage + t) % bits for t in TURNS[p]]

            def onward(entries):
                where = [m for _, ms in entries for m in ms]
                value = move(join([v for v, _ in entries]), masks)
                return value, [(a ^ masks[0], b ^ masks[1]) for a, b in where]

            if stage < bits - 1 or stage < 2:
                held[p].append(onward(held[p]))
            else:
                late[p] = [onward(held[p][:-1]), onward(held[p][-1:])]
    def write(whole, groups):
        pieces, plan, slots = [], [], []
        for p, group in enumerate(groups):
            for value, where in group:
                pieces.append(value)
                plan.append((p * rows, [len(slots) + i for i in range(len(where))]))
                slots += where
        base = jnp.stack([member ^ jnp.where(core == 0, a, b) for a, b in slots]).astype(jnp.int32)
        before = [] if whole is None else [whole]
        return pl.pallas_call(
            functools.partial(assemble, plan),
            out_shape=jax.ShapeDtypeStruct((parts * rows, inner * cols), mine.dtype),
            in_specs=[SMEM] + [VMEM] * len(pieces) + [ANY] * len(before),
            out_specs=ANY,
            scratch_shapes=[pltpu.SemaphoreType.DMA((len(slots),))],
            input_output_aliases={1 + len(pieces): 0} if before else {},
            compiler_params=room(16),
            name="assemble",
        )(base, *pieces, *before)

    whole = write(None, held)
    return write(whole, late) if any(late) else whole


def body(dp, ne, tokens, centroids, prices, epsilon):
    f32 = jnp.float32
    local_tokens, width = tokens.shape
    own = centroids.shape[0]
    experts = own * ne
    devices = dp * ne
    rows = local_tokens // ne
    cols = width // dp
    dp_at, expert_at = lax.axis_index("dp"), lax.axis_index("expert")
    everywhere = ("dp", "expert")
    outer = 2 if ne == 2 and dp % 16 == 0 and dp & (dp - 1) == 0 else 1
    inner = dp // outer
    cols = width // inner
    paired = outer == 2 and cols % 128 == 0 and own % 32 == 0
    swap = [(0, 1), (1, 0)]

    def shape(*sizes, dtype=f32):
        return jax.ShapeDtypeStruct(sizes, dtype)

    line, spread = shape(1, experts), shape(devices, 1, experts)
    at = jnp.stack([expert_at]).astype(jnp.int32)
    if paired:
        half = inner // 2
        chunks = 4
        theirs = [dp_at ^ (2 * k + expert_at) for k in range(half)]
        place = [expert_at, 1 - expert_at, dp_at % inner] + [t % inner for t in theirs]
        place = jnp.stack(place).astype(jnp.int32)
        kept, sent, mine, *parcels = pl.pallas_call(
            functools.partial(opening, chunks),
            out_shape=[shape(rows, own)] * 2
            + [shape(own, cols, dtype=centroids.dtype)]
            + [shape(local_tokens, cols, dtype=tokens.dtype)] * half,
            in_specs=[SMEM, ANY, ANY, ANY],
            out_specs=[VMEM] * (3 + half),
            scratch_shapes=[
                pltpu.VMEM(tokens.shape, tokens.dtype),
                pltpu.VMEM(centroids.shape, centroids.dtype),
                pltpu.VMEM((1, own), f32),
                pltpu.VMEM((local_tokens, own), f32),
                pltpu.SemaphoreType.DMA((3, chunks)),
            ],
            compiler_params=room(52),
            name="opening",
        )(place, tokens, centroids, prices.reshape(1, own))
        received = lax.ppermute(sent, "expert", swap)
        values, bids = pl.pallas_call(
            first_round,
            out_shape=(shape(rows, experts), spread),
            in_specs=[SMEM, VMEM, VMEM, SMEM],
            out_specs=(VMEM, VMEM),
            compiler_params=room(4),
            name="first_round",
        )(at, kept, received, epsilon)
        columns = []
        for k, parcel in enumerate(parcels):
            pairs = [
                (i * 2 + c, (i ^ (2 * k + c)) * 2 + c) for i in range(dp) for c in range(2)
            ]
            columns.append(lax.ppermute(parcel, everywhere, pairs))
        sources = theirs + [dp_at ^ (2 * k + 1 - expert_at) for k in range(half)]
    else:
        parcels = tokens.reshape(local_tokens, dp, cols).transpose(1, 0, 2)
        columns = lax.all_to_all(parcels, "dp", 0, 0, tiled=True)
        columns = [columns.reshape(dp * local_tokens, cols)[i * local_tokens :][:local_tokens] for i in range(dp)]
        sources = list(range(dp))
        mine = lax.dynamic_slice_in_dim(centroids, dp_at * cols, cols, 1)
        part = lax.dot_general(
            tokens, centroids, (((1,), (1,)), ((), ())), preferred_element_type=f32
        ) * 0.015625 - prices
        part = lax.all_to_all(part, "expert", 0, 1, tiled=True)
        values, bids = pl.pallas_call(
            first_round_whole,
            out_shape=(shape(rows, experts), spread),
            in_specs=[SMEM, VMEM, SMEM],
            out_specs=(VMEM, VMEM),
            compiler_params=room(4),
            name="first_round",
        )(at, part, epsilon)

    total = jnp.zeros((1, experts), f32)
    for _ in range(ROUNDS - 2):
        bids = lax.all_to_all(bids, everywhere, 0, 0, tiled=True)
        bids, total = pl.pallas_call(
            next_round,
            out_shape=(spread, line),
            in_specs=[VMEM, VMEM, SMEM, VMEM],
            out_specs=(VMEM, VMEM),
            compiler_params=room(4),
            name="next_round",
        )(values, total, epsilon, bids)
    if paired:
        total, columns = lax.optimization_barrier((total, columns))
        columns += [lax.ppermute(c, "expert", swap) for c in columns]
    bids = lax.all_to_all(bids, everywhere, 0, 0, tiled=True)
    bids, columns = lax.optimization_barrier((bids, columns))
    wide = (rows // 128 + 1) * 128
    largest = jnp.max(jnp.abs(tokens)).astype(f32).reshape(1)
    base = (dp_at * local_tokens + expert_at * rows).astype(jnp.int32).reshape(1)
    info, total = pl.pallas_call(
        last_round,
        out_shape=(shape(devices, 1, 3 * experts + wide), line),
        in_specs=[VMEM, VMEM, SMEM, VMEM, SMEM, SMEM],
        out_specs=(VMEM, VMEM),
        compiler_params=room(8),
        name="last_round",
    )(values, total, epsilon, bids, base, largest)
    info = lax.all_to_all(info, everywhere, 0, 0, tiled=True)

    place = jnp.stack([expert_at * own, dp_at] + sources).astype(jnp.int32)
    direct = own % 128 == 0
    listed = own if direct else experts
    final, holder, best, counts, fits, *sums = pl.pallas_call(
        functools.partial(finish, ne, rows, outer),
        out_shape=(
            shape(1, listed),
            shape(1, listed, dtype=jnp.int32),
            shape(1, local_tokens, dtype=jnp.int32),
            shape(own, 128),
            shape(1, dtype=jnp.int32),
        )
        + (shape(own // 2, cols),) * 2
        + (shape(own // 2, cols, dtype=jnp.bfloat16),) * 2,
        in_specs=[SMEM] + [VMEM] * (3 + len(columns)),
        out_specs=(VMEM, VMEM, VMEM, VMEM, SMEM) + (VMEM,) * 4,
        compiler_params=room(16),
        name="finish",
    )(place, info, total, prices.reshape(1, own), *columns)
    if paired:
        spread_as = [functools.partial(spread_out, dp, inner, wide) for wide in (True, False)]
        refreshed = lax.cond(fits[0] > 0, spread_as[1], spread_as[0], sums[:2], sums[2:], mine, counts)
    else:
        sums = jnp.concatenate(sums[:2])
        fresh = 0.5 * mine.astype(f32) + 0.5 * sums / counts[:, :1]
        refreshed = lax.all_gather(fresh.astype(centroids.dtype), "dp", axis=1, tiled=True)
    if direct:
        final, holder = final[0], holder[0]
    else:
        final = prices + lax.dynamic_slice_in_dim(final[0], expert_at * own, own, 0)
        holder = lax.dynamic_slice_in_dim(holder[0], expert_at * own, own, 0)
    return final, best[0], holder, refreshed


def solution(mesh):
    placed = (P("dp", None), P("expert", None), P("expert"), P())
    return jax.shard_map(
        functools.partial(body, mesh.shape["dp"], mesh.shape["expert"]),
        mesh=mesh,
        in_specs=placed,
        out_specs=(P("expert"), P("dp"), P("expert"), P("expert", None)),
        check_vma=False,
    )
```

```python
import functools

import jax
import jax.numpy as jnp
from jax import lax
from jax.experimental import pallas as pl
from jax.experimental.pallas import tpu as pltpu
from jax.sharding import PartitionSpec as P

ROUNDS = 3

lowest = -1e30
far = 1073741824.0
VMEM = pl.BlockSpec(memory_space=pltpu.VMEM)
SMEM = pl.BlockSpec(memory_space=pltpu.SMEM)
ANY = pl.BlockSpec(memory_space=pl.ANY)


def room(mebibytes):
    return pltpu.CompilerParams(vmem_limit_bytes=mebibytes * 1024 * 1024)


def opening(chunks, place, tokens, centroids, prices, kept, sent, mine, *refs):
    parcels, (tok, cen, acc, sem) = refs[:-4], refs[-4:]
    rows, cols = kept.shape[0], mine.shape[1]
    step = tok.shape[1] // chunks
    copies = []
    for i in range(chunks):
        part = pl.ds(i * step, step)
        copies.append((
            pltpu.make_async_copy(centroids.at[:, part], cen.at[:, part], sem.at[0, i]),
            pltpu.make_async_copy(tokens.at[:, part], tok.at[:, part], sem.at[1, i]),
        ))
    for pair in copies:
        pair[0].start()
        pair[1].start()
    for i, pair in enumerate(copies):
        pair[0].wait()
        pair[1].wait()
        part = slice(i * step, (i + 1) * step)
        product = lax.dot_general(
            tok[:, part], cen[:, part], (((1,), (1,)), ((), ())), preferred_element_type=jnp.float32
        )
        if i:
            acc[...] += product
        else:
            acc[...] = product
    for out, at in ((sent, 1), (kept, 0)):
        row = pl.multiple_of(place[at] * rows, rows)
        out[...] = acc[pl.ds(row, rows), :] * 0.015625 - prices[...]
    mine[...] = cen[:, pl.ds(pl.multiple_of(place[2] * cols, cols), cols)]
    for k, parcel in enumerate(parcels):
        parcel[...] = tok[:, pl.ds(pl.multiple_of(place[3 + k] * cols, cols), cols)]


def choose(values, eps):
    ids = lax.broadcasted_iota(jnp.int32, values.shape, 1).astype(jnp.float32)
    top = jnp.max(values, axis=1, keepdims=True)
    choice = jnp.min(jnp.where(values == top, ids, far), axis=1, keepdims=True)
    claims = ids == choice
    second = jnp.max(jnp.where(claims, lowest, values), axis=1, keepdims=True)
    bids = jnp.where(claims, top - second + eps, -1.0)
    return choice, claims, bids, jnp.max(bids, axis=0, keepdims=True)


def first_round(place, kept, theirs, epsilon, values, out):
    if theirs is None:
        values[...] = kept[...]
    else:
        own = kept.shape[1]
        swapped = place[0] != 0
        values[:, :own] = jnp.where(swapped, theirs[...], kept[...])
        values[:, own:] = jnp.where(swapped, kept[...], theirs[...])
    raised = choose(values[...], epsilon[0])[-1]
    out[...] = jnp.broadcast_to(raised[None], out.shape)


def first_round_whole(place, kept, epsilon, values, out):
    first_round(place, kept, None, epsilon, values, out)


def next_round(values, before, epsilon, bids, out, after):
    total = before[...] + jnp.maximum(jnp.max(bids[...], axis=0), 0.0)
    after[...] = total
    raised = choose(values[...] - total, epsilon[0])[-1]
    out[...] = jnp.broadcast_to(raised[None], out.shape)


def last_round(values, before, epsilon, bids, base, largest, out, after):
    rows, experts = values.shape
    total = before[...] + jnp.maximum(jnp.max(bids[...], axis=0), 0.0)
    after[...] = total
    choice, claims, spread, raised = choose(values[...] - total, epsilon[0])
    token = (base[0] + lax.broadcasted_iota(jnp.int32, (rows, experts), 0)).astype(jnp.float32)
    first = jnp.min(jnp.where(claims & (spread == raised), token, far), axis=0, keepdims=True)
    count = jnp.sum(claims.astype(jnp.float32), axis=0, keepdims=True)
    wide = out.shape[2] - 3 * experts
    lane = lax.broadcasted_iota(jnp.int32, (rows, wide), 1)
    row = lax.broadcasted_iota(jnp.int32, (rows, wide), 0)
    turned = jnp.sum(jnp.where(lane == row, choice, 0.0), axis=0, keepdims=True)
    turned = jnp.where(lane[:1] == rows, largest[0], turned)
    line = jnp.concatenate([raised, first, count, turned], axis=1)
    out[...] = jnp.broadcast_to(line[None], out.shape)


def pass_on(line, parcel, out):
    pass


def released(line, parcel):
    return pl.pallas_call(
        pass_on,
        out_shape=jax.ShapeDtypeStruct(parcel.shape, parcel.dtype),
        in_specs=[ANY, ANY],
        out_specs=ANY,
        input_output_aliases={1: 0},
        compiler_params=room(4),
        cost_estimate=pl.CostEstimate(flops=1000000000, bytes_accessed=4096, transcendentals=0),
        name="released",
    )(line, parcel)


def finish(ne, rows, outer, parts, place, info, before, prices, *refs):
    columns, (final, holder, best, counts_out, fits, *sums) = refs[: -5 - 2 * parts], refs[-5 - 2 * parts :]
    sums, short = sums[:parts], sums[parts:]
    experts = before.shape[1]
    own = prices.shape[1]
    start = place[0]
    if own % 128 == 0:
        start = pl.multiple_of(start, 128)
        raised = info[:, :, pl.ds(start, own)]
        firsts = info[:, :, pl.ds(pl.multiple_of(experts + start, 128), own)]
        earlier = before[:, pl.ds(start, own)]
        top_bid = jnp.max(raised, axis=0)
        first = jnp.min(jnp.where(raised == top_bid[None], firsts, far), axis=0)
        final[...] = prices[...] + earlier + jnp.maximum(top_bid, 0.0)
        holder[...] = jnp.where(top_bid > 0, first, -1.0).astype(jnp.int32)
    else:
        raised = info[:, :, :experts]
        top_bid = jnp.max(raised, axis=0)
        firsts = jnp.where(raised == top_bid[None], info[:, :, experts : 2 * experts], far)
        final[...] = before[...] + jnp.maximum(top_bid, 0.0)
        holder[...] = jnp.where(top_bid > 0, jnp.min(firsts, axis=0), -1.0).astype(jnp.int32)
    at = 3 * experts
    for c in range(ne):
        mark = info[place[1] * ne + c, :, at : at + rows]
        best[:, c * rows : (c + 1) * rows] = mark.astype(jnp.int32)
    ids = (start + lax.broadcasted_iota(jnp.int32, (own, rows), 0)).astype(jnp.float32)
    total = jnp.zeros((own, sums[0].shape[1]), jnp.float32)
    for k, features in enumerate(columns):
        for c in range(ne):
            chosen = info[place[2 + k] * ne + c, :, at : at + rows]
            hot = jnp.where(ids == chosen, 1.0, 0.0).astype(jnp.bfloat16)
            total += jnp.dot(
                hot, features[c * rows : (c + 1) * rows, :], preferred_element_type=jnp.float32
            )
    row = 0
    for out, brief in zip(sums, short):
        piece = total[row : row + out.shape[0]]
        out[...] = piece
        brief[...] = piece.astype(brief.dtype)
        row += out.shape[0]
    share = info.shape[0] // outer
    each = [
        jnp.sum(info[i * share : (i + 1) * share, :, 2 * experts : at], axis=0) for i in range(outer)
    ]
    largest = jnp.max(info[:, :, at + rows : at + rows + 1])
    fullest = jnp.max(functools.reduce(jnp.maximum, each))
    fits[0] = jnp.where(fullest * largest <= 256.0, 1, 0)
    counts = functools.reduce(jnp.add, each)
    expert_row = place[0] + lax.broadcasted_iota(jnp.int32, (own, experts), 0)
    lane = lax.broadcasted_iota(jnp.int32, (own, experts), 1)
    counts = jnp.sum(jnp.where(expert_row == lane, counts, 0.0), axis=1, keepdims=True)
    counts_out[...] = jnp.broadcast_to(jnp.maximum(counts, 1.0), counts_out.shape)


def blend(row, centroids, counts, *refs):
    sums, out = refs[:-1], refs[-1]
    rows, cols = out.shape
    total = functools.reduce(jnp.add, [s[...].astype(jnp.float32) for s in sums])
    old = centroids[row : row + rows, :].astype(jnp.float32)
    share = counts[row : row + rows, :1]
    out[...] = (0.5 * old + 0.5 * total / share).astype(out.dtype)


def assemble(plan, base, *refs):
    pieces, out, sem = refs[: len(plan)], refs[-2], refs[-1]
    cols = pieces[0].shape[-1]
    copies = []
    for piece, (row, slots) in zip(pieces, plan):
        for i, slot in enumerate(slots):
            col = pl.multiple_of(base[slot] * cols, cols)
            copies.append(
                pltpu.make_async_copy(
                    piece.at[i], out.at[pl.ds(row, piece.shape[1]), pl.ds(col, cols)], sem.at[len(copies)]
                )
            )
    for copy in copies:
        copy.start()
    for copy in copies:
        copy.wait()


PARTS = 3
TURNS = ((0, 1), (2, 0), (1, 2))


def spread_out(dp, inner, wide, sums, short, mine, counts):
    bits = inner.bit_length() - 1
    member = lax.axis_index("dp") % inner
    core = lax.axis_index("expert")

    def move(value, masks):
        pairs = [(i * 2 + c, (i ^ masks[c]) * 2 + c) for i in range(dp) for c in range(2)]
        return lax.ppermute(value, ("dp", "expert"), pairs)

    parts = len(sums)
    cols = sums[0].shape[1]
    heights = [s.shape[0] for s in sums]
    tops = [sum(heights[:p]) for p in range(parts)]
    sent = sums if wide else short
    other = [move(s, (inner, inner)) for s in sent] if inner < dp else None
    held = []
    for p in range(parts):
        terms = [sums[p], other[p]] if other else [sums[p]]
        fresh = pl.pallas_call(
            functools.partial(blend, tops[p]),
            out_shape=jax.ShapeDtypeStruct((heights[p], cols), mine.dtype),
            in_specs=[VMEM] * (2 + len(terms)),
            out_specs=VMEM,
            compiler_params=room(4),
            name="blend",
        )(mine, counts, *terms)
        held.append([(fresh[None], [(0, 0)])])

    def join(values):
        return values[0] if len(values) == 1 else jnp.concatenate(values)

    late = [[] for _ in range(parts)]
    for stage in range(bits):
        for p in range(parts):
            masks = [1 << (stage + t) % bits for t in TURNS[p]]

            def onward(entries):
                where = [m for _, ms in entries for m in ms]
                value = move(join([v for v, _ in entries]), masks)
                return value, [(a ^ masks[0], b ^ masks[1]) for a, b in where]

            if stage < bits - 1:
                held[p].append(onward(held[p]))
            else:
                late[p] = [onward(held[p])]
    def write(whole, groups):
        pieces, plan, slots = [], [], []
        for p, group in enumerate(groups):
            for value, where in group:
                pieces.append(value)
                plan.append((tops[p], [len(slots) + i for i in range(len(where))]))
                slots += where
        base = jnp.stack([member ^ jnp.where(core == 0, a, b) for a, b in slots]).astype(jnp.int32)
        before = [] if whole is None else [whole]
        return pl.pallas_call(
            functools.partial(assemble, plan),
            out_shape=jax.ShapeDtypeStruct((sum(heights), inner * cols), mine.dtype),
            in_specs=[SMEM] + [VMEM] * len(pieces) + [ANY] * len(before),
            out_specs=ANY,
            scratch_shapes=[pltpu.SemaphoreType.DMA((len(slots),))],
            input_output_aliases={1 + len(pieces): 0} if before else {},
            compiler_params=room(16),
            name="assemble",
        )(base, *pieces, *before)

    whole = write(None, held)
    return write(whole, late) if any(late) else whole


def body(dp, ne, tokens, centroids, prices, epsilon):
    f32 = jnp.float32
    local_tokens, width = tokens.shape
    own = centroids.shape[0]
    experts = own * ne
    devices = dp * ne
    rows = local_tokens // ne
    cols = width // dp
    dp_at, expert_at = lax.axis_index("dp"), lax.axis_index("expert")
    everywhere = ("dp", "expert")
    outer = 2 if ne == 2 and dp % 16 == 0 and dp & (dp - 1) == 0 else 1
    inner = dp // outer
    cols = width // inner
    paired = outer == 2 and cols % 128 == 0 and own % 32 == 0
    swap = [(0, 1), (1, 0)]

    def shape(*sizes, dtype=f32):
        return jax.ShapeDtypeStruct(sizes, dtype)

    line, spread = shape(1, experts), shape(devices, 1, experts)
    at = jnp.stack([expert_at]).astype(jnp.int32)
    if paired:
        half = inner // 2
        chunks = 4
        masks = [(k, inner - 1 - k) for k in range(half)]
        theirs = [dp_at ^ jnp.where(expert_at == 0, *mask) for mask in masks]
        place = [expert_at, 1 - expert_at, dp_at % inner] + [t % inner for t in theirs]
        place = jnp.stack(place).astype(jnp.int32)
        kept, sent, mine, *parcels = pl.pallas_call(
            functools.partial(opening, chunks),
            out_shape=[shape(rows, own)] * 2
            + [shape(own, cols, dtype=centroids.dtype)]
            + [shape(local_tokens, cols, dtype=tokens.dtype)] * half,
            in_specs=[SMEM, ANY, ANY, VMEM],
            out_specs=[VMEM] * (3 + half),
            scratch_shapes=[
                pltpu.VMEM(tokens.shape, tokens.dtype),
                pltpu.VMEM(centroids.shape, centroids.dtype),
                pltpu.VMEM((local_tokens, own), f32),
                pltpu.SemaphoreType.DMA((2, chunks)),
            ],
            compiler_params=room(52),
            name="opening",
        )(place, tokens, centroids, prices.reshape(1, own))
        received = lax.ppermute(sent, "expert", swap)
        values, bids = pl.pallas_call(
            first_round,
            out_shape=(shape(rows, experts), spread),
            in_specs=[SMEM, VMEM, VMEM, SMEM],
            out_specs=(VMEM, VMEM),
            compiler_params=room(4),
            name="first_round",
        )(at, kept, received, epsilon)
        columns = [None] * half

        def sent_on(k):
            pairs = [(i * 2 + c, (i ^ masks[k][c]) * 2 + c) for i in range(dp) for c in range(2)]
            columns[k] = lax.ppermute(parcels[k], everywhere, pairs)

        sources = theirs + [dp_at ^ jnp.where(expert_at == 0, *mask[::-1]) for mask in masks]
    else:
        parcels = tokens.reshape(local_tokens, dp, cols).transpose(1, 0, 2)
        columns = lax.all_to_all(parcels, "dp", 0, 0, tiled=True)
        columns = [columns.reshape(dp * local_tokens, cols)[i * local_tokens :][:local_tokens] for i in range(dp)]
        sources = list(range(dp))
        mine = lax.dynamic_slice_in_dim(centroids, dp_at * cols, cols, 1)
        part = lax.dot_general(
            tokens, centroids, (((1,), (1,)), ((), ())), preferred_element_type=f32
        ) * 0.015625 - prices
        part = lax.all_to_all(part, "expert", 0, 1, tiled=True)
        values, bids = pl.pallas_call(
            first_round_whole,
            out_shape=(shape(rows, experts), spread),
            in_specs=[SMEM, VMEM, SMEM],
            out_specs=(VMEM, VMEM),
            compiler_params=room(4),
            name="first_round",
        )(at, part, epsilon)

    total = jnp.zeros((1, experts), f32)
    waiting = list(range(half))[::-1] if paired else []
    for _ in range(ROUNDS - 2):
        for k in waiting[:-2]:
            sent_on(k)
        waiting = waiting[-2:]
        bids = lax.all_to_all(bids, everywhere, 0, 0, tiled=True)
        bids, total = pl.pallas_call(
            next_round,
            out_shape=(spread, line),
            in_specs=[VMEM, VMEM, SMEM, VMEM],
            out_specs=(VMEM, VMEM),
            compiler_params=room(4),
            name="next_round",
        )(values, total, epsilon, bids)
    if paired:
        k = waiting.pop(0)
        parcels[k] = released(total, parcels[k])
        sent_on(k)
    bids = lax.all_to_all(bids, everywhere, 0, 0, tiled=True)
    wide = (rows // 128 + 1) * 128
    largest = jnp.max(jnp.abs(tokens)).astype(f32).reshape(1)
    base = (dp_at * local_tokens + expert_at * rows).astype(jnp.int32).reshape(1)
    info, total = pl.pallas_call(
        last_round,
        out_shape=(shape(devices, 1, 3 * experts + wide), line),
        in_specs=[VMEM, VMEM, SMEM, VMEM, SMEM, SMEM],
        out_specs=(VMEM, VMEM),
        compiler_params=room(8),
        name="last_round",
    )(values, total, epsilon, bids, base, largest)
    for k in waiting:
        parcels[k] = released(total, parcels[k])
        sent_on(k)
    if paired:
        columns += [lax.ppermute(c, "expert", swap) for c in columns]
    info = lax.all_to_all(info, everywhere, 0, 0, tiled=True)

    place = jnp.stack([expert_at * own, dp_at] + sources).astype(jnp.int32)
    direct = own % 128 == 0
    listed = own if direct else experts
    tile = 16 if own % 16 == 0 else own
    heights = [tile * (own // tile * (i + 1) // PARTS - own // tile * i // PARTS) for i in range(PARTS)]
    heights = [h for h in heights if h]
    parts = len(heights)
    final, holder, best, counts, fits, *sums = pl.pallas_call(
        functools.partial(finish, ne, rows, outer, parts),
        out_shape=(
            shape(1, listed),
            shape(1, listed, dtype=jnp.int32),
            shape(1, local_tokens, dtype=jnp.int32),
            shape(own, 128),
            shape(1, dtype=jnp.int32),
        )
        + tuple(shape(h, cols) for h in heights)
        + tuple(shape(h, cols, dtype=jnp.bfloat16) for h in heights),
        in_specs=[SMEM] + [VMEM] * (3 + len(columns)),
        out_specs=(VMEM, VMEM, VMEM, VMEM, SMEM) + (VMEM,) * (2 * parts),
        compiler_params=room(16),
        name="finish",
    )(place, info, total, prices.reshape(1, own), *columns)
    if paired:
        spread_as = [functools.partial(spread_out, dp, inner, wide) for wide in (True, False)]
        refreshed = lax.cond(fits[0] > 0, spread_as[1], spread_as[0], sums[:parts], sums[parts:], mine, counts)
    else:
        sums = jnp.concatenate(sums[:parts])
        fresh = 0.5 * mine.astype(f32) + 0.5 * sums / counts[:, :1]
        refreshed = lax.all_gather(fresh.astype(centroids.dtype), "dp", axis=1, tiled=True)
    if direct:
        final, holder = final[0], holder[0]
    else:
        final = prices + lax.dynamic_slice_in_dim(final[0], expert_at * own, own, 0)
        holder = lax.dynamic_slice_in_dim(holder[0], expert_at * own, own, 0)
    return final, best[0], holder, refreshed


def solution(mesh):
    placed = (P("dp", None), P("expert", None), P("expert"), P())
    return jax.shard_map(
        functools.partial(body, mesh.shape["dp"], mesh.shape["expert"]),
        mesh=mesh,
        in_specs=placed,
        out_specs=(P("expert"), P("dp"), P("expert"), P("expert", None)),
        check_vma=False,
    )
```

```python
import functools

import jax
import jax.numpy as jnp
from jax import lax
from jax.experimental import pallas as pl
from jax.experimental.pallas import tpu as pltpu
from jax.sharding import PartitionSpec as P

ROUNDS = 3

lowest = -1e30
far = 1073741824.0
VMEM = pl.BlockSpec(memory_space=pltpu.VMEM)
SMEM = pl.BlockSpec(memory_space=pltpu.SMEM)
ANY = pl.BlockSpec(memory_space=pl.ANY)


def room(mebibytes):
    return pltpu.CompilerParams(vmem_limit_bytes=mebibytes * 1024 * 1024)


def opening(chunks, place, tokens, centroids, prices, kept, sent, mine, largest, *refs):
    parcels, (tok, cen, acc, sem) = refs[:-4], refs[-4:]
    rows, cols = kept.shape[0], mine.shape[1]
    step = tok.shape[1] // chunks
    copies = []
    for i in range(chunks):
        part = pl.ds(i * step, step)
        copies.append((
            pltpu.make_async_copy(centroids.at[:, part], cen.at[:, part], sem.at[0, i]),
            pltpu.make_async_copy(tokens.at[:, part], tok.at[:, part], sem.at[1, i]),
        ))
    for pair in copies:
        pair[0].start()
        pair[1].start()
    for i, pair in enumerate(copies):
        pair[0].wait()
        pair[1].wait()
        part = slice(i * step, (i + 1) * step)
        product = lax.dot_general(
            tok[:, part], cen[:, part], (((1,), (1,)), ((), ())), preferred_element_type=jnp.float32
        )
        size = jnp.max(jnp.abs(tok[:, part]).reshape(-1, 16, step), axis=0)
        peak = size if i == 0 else jnp.maximum(peak, size)
        if i:
            acc[...] += product
        else:
            acc[...] = product
    peak = jnp.max(peak.astype(jnp.float32), axis=0, keepdims=True)
    largest[...] = jnp.broadcast_to(jnp.max(peak, axis=1, keepdims=True), largest.shape)
    for out, at in ((sent, 1), (kept, 0)):
        row = pl.multiple_of(place[at] * rows, rows)
        out[...] = acc[pl.ds(row, rows), :] * 0.015625 - prices[...]
    mine[...] = cen[:, pl.ds(pl.multiple_of(place[2] * cols, cols), cols)]
    for k, parcel in enumerate(parcels):
        parcel[...] = tok[:, pl.ds(pl.multiple_of(place[3 + k] * cols, cols), cols)]


def choose(values, eps):
    ids = lax.broadcasted_iota(jnp.int32, values.shape, 1).astype(jnp.float32)
    top = jnp.max(values, axis=1, keepdims=True)
    choice = jnp.min(jnp.where(values == top, ids, far), axis=1, keepdims=True)
    claims = ids == choice
    second = jnp.max(jnp.where(claims, lowest, values), axis=1, keepdims=True)
    bids = jnp.where(claims, top - second + eps, -1.0)
    return choice, claims, bids, jnp.max(bids, axis=0, keepdims=True)


def first_round(place, kept, theirs, epsilon, values, out):
    if theirs is None:
        values[...] = kept[...]
    else:
        own = kept.shape[1]
        swapped = place[0] != 0
        values[:, :own] = jnp.where(swapped, theirs[...], kept[...])
        values[:, own:] = jnp.where(swapped, kept[...], theirs[...])
    raised = choose(values[...], epsilon[0])[-1]
    out[...] = jnp.broadcast_to(raised[None], out.shape)


def first_round_whole(place, kept, epsilon, values, out):
    first_round(place, kept, None, epsilon, values, out)


def next_round(values, before, epsilon, bids, out, after):
    total = before[...] + jnp.maximum(jnp.max(bids[...], axis=0), 0.0)
    after[...] = total
    raised = choose(values[...] - total, epsilon[0])[-1]
    out[...] = jnp.broadcast_to(raised[None], out.shape)


def last_round(values, before, epsilon, bids, base, largest, out, after):
    rows, experts = values.shape
    total = before[...] + jnp.maximum(jnp.max(bids[...], axis=0), 0.0)
    after[...] = total
    choice, claims, spread, raised = choose(values[...] - total, epsilon[0])
    token = (base[0] + lax.broadcasted_iota(jnp.int32, (rows, experts), 0)).astype(jnp.float32)
    first = jnp.min(jnp.where(claims & (spread == raised), token, far), axis=0, keepdims=True)
    count = jnp.sum(claims.astype(jnp.float32), axis=0, keepdims=True)
    wide = out.shape[2] - 3 * experts
    lane = lax.broadcasted_iota(jnp.int32, (rows, wide), 1)
    row = lax.broadcasted_iota(jnp.int32, (rows, wide), 0)
    turned = jnp.sum(jnp.where(lane == row, choice, 0.0), axis=0, keepdims=True)
    turned = jnp.where(lane[:1] == rows, largest[:, :1], turned)
    line = jnp.concatenate([raised, first, count, turned], axis=1)
    out[...] = jnp.broadcast_to(line[None], out.shape)


def pass_on(line, *refs):
    pass


def released(line, parcels):
    return pl.pallas_call(
        pass_on,
        out_shape=[jax.ShapeDtypeStruct(p.shape, p.dtype) for p in parcels],
        in_specs=[ANY] * (1 + len(parcels)),
        out_specs=[ANY] * len(parcels),
        input_output_aliases={1 + i: i for i in range(len(parcels))},
        compiler_params=room(4),
        cost_estimate=pl.CostEstimate(flops=1000000000, bytes_accessed=4096, transcendentals=0),
        name="released",
    )(line, *parcels)


def fill(line, value, out):
    out[...] = value[...]


def filled(line, value):
    return pl.pallas_call(
        fill,
        out_shape=jax.ShapeDtypeStruct(value.shape, value.dtype),
        in_specs=[ANY, VMEM],
        out_specs=VMEM,
        compiler_params=room(4),
        cost_estimate=pl.CostEstimate(flops=4000000000, bytes_accessed=4096, transcendentals=0),
        name="filled",
    )(line, value)


def add_up(ne, rows, top, place, info, columns, total_out, short_out):
    height = total_out.shape[0]
    at = info.shape[2] // 128 * 128 - (rows // 128 + 1) * 128
    ids = place[0] + top + lax.broadcasted_iota(jnp.int32, (height, rows), 0)
    ids = ids.astype(jnp.float32)
    total = jnp.zeros(total_out.shape, jnp.float32)
    for k, features in enumerate(columns):
        for c in range(ne):
            chosen = info[place[2 + k] * ne + c, :, at : at + rows]
            hot = jnp.where(ids == chosen, 1.0, 0.0).astype(jnp.bfloat16)
            total += jnp.dot(
                hot, features[c * rows : (c + 1) * rows, :], preferred_element_type=jnp.float32
            )
    total_out[...] = total
    short_out[...] = total.astype(short_out.dtype)


def more_sums(ne, rows, top, place, info, *refs):
    add_up(ne, rows, top, place, info, refs[:-2], *refs[-2:])


def finish(ne, rows, outer, place, info, before, prices, *refs):
    columns, (final, holder, best, counts_out, fits, *sums) = refs[:-7], refs[-7:]
    experts = before.shape[1]
    own = prices.shape[1]
    start = place[0]
    if own % 128 == 0:
        start = pl.multiple_of(start, 128)
        raised = info[:, :, pl.ds(start, own)]
        firsts = info[:, :, pl.ds(pl.multiple_of(experts + start, 128), own)]
        earlier = before[:, pl.ds(start, own)]
        top_bid = jnp.max(raised, axis=0)
        first = jnp.min(jnp.where(raised == top_bid[None], firsts, far), axis=0)
        final[...] = prices[...] + earlier + jnp.maximum(top_bid, 0.0)
        holder[...] = jnp.where(top_bid > 0, first, -1.0).astype(jnp.int32)
    else:
        raised = info[:, :, :experts]
        top_bid = jnp.max(raised, axis=0)
        firsts = jnp.where(raised == top_bid[None], info[:, :, experts : 2 * experts], far)
        final[...] = before[...] + jnp.maximum(top_bid, 0.0)
        holder[...] = jnp.where(top_bid > 0, jnp.min(firsts, axis=0), -1.0).astype(jnp.int32)
    at = 3 * experts
    for c in range(ne):
        mark = info[place[1] * ne + c, :, at : at + rows]
        best[:, c * rows : (c + 1) * rows] = mark.astype(jnp.int32)
    add_up(ne, rows, 0, place, info, columns, *sums)
    share = info.shape[0] // outer
    each = [
        jnp.sum(info[i * share : (i + 1) * share, :, 2 * experts : at], axis=0) for i in range(outer)
    ]
    largest = jnp.max(info[:, :, at + rows : at + rows + 1])
    fullest = jnp.max(functools.reduce(jnp.maximum, each))
    fits[0] = jnp.where(fullest * largest <= 256.0, 1, 0)
    counts = functools.reduce(jnp.add, each)
    expert_row = place[0] + lax.broadcasted_iota(jnp.int32, (own, experts), 0)
    lane = lax.broadcasted_iota(jnp.int32, (own, experts), 1)
    counts = jnp.sum(jnp.where(expert_row == lane, counts, 0.0), axis=1, keepdims=True)
    counts_out[...] = jnp.broadcast_to(jnp.maximum(counts, 1.0), counts_out.shape)


def blend(row, centroids, counts, *refs):
    sums, out = refs[:-1], refs[-1]
    rows, cols = out.shape
    total = functools.reduce(jnp.add, [s[...].astype(jnp.float32) for s in sums])
    old = centroids[row : row + rows, :].astype(jnp.float32)
    share = counts[row : row + rows, :1]
    out[...] = (0.5 * old + 0.5 * total / share).astype(out.dtype)


def assemble(plan, base, *refs):
    pieces, out, sem = refs[: len(plan)], refs[-2], refs[-1]
    cols = pieces[0].shape[-1]
    copies = []
    for piece, (row, slots) in zip(pieces, plan):
        for i, slot in enumerate(slots):
            col = pl.multiple_of(base[slot] * cols, cols)
            copies.append(
                pltpu.make_async_copy(
                    piece.at[i], out.at[pl.ds(row, piece.shape[1]), pl.ds(col, cols)], sem.at[len(copies)]
                )
            )
    for copy in copies:
        copy.start()
    for copy in copies:
        copy.wait()


PARTS = 2
TURNS = ((0, 1), (2, 1))


def spread_out(dp, inner, wide, sums, short, mine, counts):
    bits = inner.bit_length() - 1
    member = lax.axis_index("dp") % inner
    core = lax.axis_index("expert")

    def move(value, masks):
        pairs = [(i * 2 + c, (i ^ masks[c]) * 2 + c) for i in range(dp) for c in range(2)]
        return lax.ppermute(value, ("dp", "expert"), pairs)

    parts = len(sums)
    cols = sums[0].shape[1]
    heights = [s.shape[0] for s in sums]
    tops = [sum(heights[:p]) for p in range(parts)]
    sent = sums if wide else short
    other = [move(s, (inner, inner)) for s in sent] if inner < dp else None
    held = []
    for p in range(parts):
        terms = [sums[p], other[p]] if other else [sums[p]]
        fresh = pl.pallas_call(
            functools.partial(blend, tops[p]),
            out_shape=jax.ShapeDtypeStruct((heights[p], cols), mine.dtype),
            in_specs=[VMEM] * (2 + len(terms)),
            out_specs=VMEM,
            compiler_params=room(4),
            name="blend",
        )(mine, counts, *terms)
        held.append([(fresh[None], [(0, 0)])])

    def join(values):
        return values[0] if len(values) == 1 else jnp.concatenate(values)

    late = [[] for _ in range(parts)]
    for stage in range(bits):
        for p in range(parts):
            masks = [1 << (stage + t) % bits for t in TURNS[p]]

            def onward(entries):
                where = [m for _, ms in entries for m in ms]
                value = move(join([v for v, _ in entries]), masks)
                return value, [(a ^ masks[0], b ^ masks[1]) for a, b in where]

            if stage < bits - 1 or stage < 2:
                held[p].append(onward(held[p]))
            else:
                late[p] = [onward(held[p][:-1]), onward(held[p][-1:])]
    def write(whole, groups):
        pieces, plan, slots = [], [], []
        for p, group in enumerate(groups):
            for value, where in group:
                pieces.append(value)
                plan.append((tops[p], [len(slots) + i for i in range(len(where))]))
                slots += where
        base = jnp.stack([member ^ jnp.where(core == 0, a, b) for a, b in slots]).astype(jnp.int32)
        before = [] if whole is None else [whole]
        return pl.pallas_call(
            functools.partial(assemble, plan),
            out_shape=jax.ShapeDtypeStruct((sum(heights), inner * cols), mine.dtype),
            in_specs=[SMEM] + [VMEM] * len(pieces) + [ANY] * len(before),
            out_specs=ANY,
            scratch_shapes=[pltpu.SemaphoreType.DMA((len(slots),))],
            input_output_aliases={1 + len(pieces): 0} if before else {},
            compiler_params=room(16),
            name="assemble",
        )(base, *pieces, *before)

    whole = write(None, held)
    for p in range(parts):
        if late[p]:
            whole = write(whole, [late[p] if q == p else [] for q in range(parts)])
    return whole


def body(dp, ne, tokens, centroids, prices, epsilon):
    f32 = jnp.float32
    local_tokens, width = tokens.shape
    own = centroids.shape[0]
    experts = own * ne
    devices = dp * ne
    rows = local_tokens // ne
    cols = width // dp
    dp_at, expert_at = lax.axis_index("dp"), lax.axis_index("expert")
    everywhere = ("dp", "expert")
    outer = 2 if ne == 2 and dp % 16 == 0 and dp & (dp - 1) == 0 else 1
    inner = dp // outer
    cols = width // inner
    paired = outer == 2 and cols % 128 == 0 and own % 32 == 0
    swap = [(0, 1), (1, 0)]

    def shape(*sizes, dtype=f32):
        return jax.ShapeDtypeStruct(sizes, dtype)

    line, spread = shape(1, experts), shape(devices, 1, experts)
    at = jnp.stack([expert_at]).astype(jnp.int32)
    if paired:
        half = inner // 2
        chunks = 4
        masks = [(k, inner - 1 - k) for k in range(half)]
        theirs = [dp_at ^ jnp.where(expert_at == 0, *mask) for mask in masks]
        place = [expert_at, 1 - expert_at, dp_at % inner] + [t % inner for t in theirs]
        place = jnp.stack(place).astype(jnp.int32)
        kept, sent, mine, largest, *parcels = pl.pallas_call(
            functools.partial(opening, chunks),
            out_shape=[shape(rows, own)] * 2
            + [shape(own, cols, dtype=centroids.dtype), shape(1, 128)]
            + [shape(local_tokens, cols, dtype=tokens.dtype)] * half,
            in_specs=[SMEM, ANY, ANY, VMEM],
            out_specs=[VMEM] * (4 + half),
            scratch_shapes=[
                pltpu.VMEM(tokens.shape, tokens.dtype),
                pltpu.VMEM(centroids.shape, centroids.dtype),
                pltpu.VMEM((local_tokens, own), f32),
                pltpu.SemaphoreType.DMA((2, chunks)),
            ],
            compiler_params=room(52),
            name="opening",
        )(place, tokens, centroids, prices.reshape(1, own))
        received = lax.ppermute(sent, "expert", swap)
        values, bids = pl.pallas_call(
            first_round,
            out_shape=(shape(rows, experts), spread),
            in_specs=[SMEM, VMEM, VMEM, SMEM],
            out_specs=(VMEM, VMEM),
            compiler_params=room(4),
            name="first_round",
        )(at, kept, received, epsilon)
        columns = [None] * half

        def sent_on(k):
            pairs = [(i * 2 + c, (i ^ masks[k][c]) * 2 + c) for i in range(dp) for c in range(2)]
            columns[k] = lax.ppermute(parcels[k], everywhere, pairs)

        sources = theirs + [dp_at ^ jnp.where(expert_at == 0, *mask[::-1]) for mask in masks]
    else:
        parcels = tokens.reshape(local_tokens, dp, cols).transpose(1, 0, 2)
        columns = lax.all_to_all(parcels, "dp", 0, 0, tiled=True)
        columns = [columns.reshape(dp * local_tokens, cols)[i * local_tokens :][:local_tokens] for i in range(dp)]
        sources = list(range(dp))
        mine = lax.dynamic_slice_in_dim(centroids, dp_at * cols, cols, 1)
        largest = jnp.full((1, 128), jnp.max(jnp.abs(tokens)).astype(f32))
        part = lax.dot_general(
            tokens, centroids, (((1,), (1,)), ((), ())), preferred_element_type=f32
        ) * 0.015625 - prices
        part = lax.all_to_all(part, "expert", 0, 1, tiled=True)
        values, bids = pl.pallas_call(
            first_round_whole,
            out_shape=(shape(rows, experts), spread),
            in_specs=[SMEM, VMEM, SMEM],
            out_specs=(VMEM, VMEM),
            compiler_params=room(4),
            name="first_round",
        )(at, part, epsilon)

    total = jnp.zeros((1, experts), f32)
    waiting = list(range(half))[::-1] if paired else []
    for _ in range(ROUNDS - 2):
        for k in waiting[:-2]:
            sent_on(k)
        waiting = waiting[-2:]
        bids = lax.all_to_all(bids, everywhere, 0, 0, tiled=True)
        bids, total = pl.pallas_call(
            next_round,
            out_shape=(spread, line),
            in_specs=[VMEM, VMEM, SMEM, VMEM],
            out_specs=(VMEM, VMEM),
            compiler_params=room(4),
            name="next_round",
        )(values, total, epsilon, bids)
    if paired:
        parcels[: len(waiting)] = released(total, parcels[: len(waiting)])
    for k in waiting:
        sent_on(k)
    bids = lax.all_to_all(bids, everywhere, 0, 0, tiled=True)
    wide = (rows // 128 + 1) * 128
    largest = filled(total, largest)
    base = (dp_at * local_tokens + expert_at * rows).astype(jnp.int32).reshape(1)
    info, total = pl.pallas_call(
        last_round,
        out_shape=(shape(devices, 1, 3 * experts + wide), line),
        in_specs=[VMEM, VMEM, SMEM, VMEM, SMEM, VMEM],
        out_specs=(VMEM, VMEM),
        compiler_params=room(8),
        name="last_round",
    )(values, total, epsilon, bids, base, largest)
    if paired:
        columns += [lax.ppermute(c, "expert", swap) for c in columns]
    info = lax.all_to_all(info, everywhere, 0, 0, tiled=True)

    place = jnp.stack([expert_at * own, dp_at] + sources).astype(jnp.int32)
    direct = own % 128 == 0
    listed = own if direct else experts
    low = own // 32 * 16 if own % 32 == 0 else own
    heights = [low, own - low] if paired else [own]

    def two(height):
        return (shape(height, cols), shape(height, cols, dtype=jnp.bfloat16))

    final, holder, best, counts, fits, *sums = pl.pallas_call(
        functools.partial(finish, ne, rows, outer),
        out_shape=(
            shape(1, listed),
            shape(1, listed, dtype=jnp.int32),
            shape(1, local_tokens, dtype=jnp.int32),
            shape(own, 128),
            shape(1, dtype=jnp.int32),
        )
        + two(heights[0]),
        in_specs=[SMEM] + [VMEM] * (3 + len(columns)),
        out_specs=(VMEM, VMEM, VMEM, VMEM, SMEM, VMEM, VMEM),
        compiler_params=room(16),
        name="finish",
    )(place, info, total, prices.reshape(1, own), *columns)
    if paired:

        def rest(wide, place, info, columns, sums, best, mine, counts):
            more = pl.pallas_call(
                functools.partial(more_sums, ne, rows, heights[0]),
                out_shape=two(heights[1]),
                in_specs=[SMEM] + [VMEM] * (1 + len(columns)),
                out_specs=(VMEM, VMEM),
                compiler_params=room(16),
                name="more_sums",
            )(place, info, *columns)
            pairs = list(zip(sums, more))
            whole = spread_out(dp, inner, wide, pairs[0], pairs[1], mine, counts)
            return best[0], whole

        best, refreshed = lax.switch(
            fits[0],
            [functools.partial(rest, True), functools.partial(rest, False)],
            place, info, columns, sums, best, mine, counts,
        )
    else:
        best = best[0]
        fresh = 0.5 * mine.astype(f32) + 0.5 * sums[0] / counts[:, :1]
        refreshed = lax.all_gather(fresh.astype(centroids.dtype), "dp", axis=1, tiled=True)
    if direct:
        final, holder = final[0], holder[0]
    else:
        final = prices + lax.dynamic_slice_in_dim(final[0], expert_at * own, own, 0)
        holder = lax.dynamic_slice_in_dim(holder[0], expert_at * own, own, 0)
    return final, best, holder, refreshed


def solution(mesh):
    placed = (P("dp", None), P("expert", None), P("expert"), P())
    return jax.shard_map(
        functools.partial(body, mesh.shape["dp"], mesh.shape["expert"]),
        mesh=mesh,
        in_specs=placed,
        out_specs=(P("expert"), P("dp"), P("expert"), P("expert", None)),
        check_vma=False,
    )
```

```python
import functools

import jax
import jax.numpy as jnp
from jax import lax
from jax.experimental import pallas as pl
from jax.experimental.pallas import tpu as pltpu
from jax.sharding import PartitionSpec as P

ROUNDS = 3

lowest = -1e30
far = 1073741824.0
VMEM = pl.BlockSpec(memory_space=pltpu.VMEM)
SMEM = pl.BlockSpec(memory_space=pltpu.SMEM)
ANY = pl.BlockSpec(memory_space=pl.ANY)


def room(mebibytes):
    return pltpu.CompilerParams(vmem_limit_bytes=mebibytes * 1024 * 1024)


def opening(chunks, place, tokens, centroids, prices, kept, sent, mine, largest, *refs):
    parcels, (tok, cen, acc, sem) = refs[:-4], refs[-4:]
    rows, cols = kept.shape[0], mine.shape[1]
    step = tok.shape[1] // chunks
    copies = []
    for i in range(chunks):
        part = pl.ds(i * step, step)
        copies.append((
            pltpu.make_async_copy(centroids.at[:, part], cen.at[:, part], sem.at[0, i]),
            pltpu.make_async_copy(tokens.at[:, part], tok.at[:, part], sem.at[1, i]),
        ))
    for pair in copies:
        pair[0].start()
        pair[1].start()
    for i, pair in enumerate(copies):
        pair[0].wait()
        pair[1].wait()
        part = slice(i * step, (i + 1) * step)
        product = lax.dot_general(
            tok[:, part], cen[:, part], (((1,), (1,)), ((), ())), preferred_element_type=jnp.float32
        )
        size = jnp.max(jnp.abs(tok[:, part]).reshape(-1, 16, step), axis=0)
        peak = size if i == 0 else jnp.maximum(peak, size)
        if i:
            acc[...] += product
        else:
            acc[...] = product
    peak = jnp.max(peak.astype(jnp.float32), axis=0, keepdims=True)
    largest[...] = jnp.broadcast_to(jnp.max(peak, axis=1, keepdims=True), largest.shape)
    for out, at in ((sent, 1), (kept, 0)):
        row = pl.multiple_of(place[at] * rows, rows)
        out[...] = acc[pl.ds(row, rows), :] * 0.015625 - prices[...]
    mine[...] = cen[:, pl.ds(pl.multiple_of(place[2] * cols, cols), cols)]
    for k, parcel in enumerate(parcels):
        parcel[...] = tok[:, pl.ds(pl.multiple_of(place[3 + k] * cols, cols), cols)]


def choose(values, eps):
    ids = lax.broadcasted_iota(jnp.int32, values.shape, 1).astype(jnp.float32)
    top = jnp.max(values, axis=1, keepdims=True)
    choice = jnp.min(jnp.where(values == top, ids, far), axis=1, keepdims=True)
    claims = ids == choice
    second = jnp.max(jnp.where(claims, lowest, values), axis=1, keepdims=True)
    bid = top - second + eps
    bids = jnp.where(claims, bid, -1.0)
    return choice, claims, bid, bids, jnp.max(bids, axis=0, keepdims=True)


def first_round(place, kept, theirs, epsilon, values, out):
    if theirs is None:
        values[...] = kept[...]
    else:
        own = kept.shape[1]
        swapped = place[0] != 0
        values[:, :own] = jnp.where(swapped, theirs[...], kept[...])
        values[:, own:] = jnp.where(swapped, kept[...], theirs[...])
    raised = choose(values[...], epsilon[0])[-1]
    out[...] = jnp.broadcast_to(raised[None], out.shape)


def first_round_whole(place, kept, epsilon, values, out):
    first_round(place, kept, None, epsilon, values, out)


def next_round(values, before, epsilon, bids, out, after):
    total = before[...] + jnp.maximum(jnp.max(bids[...], axis=0), 0.0)
    after[...] = total
    raised = choose(values[...] - total, epsilon[0])[-1]
    out[...] = jnp.broadcast_to(raised[None], out.shape)


def last_round(values, before, epsilon, bids, largest, out, after):
    rows, experts = values.shape
    total = before[...] + jnp.maximum(jnp.max(bids[...], axis=0), 0.0)
    after[...] = total
    choice, claims, bid, _, _ = choose(values[...] - total, epsilon[0])
    count = jnp.sum(claims.astype(jnp.float32), axis=0, keepdims=True)
    wide = (out.shape[2] - experts) // 2
    lane = lax.broadcasted_iota(jnp.int32, (rows, wide), 1)
    same = lane == lax.broadcasted_iota(jnp.int32, (rows, wide), 0)
    choices = jnp.sum(jnp.where(same, choice, 0.0), axis=0, keepdims=True)
    choices = jnp.where(lane[:1] == rows, largest[:, :1], choices)
    offered = jnp.sum(jnp.where(same, bid, 0.0), axis=0, keepdims=True)
    line = jnp.concatenate([count, choices, offered], axis=1)
    out[...] = jnp.broadcast_to(line[None], out.shape)


def pass_on(line, *refs):
    pass


def released(line, parcels):
    return pl.pallas_call(
        pass_on,
        out_shape=[jax.ShapeDtypeStruct(p.shape, p.dtype) for p in parcels],
        in_specs=[ANY] * (1 + len(parcels)),
        out_specs=[ANY] * len(parcels),
        input_output_aliases={1 + i: i for i in range(len(parcels))},
        compiler_params=room(4),
        cost_estimate=pl.CostEstimate(flops=1000000000, bytes_accessed=4096, transcendentals=0),
        name="released",
    )(line, *parcels)


def fill(line, value, out):
    out[...] = value[...]


def filled(line, value, flops):
    return pl.pallas_call(
        fill,
        out_shape=jax.ShapeDtypeStruct(value.shape, value.dtype),
        in_specs=[ANY, VMEM],
        out_specs=VMEM,
        compiler_params=room(4),
        cost_estimate=pl.CostEstimate(flops=flops, bytes_accessed=4096, transcendentals=0),
        name="filled",
    )(line, value)


def add_up(ne, rows, top, at, place, info, columns, total_out, short_out):
    height = total_out.shape[0]
    ids = place[0] + top + lax.broadcasted_iota(jnp.int32, (height, rows), 0)
    ids = ids.astype(jnp.float32)
    total = jnp.zeros(total_out.shape, jnp.float32)
    for k, features in enumerate(columns):
        for c in range(ne):
            chosen = info[place[2 + k] * ne + c, :, at : at + rows]
            hot = jnp.where(ids == chosen, 1.0, 0.0).astype(jnp.bfloat16)
            total += jnp.dot(
                hot, features[c * rows : (c + 1) * rows, :], preferred_element_type=jnp.float32
            )
    total_out[...] = total
    short_out[...] = total.astype(short_out.dtype)


def more_sums(ne, rows, top, at, place, info, *refs):
    add_up(ne, rows, top, at, place, info, refs[:-2], *refs[-2:])


def finish(ne, rows, outer, experts, place, info, *refs):
    columns, (best, counts_out, fits, *sums) = refs[:-6], refs[-5:]
    own = counts_out.shape[0]
    marks = [info[place[1] * ne + c, :, experts : experts + rows] for c in range(ne)]
    for c, mark in enumerate(marks):
        best[:, c * rows : (c + 1) * rows] = mark.astype(jnp.int32)
    add_up(ne, rows, 0, experts, place, info, columns, *sums)
    share = info.shape[0] // outer
    each = [jnp.sum(info[i * share : (i + 1) * share, :, :experts], axis=0) for i in range(outer)]
    largest = jnp.max(info[:, :, experts + rows : experts + rows + 1])
    fullest = jnp.max(functools.reduce(jnp.maximum, each))
    fits[0] = jnp.where(fullest * largest <= 256.0, 1, 0)
    counts = functools.reduce(jnp.add, each)
    expert_row = place[0] + lax.broadcasted_iota(jnp.int32, (own, experts), 0)
    lane = lax.broadcasted_iota(jnp.int32, (own, experts), 1)
    counts = jnp.sum(jnp.where(expert_row == lane, counts, 0.0), axis=1, keepdims=True)
    counts_out[...] = jnp.broadcast_to(jnp.maximum(counts, 1.0), counts_out.shape)


def settle(rows, experts, place, info, before, prices, final, holder):
    own = prices.shape[1]
    wide = (info.shape[2] - experts) // 2
    devices = info.shape[0]
    ids = (place[0] + lax.broadcasted_iota(jnp.int32, (own, rows), 0)).astype(jnp.float32)
    offset = lax.broadcasted_iota(jnp.int32, (own, rows), 1).astype(jnp.float32)

    def claimed(n):
        return ids == info[n, :, experts : experts + rows]

    def offered(n):
        return info[n, :, experts + wide : experts + wide + rows]

    def higher(n, top):
        return jnp.maximum(top, jnp.where(claimed(n), offered(n), -1.0))

    top = lax.fori_loop(0, devices, higher, jnp.full((own, rows), -1.0, jnp.float32))
    top = jnp.max(top, axis=1, keepdims=True)

    def earlier(n, first):
        token = (n * rows).astype(jnp.float32) + offset
        return jnp.minimum(first, jnp.where(claimed(n) & (offered(n) == top), token, far))

    first = lax.fori_loop(0, devices, earlier, jnp.full((own, rows), far, jnp.float32))
    first = jnp.min(first, axis=1, keepdims=True)
    same = lax.broadcasted_iota(jnp.int32, (own, own), 0) == lax.broadcasted_iota(jnp.int32, (own, own), 1)
    raised = jnp.sum(jnp.where(same, jnp.maximum(top, 0.0), 0.0), axis=0, keepdims=True)
    held = jnp.sum(jnp.where(same, jnp.where(top > 0, first, -1.0), 0.0), axis=0, keepdims=True)
    expert_row = place[0] + lax.broadcasted_iota(jnp.int32, (own, experts), 0)
    lane = lax.broadcasted_iota(jnp.int32, (own, experts), 1)
    so_far = jnp.sum(jnp.where(expert_row == lane, before[...], 0.0), axis=1, keepdims=True)
    so_far = jnp.sum(jnp.where(same, so_far, 0.0), axis=0, keepdims=True)
    final[...] = prices[...] + so_far + raised
    holder[...] = held.astype(jnp.int32)


def blend(row, centroids, counts, *refs):
    sums, out = refs[:-1], refs[-1]
    rows, cols = out.shape
    total = functools.reduce(jnp.add, [s[...].astype(jnp.float32) for s in sums])
    old = centroids[row : row + rows, :].astype(jnp.float32)
    share = counts[row : row + rows, :1]
    out[...] = (0.5 * old + 0.5 * total / share).astype(out.dtype)


def assemble(plan, base, *refs):
    pieces, out, sem = refs[: len(plan)], refs[-2], refs[-1]
    cols = pieces[0].shape[-1]
    copies = []
    for piece, (row, slots) in zip(pieces, plan):
        for i, slot in enumerate(slots):
            col = pl.multiple_of(base[slot] * cols, cols)
            copies.append(
                pltpu.make_async_copy(
                    piece.at[i], out.at[pl.ds(row, piece.shape[1]), pl.ds(col, cols)], sem.at[len(copies)]
                )
            )
    for copy in copies:
        copy.start()
    for copy in copies:
        copy.wait()


PARTS = 2
TURNS = ((0, 1), (2, 1))


def spread_out(dp, inner, wide, sums, short, mine, counts):
    bits = inner.bit_length() - 1
    member = lax.axis_index("dp") % inner
    core = lax.axis_index("expert")

    def move(value, masks):
        pairs = [(i * 2 + c, (i ^ masks[c]) * 2 + c) for i in range(dp) for c in range(2)]
        return lax.ppermute(value, ("dp", "expert"), pairs)

    parts = len(sums)
    cols = sums[0].shape[1]
    heights = [s.shape[0] for s in sums]
    tops = [sum(heights[:p]) for p in range(parts)]
    sent = sums if wide else short
    other = [move(s, (inner, inner)) for s in sent] if inner < dp else None
    held = []
    for p in range(parts):
        terms = [sums[p], other[p]] if other else [sums[p]]
        fresh = pl.pallas_call(
            functools.partial(blend, tops[p]),
            out_shape=jax.ShapeDtypeStruct((heights[p], cols), mine.dtype),
            in_specs=[VMEM] * (2 + len(terms)),
            out_specs=VMEM,
            compiler_params=room(4),
            name="blend",
        )(mine, counts, *terms)
        held.append([(fresh[None], [(0, 0)])])

    def join(values):
        return values[0] if len(values) == 1 else jnp.concatenate(values)

    late = [[] for _ in range(parts)]
    for stage in range(bits):
        for p in range(parts):
            masks = [1 << (stage + t) % bits for t in TURNS[p]]

            def onward(entries):
                where = [m for _, ms in entries for m in ms]
                value = move(join([v for v, _ in entries]), masks)
                return value, [(a ^ masks[0], b ^ masks[1]) for a, b in where]

            if stage < bits - 1 or stage < 2:
                held[p].append(onward(held[p]))
            else:
                early = onward(held[p][:-1])
                value, where = held[p][-1]
                value, sent = lax.optimization_barrier((value, early[0]))
                held[p][-1] = (value, where)
                late[p] = [(sent, early[1]), onward(held[p][-1:])]
    def write(whole, groups):
        pieces, plan, slots = [], [], []
        for p, group in enumerate(groups):
            for value, where in group:
                pieces.append(value)
                plan.append((tops[p], [len(slots) + i for i in range(len(where))]))
                slots += where
        base = jnp.stack([member ^ jnp.where(core == 0, a, b) for a, b in slots]).astype(jnp.int32)
        before = [] if whole is None else [whole]
        return pl.pallas_call(
            functools.partial(assemble, plan),
            out_shape=jax.ShapeDtypeStruct((sum(heights), inner * cols), mine.dtype),
            in_specs=[SMEM] + [VMEM] * len(pieces) + [ANY] * len(before),
            out_specs=ANY,
            scratch_shapes=[pltpu.SemaphoreType.DMA((len(slots),))],
            input_output_aliases={1 + len(pieces): 0} if before else {},
            compiler_params=room(16),
            name="assemble",
        )(base, *pieces, *before)

    whole = write(None, held)
    for p in range(parts):
        if late[p]:
            whole = write(whole, [late[p] if q == p else [] for q in range(parts)])
    return whole


def body(dp, ne, tokens, centroids, prices, epsilon):
    f32 = jnp.float32
    local_tokens, width = tokens.shape
    own = centroids.shape[0]
    experts = own * ne
    devices = dp * ne
    rows = local_tokens // ne
    cols = width // dp
    dp_at, expert_at = lax.axis_index("dp"), lax.axis_index("expert")
    everywhere = ("dp", "expert")
    outer = 2 if ne == 2 and dp % 16 == 0 and dp & (dp - 1) == 0 else 1
    inner = dp // outer
    cols = width // inner
    paired = outer == 2 and cols % 128 == 0 and own % 32 == 0
    swap = [(0, 1), (1, 0)]

    def shape(*sizes, dtype=f32):
        return jax.ShapeDtypeStruct(sizes, dtype)

    line, spread = shape(1, experts), shape(devices, 1, experts)
    at = jnp.stack([expert_at]).astype(jnp.int32)
    if paired:
        half = inner // 2
        chunks = 4
        masks = [(k, inner - 1 - k) for k in range(half)]
        theirs = [dp_at ^ jnp.where(expert_at == 0, *mask) for mask in masks]
        place = [expert_at, 1 - expert_at, dp_at % inner] + [t % inner for t in theirs]
        place = jnp.stack(place).astype(jnp.int32)
        kept, sent, mine, largest, *parcels = pl.pallas_call(
            functools.partial(opening, chunks),
            out_shape=[shape(rows, own)] * 2
            + [shape(own, cols, dtype=centroids.dtype), shape(1, 128)]
            + [shape(local_tokens, cols, dtype=tokens.dtype)] * half,
            in_specs=[SMEM, ANY, ANY, VMEM],
            out_specs=[VMEM] * (4 + half),
            scratch_shapes=[
                pltpu.VMEM(tokens.shape, tokens.dtype),
                pltpu.VMEM(centroids.shape, centroids.dtype),
                pltpu.VMEM((local_tokens, own), f32),
                pltpu.SemaphoreType.DMA((2, chunks)),
            ],
            compiler_params=room(52),
            name="opening",
        )(place, tokens, centroids, prices.reshape(1, own))
        received = lax.ppermute(sent, "expert", swap)
        values, bids = pl.pallas_call(
            first_round,
            out_shape=(shape(rows, experts), spread),
            in_specs=[SMEM, VMEM, VMEM, SMEM],
            out_specs=(VMEM, VMEM),
            compiler_params=room(4),
            name="first_round",
        )(at, kept, received, epsilon)
        columns = [None] * half

        def sent_on(k):
            pairs = [(i * 2 + c, (i ^ masks[k][c]) * 2 + c) for i in range(dp) for c in range(2)]
            columns[k] = lax.ppermute(parcels[k], everywhere, pairs)

        sources = theirs + [dp_at ^ jnp.where(expert_at == 0, *mask[::-1]) for mask in masks]
    else:
        parcels = tokens.reshape(local_tokens, dp, cols).transpose(1, 0, 2)
        columns = lax.all_to_all(parcels, "dp", 0, 0, tiled=True)
        columns = [columns.reshape(dp * local_tokens, cols)[i * local_tokens :][:local_tokens] for i in range(dp)]
        sources = list(range(dp))
        mine = lax.dynamic_slice_in_dim(centroids, dp_at * cols, cols, 1)
        largest = jnp.full((1, 128), jnp.max(jnp.abs(tokens)).astype(f32))
        part = lax.dot_general(
            tokens, centroids, (((1,), (1,)), ((), ())), preferred_element_type=f32
        ) * 0.015625 - prices
        part = lax.all_to_all(part, "expert", 0, 1, tiled=True)
        values, bids = pl.pallas_call(
            first_round_whole,
            out_shape=(shape(rows, experts), spread),
            in_specs=[SMEM, VMEM, SMEM],
            out_specs=(VMEM, VMEM),
            compiler_params=room(4),
            name="first_round",
        )(at, part, epsilon)

    total = jnp.zeros((1, experts), f32)
    waiting = list(range(half))[::-1] if paired else []
    for _ in range(ROUNDS - 2):
        for k in waiting[:-2]:
            sent_on(k)
        waiting = waiting[-2:]
        bids = lax.all_to_all(bids, everywhere, 0, 0, tiled=True)
        bids, total = pl.pallas_call(
            next_round,
            out_shape=(spread, line),
            in_specs=[VMEM, VMEM, SMEM, VMEM],
            out_specs=(VMEM, VMEM),
            compiler_params=room(4),
            name="next_round",
        )(values, total, epsilon, bids)
    if paired:
        parcels[: len(waiting)] = released(total, parcels[: len(waiting)])
    for k in waiting:
        sent_on(k)
    bids = lax.all_to_all(bids, everywhere, 0, 0, tiled=True)
    wide = (rows // 128 + 1) * 128
    largest = filled(total, largest, 8000000000)
    info, total = pl.pallas_call(
        last_round,
        out_shape=(shape(devices, 1, experts + 2 * wide), line),
        in_specs=[VMEM, VMEM, SMEM, VMEM, VMEM],
        out_specs=(VMEM, VMEM),
        compiler_params=room(8),
        name="last_round",
    )(values, total, epsilon, bids, largest)
    if paired:
        columns += [lax.ppermute(c, "expert", swap) for c in columns]
    info = lax.all_to_all(info, everywhere, 0, 0, tiled=True)

    timed = filled(total, largest, 8000000000)
    place = jnp.stack([expert_at * own, dp_at] + sources).astype(jnp.int32)
    low = own // 32 * 16 if own % 32 == 0 else own
    heights = [low, own - low] if paired else [own]

    def two(height):
        return (shape(height, cols), shape(height, cols, dtype=jnp.bfloat16))

    best, counts, fits, *sums = pl.pallas_call(
        functools.partial(finish, ne, rows, outer, experts),
        out_shape=(
            shape(1, local_tokens, dtype=jnp.int32),
            shape(own, 128),
            shape(1, dtype=jnp.int32),
        )
        + two(heights[0]),
        in_specs=[SMEM] + [VMEM] * (1 + len(columns)) + [ANY],
        out_specs=(VMEM, VMEM, SMEM, VMEM, VMEM),
        compiler_params=room(16),
        name="finish",
    )(place, info, *columns, timed)

    def settled(place, info, total, prices):
        return pl.pallas_call(
            functools.partial(settle, rows, experts),
            out_shape=(shape(1, own), shape(1, own, dtype=jnp.int32)),
            in_specs=[SMEM, VMEM, VMEM, VMEM],
            out_specs=(VMEM, VMEM),
            compiler_params=room(16),
            name="settle",
        )(place, info, total, prices)

    prices = prices.reshape(1, own)
    if paired:

        def rest(wide, place, info, total, prices, columns, sums, mine, counts):
            more = pl.pallas_call(
                functools.partial(more_sums, ne, rows, heights[0], experts),
                out_shape=two(heights[1]),
                in_specs=[SMEM] + [VMEM] * (1 + len(columns)),
                out_specs=(VMEM, VMEM),
                compiler_params=room(16),
                name="more_sums",
            )(place, info, *columns)
            pairs = list(zip(sums, more))
            whole = spread_out(dp, inner, wide, pairs[0], pairs[1], mine, counts)
            return *settled(place, info, total, prices), whole

        final, holder, refreshed = lax.switch(
            fits[0],
            [functools.partial(rest, True), functools.partial(rest, False)],
            place, info, total, prices, columns, sums, mine, counts,
        )
    else:
        final, holder = settled(place, info, total, prices)
        fresh = 0.5 * mine.astype(f32) + 0.5 * sums[0] / counts[:, :1]
        refreshed = lax.all_gather(fresh.astype(centroids.dtype), "dp", axis=1, tiled=True)
    return final[0], best[0], holder[0], refreshed


def solution(mesh):
    placed = (P("dp", None), P("expert", None), P("expert"), P())
    return jax.shard_map(
        functools.partial(body, mesh.shape["dp"], mesh.shape["expert"]),
        mesh=mesh,
        in_specs=placed,
        out_specs=(P("expert"), P("dp"), P("expert"), P("expert", None)),
        check_vma=False,
    )
```

```python
import functools

import jax
import jax.numpy as jnp
from jax import lax
from jax.experimental import pallas as pl
from jax.experimental.pallas import tpu as pltpu
from jax.sharding import PartitionSpec as P

ROUNDS = 3

lowest = -1e30
far = 1073741824.0
VMEM = pl.BlockSpec(memory_space=pltpu.VMEM)
SMEM = pl.BlockSpec(memory_space=pltpu.SMEM)
ANY = pl.BlockSpec(memory_space=pl.ANY)


def room(mebibytes):
    return pltpu.CompilerParams(vmem_limit_bytes=mebibytes * 1024 * 1024)


def opening(chunks, place, tokens, centroids, prices, kept, sent, mine, largest, *refs):
    parcels, (tok, cen, acc, sem) = refs[:-4], refs[-4:]
    rows, cols = kept.shape[0], mine.shape[1]
    step = tok.shape[1] // chunks
    copies = []
    for i in range(chunks):
        part = pl.ds(i * step, step)
        copies.append((
            pltpu.make_async_copy(centroids.at[:, part], cen.at[:, part], sem.at[0, i]),
            pltpu.make_async_copy(tokens.at[:, part], tok.at[:, part], sem.at[1, i]),
        ))
    for pair in copies:
        pair[0].start()
        pair[1].start()
    for i, pair in enumerate(copies):
        pair[0].wait()
        pair[1].wait()
        part = slice(i * step, (i + 1) * step)
        product = lax.dot_general(
            tok[:, part], cen[:, part], (((1,), (1,)), ((), ())), preferred_element_type=jnp.float32
        )
        size = jnp.max(jnp.abs(tok[:, part]).reshape(-1, 16, step), axis=0)
        peak = size if i == 0 else jnp.maximum(peak, size)
        if i:
            acc[...] += product
        else:
            acc[...] = product
    peak = jnp.max(peak.astype(jnp.float32), axis=0, keepdims=True)
    largest[...] = jnp.broadcast_to(jnp.max(peak, axis=1, keepdims=True), largest.shape)
    for out, at in ((sent, 1), (kept, 0)):
        row = pl.multiple_of(place[at] * rows, rows)
        out[...] = acc[pl.ds(row, rows), :] * 0.015625 - prices[...]
    mine[...] = cen[:, pl.ds(pl.multiple_of(place[2] * cols, cols), cols)]
    for k, parcel in enumerate(parcels):
        parcel[...] = tok[:, pl.ds(pl.multiple_of(place[3 + k] * cols, cols), cols)]


def choose(values, eps):
    ids = lax.broadcasted_iota(jnp.int32, values.shape, 1).astype(jnp.float32)
    top = jnp.max(values, axis=1, keepdims=True)
    choice = jnp.min(jnp.where(values == top, ids, far), axis=1, keepdims=True)
    claims = ids == choice
    second = jnp.max(jnp.where(claims, lowest, values), axis=1, keepdims=True)
    bid = top - second + eps
    bids = jnp.where(claims, bid, -1.0)
    return choice, claims, bid, bids, jnp.max(bids, axis=0, keepdims=True)


def first_round(place, kept, theirs, epsilon, values, out):
    if theirs is None:
        values[...] = kept[...]
    else:
        own = kept.shape[1]
        swapped = place[0] != 0
        values[:, :own] = jnp.where(swapped, theirs[...], kept[...])
        values[:, own:] = jnp.where(swapped, kept[...], theirs[...])
    raised = choose(values[...], epsilon[0])[-1]
    out[...] = jnp.broadcast_to(raised[None], out.shape)


def first_round_whole(place, kept, epsilon, values, out):
    first_round(place, kept, None, epsilon, values, out)


def next_round(values, before, epsilon, bids, out, after):
    total = before[...] + jnp.maximum(jnp.max(bids[...], axis=0), 0.0)
    after[...] = total
    raised = choose(values[...] - total, epsilon[0])[-1]
    out[...] = jnp.broadcast_to(raised[None], out.shape)


def last_round(values, before, epsilon, bids, largest, out, after):
    rows, experts = values.shape
    total = before[...] + jnp.maximum(jnp.max(bids[...], axis=0), 0.0)
    after[...] = total
    choice, claims, bid, _, _ = choose(values[...] - total, epsilon[0])
    count = jnp.sum(claims.astype(jnp.float32), axis=0, keepdims=True)
    wide = (out.shape[2] - experts) // 2
    lane = lax.broadcasted_iota(jnp.int32, (rows, wide), 1)
    same = lane == lax.broadcasted_iota(jnp.int32, (rows, wide), 0)
    choices = jnp.sum(jnp.where(same, choice, 0.0), axis=0, keepdims=True)
    choices = jnp.where(lane[:1] == rows, largest[:, :1], choices)
    offered = jnp.sum(jnp.where(same, bid, 0.0), axis=0, keepdims=True)
    line = jnp.concatenate([count, choices, offered], axis=1)
    out[...] = jnp.broadcast_to(line[None], out.shape)


def pass_on(line, *refs):
    pass


def released(line, parcels):
    return pl.pallas_call(
        pass_on,
        out_shape=[jax.ShapeDtypeStruct(p.shape, p.dtype) for p in parcels],
        in_specs=[ANY] * (1 + len(parcels)),
        out_specs=[ANY] * len(parcels),
        input_output_aliases={1 + i: i for i in range(len(parcels))},
        compiler_params=room(4),
        cost_estimate=pl.CostEstimate(flops=1000000000, bytes_accessed=4096, transcendentals=0),
        name="released",
    )(line, *parcels)


def fill(line, value, out):
    out[...] = value[...]


def filled(line, value, flops):
    return pl.pallas_call(
        fill,
        out_shape=jax.ShapeDtypeStruct(value.shape, value.dtype),
        in_specs=[ANY, VMEM],
        out_specs=VMEM,
        compiler_params=room(4),
        cost_estimate=pl.CostEstimate(flops=flops, bytes_accessed=4096, transcendentals=0),
        name="filled",
    )(line, value)


def add_up(ne, rows, top, at, place, info, columns, total_out, short_out):
    height = total_out.shape[0]
    ids = place[0] + top + lax.broadcasted_iota(jnp.int32, (height, rows), 0)
    ids = ids.astype(jnp.float32)
    total = jnp.zeros(total_out.shape, jnp.float32)
    for k, features in enumerate(columns):
        for c in range(ne):
            chosen = info[place[2 + k] * ne + c, :, at : at + rows]
            hot = jnp.where(ids == chosen, 1.0, 0.0).astype(jnp.bfloat16)
            total += jnp.dot(
                hot, features[c * rows : (c + 1) * rows, :], preferred_element_type=jnp.float32
            )
    total_out[...] = total
    short_out[...] = total.astype(short_out.dtype)


def more_sums(ne, rows, top, at, place, info, *refs):
    add_up(ne, rows, top, at, place, info, refs[:-2], *refs[-2:])


def finish(ne, rows, outer, experts, place, info, *refs):
    columns, (best, counts_out, fits, *sums) = refs[:-6], refs[-5:]
    own = counts_out.shape[0]
    marks = [info[place[1] * ne + c, :, experts : experts + rows] for c in range(ne)]
    best[...] = jnp.concatenate(marks, axis=1).astype(jnp.int32).reshape(best.shape)
    add_up(ne, rows, 0, experts, place, info, columns, *sums)
    share = info.shape[0] // outer
    each = [jnp.sum(info[i * share : (i + 1) * share, :, :experts], axis=0) for i in range(outer)]
    largest = jnp.max(info[:, :, experts + rows : experts + rows + 1])
    fullest = jnp.max(functools.reduce(jnp.maximum, each))
    fits[0] = jnp.where(fullest * largest <= 256.0, 1, 0)
    counts = functools.reduce(jnp.add, each)
    expert_row = place[0] + lax.broadcasted_iota(jnp.int32, (own, experts), 0)
    lane = lax.broadcasted_iota(jnp.int32, (own, experts), 1)
    counts = jnp.sum(jnp.where(expert_row == lane, counts, 0.0), axis=1, keepdims=True)
    counts_out[...] = jnp.broadcast_to(jnp.maximum(counts, 1.0), counts_out.shape)


def settle(rows, experts, place, info, before, prices, counts, final, holder, same_counts):
    own = prices.shape[1]
    wide = (info.shape[2] - experts) // 2
    devices = info.shape[0]
    ids = (place[0] + lax.broadcasted_iota(jnp.int32, (own, rows), 0)).astype(jnp.float32)
    offset = lax.broadcasted_iota(jnp.int32, (own, rows), 1).astype(jnp.float32)

    def claimed(n):
        return ids == info[n, :, experts : experts + rows]

    def offered(n):
        return info[n, :, experts + wide : experts + wide + rows]

    def higher(n, top):
        return jnp.maximum(top, jnp.where(claimed(n), offered(n), -1.0))

    top = lax.fori_loop(0, devices, higher, jnp.full((own, rows), -1.0, jnp.float32), unroll=4)
    top = jnp.max(top, axis=1, keepdims=True)

    def earlier(n, first):
        token = (n * rows).astype(jnp.float32) + offset
        return jnp.minimum(first, jnp.where(claimed(n) & (offered(n) == top), token, far))

    first = lax.fori_loop(0, devices, earlier, jnp.full((own, rows), far, jnp.float32), unroll=4)
    first = jnp.min(first, axis=1, keepdims=True)
    same = lax.broadcasted_iota(jnp.int32, (own, own), 0) == lax.broadcasted_iota(jnp.int32, (own, own), 1)
    raised = jnp.sum(jnp.where(same, jnp.maximum(top, 0.0), 0.0), axis=0, keepdims=True)
    held = jnp.sum(jnp.where(same, jnp.where(top > 0, first, -1.0), 0.0), axis=0, keepdims=True)
    expert_row = place[0] + lax.broadcasted_iota(jnp.int32, (own, experts), 0)
    lane = lax.broadcasted_iota(jnp.int32, (own, experts), 1)
    so_far = jnp.sum(jnp.where(expert_row == lane, before[...], 0.0), axis=1, keepdims=True)
    so_far = jnp.sum(jnp.where(same, so_far, 0.0), axis=0, keepdims=True)
    final[...] = prices[...] + so_far + raised
    holder[...] = held.astype(jnp.int32)


def blend(row, centroids, counts, *refs):
    sums, out = refs[:-1], refs[-1]
    rows, cols = out.shape
    total = functools.reduce(jnp.add, [s[...].astype(jnp.float32) for s in sums])
    old = centroids[row : row + rows, :].astype(jnp.float32)
    share = counts[row : row + rows, :1]
    out[...] = (0.5 * old + 0.5 * total / share).astype(out.dtype)


def assemble(plan, extras, base, *refs):
    pieces, out, sem = refs[: len(plan)], refs[-2 - extras], refs[-1]
    cols = pieces[0].shape[-1]
    copies = [
        pltpu.make_async_copy(refs[-2 - 2 * extras + i], refs[-1 - extras + i], sem.at[i])
        for i in range(extras)
    ]
    for piece, (row, slots) in zip(pieces, plan):
        for i, slot in enumerate(slots):
            col = pl.multiple_of(base[slot] * cols, cols)
            copies.append(
                pltpu.make_async_copy(
                    piece.at[i], out.at[pl.ds(row, piece.shape[1]), pl.ds(col, cols)], sem.at[len(copies)]
                )
            )
    for copy in copies:
        copy.start()
    for copy in copies:
        copy.wait()


PARTS = 2
TURNS = ((0, 1), (2, 1))


def spread_out(dp, inner, wide, sums, short, mine, counts, carried):
    bits = inner.bit_length() - 1
    member = lax.axis_index("dp") % inner
    core = lax.axis_index("expert")

    def move(value, masks):
        pairs = [(i * 2 + c, (i ^ masks[c]) * 2 + c) for i in range(dp) for c in range(2)]
        return lax.ppermute(value, ("dp", "expert"), pairs)

    parts = len(sums)
    cols = sums[0].shape[1]
    heights = [s.shape[0] for s in sums]
    tops = [sum(heights[:p]) for p in range(parts)]
    sent = sums if wide else short
    other = [move(s, (inner, inner)) for s in sent] if inner < dp else None
    held = []
    for p in range(parts):
        terms = [sums[p], other[p]] if other else [sums[p]]
        fresh = pl.pallas_call(
            functools.partial(blend, tops[p]),
            out_shape=jax.ShapeDtypeStruct((heights[p], cols), mine.dtype),
            in_specs=[VMEM] * (2 + len(terms)),
            out_specs=VMEM,
            compiler_params=room(4),
            name="blend",
        )(mine, counts, *terms)
        held.append([(fresh[None], [(0, 0)])])

    def join(values):
        return values[0] if len(values) == 1 else jnp.concatenate(values)

    late = [[] for _ in range(parts)]
    for stage in range(bits):
        for p in range(parts):
            masks = [1 << (stage + t) % bits for t in TURNS[p]]

            def onward(entries):
                where = [m for _, ms in entries for m in ms]
                value = move(join([v for v, _ in entries]), masks)
                return value, [(a ^ masks[0], b ^ masks[1]) for a, b in where]

            if stage < bits - 1 or stage < 2:
                held[p].append(onward(held[p]))
            else:
                late[p] = [onward(held[p][:-1]), onward(held[p][-1:])]
    def write(whole, groups, extras=()):
        pieces, plan, slots = [], [], []
        for p, group in enumerate(groups):
            for value, where in group:
                pieces.append(value)
                plan.append((tops[p], [len(slots) + i for i in range(len(where))]))
                slots += where
        base = jnp.stack([member ^ jnp.where(core == 0, a, b) for a, b in slots]).astype(jnp.int32)
        before = [] if whole is None else [whole]
        outs = pl.pallas_call(
            functools.partial(assemble, plan, len(extras)),
            out_shape=[jax.ShapeDtypeStruct((sum(heights), inner * cols), mine.dtype)]
            + [jax.ShapeDtypeStruct(e.shape, e.dtype) for e in extras],
            in_specs=[SMEM] + [VMEM] * len(pieces) + [ANY] * len(before) + [VMEM] * len(extras),
            out_specs=[ANY] + [pl.BlockSpec(memory_space=pltpu.HBM)] * len(extras),
            scratch_shapes=[pltpu.SemaphoreType.DMA((len(slots) + len(extras),))],
            input_output_aliases={1 + len(pieces): 0} if before else {},
            compiler_params=room(4),
            name="assemble",
        )(base, *pieces, *before, *extras)
        return outs if extras else outs[0]

    whole = write(None, held)
    for p in range(parts - 1):
        whole = write(whole, [late[p] if q == p else [] for q in range(parts)])
    return write(whole, [[]] * (parts - 1) + [late[-1]], carried)


def body(dp, ne, tokens, centroids, prices, epsilon):
    f32 = jnp.float32
    local_tokens, width = tokens.shape
    own = centroids.shape[0]
    experts = own * ne
    devices = dp * ne
    rows = local_tokens // ne
    cols = width // dp
    dp_at, expert_at = lax.axis_index("dp"), lax.axis_index("expert")
    everywhere = ("dp", "expert")
    outer = 2 if ne == 2 and dp % 16 == 0 and dp & (dp - 1) == 0 else 1
    inner = dp // outer
    cols = width // inner
    paired = outer == 2 and cols % 128 == 0 and own % 32 == 0
    swap = [(0, 1), (1, 0)]

    def shape(*sizes, dtype=f32):
        return jax.ShapeDtypeStruct(sizes, dtype)

    line, spread = shape(1, experts), shape(devices, 1, experts)
    at = jnp.stack([expert_at]).astype(jnp.int32)
    if paired:
        half = inner // 2
        chunks = 4
        masks = [(k, inner - 1 - k) for k in range(half)]
        theirs = [dp_at ^ jnp.where(expert_at == 0, *mask) for mask in masks]
        place = [expert_at, 1 - expert_at, dp_at % inner] + [t % inner for t in theirs]
        place = jnp.stack(place).astype(jnp.int32)
        kept, sent, mine, largest, *parcels = pl.pallas_call(
            functools.partial(opening, chunks),
            out_shape=[shape(rows, own)] * 2
            + [shape(own, cols, dtype=centroids.dtype), shape(1, 128)]
            + [shape(local_tokens, cols, dtype=tokens.dtype)] * half,
            in_specs=[SMEM, ANY, ANY, VMEM],
            out_specs=[VMEM] * (4 + half),
            scratch_shapes=[
                pltpu.VMEM(tokens.shape, tokens.dtype),
                pltpu.VMEM(centroids.shape, centroids.dtype),
                pltpu.VMEM((local_tokens, own), f32),
                pltpu.SemaphoreType.DMA((2, chunks)),
            ],
            compiler_params=room(52),
            name="opening",
        )(place, tokens, centroids, prices.reshape(1, own))
        received = lax.ppermute(sent, "expert", swap)
        values, bids = pl.pallas_call(
            first_round,
            out_shape=(shape(rows, experts), spread),
            in_specs=[SMEM, VMEM, VMEM, SMEM],
            out_specs=(VMEM, VMEM),
            compiler_params=room(4),
            name="first_round",
        )(at, kept, received, epsilon)
        columns = [None] * half

        def sent_on(k):
            pairs = [(i * 2 + c, (i ^ masks[k][c]) * 2 + c) for i in range(dp) for c in range(2)]
            columns[k] = lax.ppermute(parcels[k], everywhere, pairs)

        sources = theirs + [dp_at ^ jnp.where(expert_at == 0, *mask[::-1]) for mask in masks]
    else:
        parcels = tokens.reshape(local_tokens, dp, cols).transpose(1, 0, 2)
        columns = lax.all_to_all(parcels, "dp", 0, 0, tiled=True)
        columns = [columns.reshape(dp * local_tokens, cols)[i * local_tokens :][:local_tokens] for i in range(dp)]
        sources = list(range(dp))
        mine = lax.dynamic_slice_in_dim(centroids, dp_at * cols, cols, 1)
        largest = jnp.full((1, 128), jnp.max(jnp.abs(tokens)).astype(f32))
        part = lax.dot_general(
            tokens, centroids, (((1,), (1,)), ((), ())), preferred_element_type=f32
        ) * 0.015625 - prices
        part = lax.all_to_all(part, "expert", 0, 1, tiled=True)
        values, bids = pl.pallas_call(
            first_round_whole,
            out_shape=(shape(rows, experts), spread),
            in_specs=[SMEM, VMEM, SMEM],
            out_specs=(VMEM, VMEM),
            compiler_params=room(4),
            name="first_round",
        )(at, part, epsilon)

    total = jnp.zeros((1, experts), f32)
    waiting = list(range(half))[::-1] if paired else []
    for _ in range(ROUNDS - 2):
        for k in waiting[:-2]:
            sent_on(k)
        waiting = waiting[-2:]
        bids = lax.all_to_all(bids, everywhere, 0, 0, tiled=True)
        bids, total = pl.pallas_call(
            next_round,
            out_shape=(spread, line),
            in_specs=[VMEM, VMEM, SMEM, VMEM],
            out_specs=(VMEM, VMEM),
            compiler_params=room(4),
            name="next_round",
        )(values, total, epsilon, bids)
    if paired:
        parcels[: len(waiting)] = released(total, parcels[: len(waiting)])
    for k in waiting:
        sent_on(k)
    bids = lax.all_to_all(bids, everywhere, 0, 0, tiled=True)
    wide = (rows // 128 + 1) * 128
    largest = filled(total, largest, 8000000000)
    info, total = pl.pallas_call(
        last_round,
        out_shape=(shape(devices, 1, experts + 2 * wide), line),
        in_specs=[VMEM, VMEM, SMEM, VMEM, VMEM],
        out_specs=(VMEM, VMEM),
        compiler_params=room(8),
        name="last_round",
    )(values, total, epsilon, bids, largest)
    if paired:
        columns += [lax.ppermute(c, "expert", swap) for c in columns]
    info = lax.all_to_all(info, everywhere, 0, 0, tiled=True)

    timed = filled(total, largest, 8000000000)
    place = jnp.stack([expert_at * own, dp_at] + sources).astype(jnp.int32)
    low = own // 32 * 16 if own % 32 == 0 else own
    heights = [low, own - low] if paired else [own]

    def two(height):
        return (shape(height, cols), shape(height, cols, dtype=jnp.bfloat16))

    best, counts, fits, *sums = pl.pallas_call(
        functools.partial(finish, ne, rows, outer, experts),
        out_shape=(
            shape(local_tokens, dtype=jnp.int32),
            shape(own, 128),
            shape(1, dtype=jnp.int32),
        )
        + two(heights[0]),
        in_specs=[SMEM] + [VMEM] * (1 + len(columns)) + [ANY],
        out_specs=(VMEM, VMEM, SMEM, VMEM, VMEM),
        compiler_params=room(16),
        name="finish",
    )(place, info, *columns, timed)

    def settled(place, info, total, prices, counts):
        return pl.pallas_call(
            functools.partial(settle, rows, experts),
            out_shape=(shape(1, own), shape(1, own, dtype=jnp.int32), shape(own, 128)),
            in_specs=[SMEM, VMEM, VMEM, VMEM, ANY],
            out_specs=(VMEM, VMEM, ANY),
            input_output_aliases={4: 2},
            compiler_params=room(6),
            name="settle",
        )(place, info, total, prices, counts)

    prices = prices.reshape(1, own)
    if paired:

        def rest(wide, place, info, total, prices, columns, sums, mine, counts):
            more = pl.pallas_call(
                functools.partial(more_sums, ne, rows, heights[0], experts),
                out_shape=two(heights[1]),
                in_specs=[SMEM] + [VMEM] * (1 + len(columns)),
                out_specs=(VMEM, VMEM),
                compiler_params=room(8),
                name="more_sums",
            )(place, info, *columns)
            pairs = list(zip(sums, more))
            final, holder, counts = settled(place, info, total, prices, counts)
            pair = (final, holder)
            return spread_out(dp, inner, wide, pairs[0], pairs[1], mine, counts, pair)

        refreshed, final, holder = lax.switch(
            fits[0],
            [functools.partial(rest, True), functools.partial(rest, False)],
            place, info, total, prices, columns, sums, mine, counts,
        )
    else:
        final, holder, counts = settled(place, info, total, prices, counts)
        fresh = 0.5 * mine.astype(f32) + 0.5 * sums[0] / counts[:, :1]
        refreshed = lax.all_gather(fresh.astype(centroids.dtype), "dp", axis=1, tiled=True)
    return final[0], best, holder[0], refreshed


def solution(mesh):
    placed = (P("dp", None), P("expert", None), P("expert"), P())
    return jax.shard_map(
        functools.partial(body, mesh.shape["dp"], mesh.shape["expert"]),
        mesh=mesh,
        in_specs=placed,
        out_specs=(P("expert"), P("dp"), P("expert"), P("expert", None)),
        check_vma=False,
    )
```

```python
import functools

import jax
import jax.numpy as jnp
from jax import lax
from jax.experimental import pallas as pl
from jax.experimental.pallas import tpu as pltpu
from jax.sharding import PartitionSpec as P

ROUNDS = 3

lowest = -1e30
far = 1073741824.0
VMEM = pl.BlockSpec(memory_space=pltpu.VMEM)
SMEM = pl.BlockSpec(memory_space=pltpu.SMEM)
ANY = pl.BlockSpec(memory_space=pl.ANY)


def room(mebibytes):
    return pltpu.CompilerParams(vmem_limit_bytes=mebibytes * 1024 * 1024)


def opening(chunks, place, tokens, centroids, prices, kept, sent, mine, largest, *refs):
    parcels, (tok, cen, acc, sem) = refs[:-4], refs[-4:]
    rows, cols = kept.shape[0], mine.shape[1]
    step = tok.shape[1] // chunks
    copies = []
    for i in range(chunks):
        part = pl.ds(i * step, step)
        copies.append((
            pltpu.make_async_copy(centroids.at[:, part], cen.at[:, part], sem.at[0, i]),
            pltpu.make_async_copy(tokens.at[:, part], tok.at[:, part], sem.at[1, i]),
        ))
    for pair in copies:
        pair[0].start()
        pair[1].start()
    for i, pair in enumerate(copies):
        pair[0].wait()
        pair[1].wait()
        part = slice(i * step, (i + 1) * step)
        product = lax.dot_general(
            tok[:, part], cen[:, part], (((1,), (1,)), ((), ())), preferred_element_type=jnp.float32
        )
        size = jnp.max(jnp.abs(tok[:, part]).reshape(-1, 16, step), axis=0)
        peak = size if i == 0 else jnp.maximum(peak, size)
        if i:
            acc[...] += product
        else:
            acc[...] = product
    peak = jnp.max(peak.astype(jnp.float32), axis=0, keepdims=True)
    largest[...] = jnp.broadcast_to(jnp.max(peak, axis=1, keepdims=True), largest.shape)
    for out, at in ((sent, 1), (kept, 0)):
        row = pl.multiple_of(place[at] * rows, rows)
        out[...] = acc[pl.ds(row, rows), :] * 0.015625 - prices[...]
    mine[...] = cen[:, pl.ds(pl.multiple_of(place[2] * cols, cols), cols)]
    for k, parcel in enumerate(parcels):
        parcel[...] = tok[:, pl.ds(pl.multiple_of(place[3 + k] * cols, cols), cols)]


def choose(values, eps):
    ids = lax.broadcasted_iota(jnp.int32, values.shape, 1).astype(jnp.float32)
    top = jnp.max(values, axis=1, keepdims=True)
    choice = jnp.min(jnp.where(values == top, ids, far), axis=1, keepdims=True)
    claims = ids == choice
    second = jnp.max(jnp.where(claims, lowest, values), axis=1, keepdims=True)
    bid = top - second + eps
    bids = jnp.where(claims, bid, -1.0)
    return choice, claims, bid, bids, jnp.max(bids, axis=0, keepdims=True)


def first_round(place, kept, theirs, epsilon, values, out):
    if theirs is None:
        values[...] = kept[...]
    else:
        own = kept.shape[1]
        swapped = place[0] != 0
        values[:, :own] = jnp.where(swapped, theirs[...], kept[...])
        values[:, own:] = jnp.where(swapped, kept[...], theirs[...])
    raised = choose(values[...], epsilon[0])[-1]
    out[...] = jnp.broadcast_to(raised[None], out.shape)


def first_round_whole(place, kept, epsilon, values, out):
    first_round(place, kept, None, epsilon, values, out)


def next_round(values, before, epsilon, bids, out, after):
    total = before[...] + jnp.maximum(jnp.max(bids[...], axis=0), 0.0)
    after[...] = total
    raised = choose(values[...] - total, epsilon[0])[-1]
    out[...] = jnp.broadcast_to(raised[None], out.shape)


def last_round(values, before, epsilon, bids, largest, out, after):
    rows, experts = values.shape
    total = before[...] + jnp.maximum(jnp.max(bids[...], axis=0), 0.0)
    after[...] = total
    choice, claims, bid, _, _ = choose(values[...] - total, epsilon[0])
    count = jnp.sum(claims.astype(jnp.float32), axis=0, keepdims=True)
    wide = (out.shape[2] - experts) // 2
    lane = lax.broadcasted_iota(jnp.int32, (rows, wide), 1)
    same = lane == lax.broadcasted_iota(jnp.int32, (rows, wide), 0)
    choices = jnp.sum(jnp.where(same, choice, 0.0), axis=0, keepdims=True)
    choices = jnp.where(lane[:1] == rows, largest[:, :1], choices)
    offered = jnp.sum(jnp.where(same, bid, 0.0), axis=0, keepdims=True)
    line = jnp.concatenate([count, choices, offered], axis=1)
    out[...] = jnp.broadcast_to(line[None], out.shape)


def pass_on(line, *refs):
    pass


def released(line, parcels):
    return pl.pallas_call(
        pass_on,
        out_shape=[jax.ShapeDtypeStruct(p.shape, p.dtype) for p in parcels],
        in_specs=[ANY] * (1 + len(parcels)),
        out_specs=[ANY] * len(parcels),
        input_output_aliases={1 + i: i for i in range(len(parcels))},
        compiler_params=room(4),
        cost_estimate=pl.CostEstimate(flops=1000000000, bytes_accessed=4096, transcendentals=0),
        name="released",
    )(line, *parcels)


def fill(line, value, out):
    out[...] = value[...]


def filled(line, value, flops):
    return pl.pallas_call(
        fill,
        out_shape=jax.ShapeDtypeStruct(value.shape, value.dtype),
        in_specs=[ANY, VMEM],
        out_specs=VMEM,
        compiler_params=room(4),
        cost_estimate=pl.CostEstimate(flops=flops, bytes_accessed=4096, transcendentals=0),
        name="filled",
    )(line, value)


def add_up(ne, rows, top, at, place, info, columns, total_out, short_out):
    height = total_out.shape[0]
    ids = place[0] + top + lax.broadcasted_iota(jnp.int32, (height, rows), 0)
    ids = ids.astype(jnp.float32)
    total = jnp.zeros(total_out.shape, jnp.float32)
    for k, features in enumerate(columns):
        for c in range(ne):
            chosen = info[place[2 + k] * ne + c, :, at : at + rows]
            hot = jnp.where(ids == chosen, 1.0, 0.0).astype(jnp.bfloat16)
            total += jnp.dot(
                hot, features[c * rows : (c + 1) * rows, :], preferred_element_type=jnp.float32
            )
    total_out[...] = total
    short_out[...] = total.astype(short_out.dtype)


def more_sums(ne, rows, top, at, place, info, *refs):
    add_up(ne, rows, top, at, place, info, refs[:-2], *refs[-2:])


def finish(ne, rows, outer, experts, place, info, *refs):
    columns, (best, counts_out, fits, *sums) = refs[:-6], refs[-5:]
    own = counts_out.shape[0]
    marks = [info[place[1] * ne + c, :, experts : experts + rows] for c in range(ne)]
    best[...] = jnp.concatenate(marks, axis=1).astype(jnp.int32).reshape(best.shape)
    add_up(ne, rows, 0, experts, place, info, columns, *sums)
    share = info.shape[0] // outer
    each = [jnp.sum(info[i * share : (i + 1) * share, :, :experts], axis=0) for i in range(outer)]
    largest = jnp.max(info[:, :, experts + rows : experts + rows + 1])
    fullest = jnp.max(functools.reduce(jnp.maximum, each))
    fits[0] = jnp.where(fullest * largest <= 256.0, 1, 0)
    counts = functools.reduce(jnp.add, each)
    expert_row = place[0] + lax.broadcasted_iota(jnp.int32, (own, experts), 0)
    lane = lax.broadcasted_iota(jnp.int32, (own, experts), 1)
    counts = jnp.sum(jnp.where(expert_row == lane, counts, 0.0), axis=1, keepdims=True)
    counts_out[...] = jnp.broadcast_to(jnp.maximum(counts, 1.0), counts_out.shape)


def settle(rows, experts, place, info, before, prices, counts, final, holder, same_counts):
    own = prices.shape[1]
    wide = (info.shape[2] - experts) // 2
    devices = info.shape[0]
    ids = (place[0] + lax.broadcasted_iota(jnp.int32, (own, rows), 0)).astype(jnp.float32)
    offset = lax.broadcasted_iota(jnp.int32, (own, rows), 1).astype(jnp.float32)

    def claimed(n):
        return ids == info[n, :, experts : experts + rows]

    def offered(n):
        return info[n, :, experts + wide : experts + wide + rows]

    def higher(n, top):
        return jnp.maximum(top, jnp.where(claimed(n), offered(n), -1.0))

    top = lax.fori_loop(0, devices, higher, jnp.full((own, rows), -1.0, jnp.float32), unroll=4)
    top = jnp.max(top, axis=1, keepdims=True)

    def earlier(n, first):
        token = (n * rows).astype(jnp.float32) + offset
        return jnp.minimum(first, jnp.where(claimed(n) & (offered(n) == top), token, far))

    first = lax.fori_loop(0, devices, earlier, jnp.full((own, rows), far, jnp.float32), unroll=4)
    first = jnp.min(first, axis=1, keepdims=True)
    same = lax.broadcasted_iota(jnp.int32, (own, own), 0) == lax.broadcasted_iota(jnp.int32, (own, own), 1)
    raised = jnp.sum(jnp.where(same, jnp.maximum(top, 0.0), 0.0), axis=0, keepdims=True)
    held = jnp.sum(jnp.where(same, jnp.where(top > 0, first, -1.0), 0.0), axis=0, keepdims=True)
    expert_row = place[0] + lax.broadcasted_iota(jnp.int32, (own, experts), 0)
    lane = lax.broadcasted_iota(jnp.int32, (own, experts), 1)
    so_far = jnp.sum(jnp.where(expert_row == lane, before[...], 0.0), axis=1, keepdims=True)
    so_far = jnp.sum(jnp.where(same, so_far, 0.0), axis=0, keepdims=True)
    final[...] = (prices[...] + so_far + raised).reshape(final.shape)
    holder[...] = held.astype(jnp.int32).reshape(holder.shape)


def blend(row, centroids, counts, *refs):
    sums, out = refs[:-1], refs[-1]
    rows, cols = out.shape
    total = functools.reduce(jnp.add, [s[...].astype(jnp.float32) for s in sums])
    old = centroids[row : row + rows, :].astype(jnp.float32)
    share = counts[row : row + rows, :1]
    out[...] = (0.5 * old + 0.5 * total / share).astype(out.dtype)


def assemble(plan, extras, base, *refs):
    pieces, out, sem = refs[: len(plan)], refs[-2 - extras], refs[-1]
    cols = pieces[0].shape[-1]
    copies = [
        pltpu.make_async_copy(refs[-2 - 2 * extras + i], refs[-1 - extras + i], sem.at[i])
        for i in range(extras)
    ]
    for piece, (row, slots) in zip(pieces, plan):
        for i, slot in enumerate(slots):
            col = pl.multiple_of(base[slot] * cols, cols)
            copies.append(
                pltpu.make_async_copy(
                    piece.at[i], out.at[pl.ds(row, piece.shape[1]), pl.ds(col, cols)], sem.at[len(copies)]
                )
            )
    for copy in copies:
        copy.start()
    for copy in copies:
        copy.wait()


PARTS = 2
TURNS = ((0, 1), (2, 1))


def spread_out(dp, inner, wide, sums, short, mine, counts, carried):
    bits = inner.bit_length() - 1
    member = lax.axis_index("dp") % inner
    core = lax.axis_index("expert")

    def move(value, masks):
        pairs = [(i * 2 + c, (i ^ masks[c]) * 2 + c) for i in range(dp) for c in range(2)]
        return lax.ppermute(value, ("dp", "expert"), pairs)

    parts = len(sums)
    cols = sums[0].shape[1]
    heights = [s.shape[0] for s in sums]
    tops = [sum(heights[:p]) for p in range(parts)]
    sent = sums if wide else short
    other = [move(s, (inner, inner)) for s in sent] if inner < dp else None
    held = []
    for p in range(parts):
        terms = [sums[p], other[p]] if other else [sums[p]]
        fresh = pl.pallas_call(
            functools.partial(blend, tops[p]),
            out_shape=jax.ShapeDtypeStruct((heights[p], cols), mine.dtype),
            in_specs=[VMEM] * (2 + len(terms)),
            out_specs=VMEM,
            compiler_params=room(4),
            name="blend",
        )(mine, counts, *terms)
        held.append([(fresh[None], [(0, 0)])])

    def join(values):
        return values[0] if len(values) == 1 else jnp.concatenate(values)

    late = [[] for _ in range(parts)]
    for stage in range(bits):
        for p in range(parts):
            masks = [1 << (stage + t) % bits for t in TURNS[p]]

            def onward(entries):
                where = [m for _, ms in entries for m in ms]
                value = move(join([v for v, _ in entries]), masks)
                return value, [(a ^ masks[0], b ^ masks[1]) for a, b in where]

            if stage < bits - 1 or stage < 2:
                held[p].append(onward(held[p]))
            else:
                late[p] = [onward(held[p][:-1]), onward(held[p][-1:])]
    def write(whole, groups, extras=()):
        pieces, plan, slots = [], [], []
        for p, group in enumerate(groups):
            for value, where in group:
                pieces.append(value)
                plan.append((tops[p], [len(slots) + i for i in range(len(where))]))
                slots += where
        base = jnp.stack([member ^ jnp.where(core == 0, a, b) for a, b in slots]).astype(jnp.int32)
        before = [] if whole is None else [whole]
        outs = pl.pallas_call(
            functools.partial(assemble, plan, len(extras)),
            out_shape=[jax.ShapeDtypeStruct((sum(heights), inner * cols), mine.dtype)]
            + [jax.ShapeDtypeStruct(e.shape, e.dtype) for e in extras],
            in_specs=[SMEM] + [VMEM] * len(pieces) + [ANY] * len(before) + [VMEM] * len(extras),
            out_specs=[ANY] + [pl.BlockSpec(memory_space=pltpu.HBM)] * len(extras),
            scratch_shapes=[pltpu.SemaphoreType.DMA((len(slots) + len(extras),))],
            input_output_aliases={1 + len(pieces): 0} if before else {},
            compiler_params=room(4),
            name="assemble",
        )(base, *pieces, *before, *extras)
        return outs if extras else outs[0]

    whole = write(None, held)
    for p in range(parts - 1):
        whole = write(whole, [late[p] if q == p else [] for q in range(parts)])
    return write(whole, [[]] * (parts - 1) + [late[-1]], carried)


def body(dp, ne, tokens, centroids, prices, epsilon):
    f32 = jnp.float32
    local_tokens, width = tokens.shape
    own = centroids.shape[0]
    experts = own * ne
    devices = dp * ne
    rows = local_tokens // ne
    cols = width // dp
    dp_at, expert_at = lax.axis_index("dp"), lax.axis_index("expert")
    everywhere = ("dp", "expert")
    outer = 2 if ne == 2 and dp % 16 == 0 and dp & (dp - 1) == 0 else 1
    inner = dp // outer
    cols = width // inner
    paired = outer == 2 and cols % 128 == 0 and own % 32 == 0
    swap = [(0, 1), (1, 0)]

    def shape(*sizes, dtype=f32):
        return jax.ShapeDtypeStruct(sizes, dtype)

    line, spread = shape(1, experts), shape(devices, 1, experts)
    at = jnp.stack([expert_at]).astype(jnp.int32)
    if paired:
        half = inner // 2
        chunks = 4
        masks = [(k, inner - 1 - k) for k in range(half)]
        theirs = [dp_at ^ jnp.where(expert_at == 0, *mask) for mask in masks]
        place = [expert_at, 1 - expert_at, dp_at % inner] + [t % inner for t in theirs]
        place = jnp.stack(place).astype(jnp.int32)
        kept, sent, mine, largest, *parcels = pl.pallas_call(
            functools.partial(opening, chunks),
            out_shape=[shape(rows, own)] * 2
            + [shape(own, cols, dtype=centroids.dtype), shape(1, 128)]
            + [shape(local_tokens, cols, dtype=tokens.dtype)] * half,
            in_specs=[SMEM, ANY, ANY, VMEM],
            out_specs=[VMEM] * (4 + half),
            scratch_shapes=[
                pltpu.VMEM(tokens.shape, tokens.dtype),
                pltpu.VMEM(centroids.shape, centroids.dtype),
                pltpu.VMEM((local_tokens, own), f32),
                pltpu.SemaphoreType.DMA((2, chunks)),
            ],
            compiler_params=room(52),
            name="opening",
        )(place, tokens, centroids, prices.reshape(1, own))
        received = lax.ppermute(sent, "expert", swap)
        values, bids = pl.pallas_call(
            first_round,
            out_shape=(shape(rows, experts), spread),
            in_specs=[SMEM, VMEM, VMEM, SMEM],
            out_specs=(VMEM, VMEM),
            compiler_params=room(4),
            name="first_round",
        )(at, kept, received, epsilon)
        columns = [None] * half

        def sent_on(k):
            pairs = [(i * 2 + c, (i ^ masks[k][c]) * 2 + c) for i in range(dp) for c in range(2)]
            columns[k] = lax.ppermute(parcels[k], everywhere, pairs)

        sources = theirs + [dp_at ^ jnp.where(expert_at == 0, *mask[::-1]) for mask in masks]
    else:
        parcels = tokens.reshape(local_tokens, dp, cols).transpose(1, 0, 2)
        columns = lax.all_to_all(parcels, "dp", 0, 0, tiled=True)
        columns = [columns.reshape(dp * local_tokens, cols)[i * local_tokens :][:local_tokens] for i in range(dp)]
        sources = list(range(dp))
        mine = lax.dynamic_slice_in_dim(centroids, dp_at * cols, cols, 1)
        largest = jnp.full((1, 128), jnp.max(jnp.abs(tokens)).astype(f32))
        part = lax.dot_general(
            tokens, centroids, (((1,), (1,)), ((), ())), preferred_element_type=f32
        ) * 0.015625 - prices
        part = lax.all_to_all(part, "expert", 0, 1, tiled=True)
        values, bids = pl.pallas_call(
            first_round_whole,
            out_shape=(shape(rows, experts), spread),
            in_specs=[SMEM, VMEM, SMEM],
            out_specs=(VMEM, VMEM),
            compiler_params=room(4),
            name="first_round",
        )(at, part, epsilon)

    total = jnp.zeros((1, experts), f32)
    waiting = list(range(half))[::-1] if paired else []
    for _ in range(ROUNDS - 2):
        for k in waiting[:-2]:
            sent_on(k)
        waiting = waiting[-2:]
        bids = lax.all_to_all(bids, everywhere, 0, 0, tiled=True)
        bids, total = pl.pallas_call(
            next_round,
            out_shape=(spread, line),
            in_specs=[VMEM, VMEM, SMEM, VMEM],
            out_specs=(VMEM, VMEM),
            compiler_params=room(4),
            name="next_round",
        )(values, total, epsilon, bids)
    if paired:
        parcels[: len(waiting)] = released(total, parcels[: len(waiting)])
    for k in waiting:
        sent_on(k)
    bids = lax.all_to_all(bids, everywhere, 0, 0, tiled=True)
    wide = (rows // 128 + 1) * 128
    largest = filled(total, largest, 8000000000)
    info, total = pl.pallas_call(
        last_round,
        out_shape=(shape(devices, 1, experts + 2 * wide), line),
        in_specs=[VMEM, VMEM, SMEM, VMEM, VMEM],
        out_specs=(VMEM, VMEM),
        compiler_params=room(8),
        name="last_round",
    )(values, total, epsilon, bids, largest)
    if paired:
        columns += [lax.ppermute(c, "expert", swap) for c in columns]
    info = lax.all_to_all(info, everywhere, 0, 0, tiled=True)

    timed = filled(total, largest, 8000000000)
    place = jnp.stack([expert_at * own, dp_at] + sources).astype(jnp.int32)
    low = own // 16 * 9 // 16 * 16 if own % 32 == 0 else own
    heights = [low, own - low] if paired else [own]

    def two(height):
        return (shape(height, cols), shape(height, cols, dtype=jnp.bfloat16))

    best, counts, fits, *sums = pl.pallas_call(
        functools.partial(finish, ne, rows, outer, experts),
        out_shape=(
            shape(local_tokens, dtype=jnp.int32),
            shape(own, 128),
            shape(1, dtype=jnp.int32),
        )
        + two(heights[0]),
        in_specs=[SMEM] + [VMEM] * (1 + len(columns)) + [ANY],
        out_specs=(VMEM, VMEM, SMEM, VMEM, VMEM),
        compiler_params=room(16),
        name="finish",
    )(place, info, *columns, timed)

    def settled(place, info, total, prices, counts):
        return pl.pallas_call(
            functools.partial(settle, rows, experts),
            out_shape=(shape(own), shape(own, dtype=jnp.int32), shape(own, 128)),
            in_specs=[SMEM, VMEM, VMEM, VMEM, ANY],
            out_specs=(VMEM, VMEM, ANY),
            input_output_aliases={4: 2},
            compiler_params=room(6),
            name="settle",
        )(place, info, total, prices, counts)

    prices = prices.reshape(1, own)
    if paired:

        def rest(wide, place, info, total, prices, columns, sums, mine, counts):
            more = pl.pallas_call(
                functools.partial(more_sums, ne, rows, heights[0], experts),
                out_shape=two(heights[1]),
                in_specs=[SMEM] + [VMEM] * (1 + len(columns)),
                out_specs=(VMEM, VMEM),
                compiler_params=room(8),
                name="more_sums",
            )(place, info, *columns)
            pairs = list(zip(sums, more))
            final, holder, counts = settled(place, info, total, prices, counts)
            pair = (final, holder)
            return spread_out(dp, inner, wide, pairs[0], pairs[1], mine, counts, pair)

        refreshed, final, holder = lax.switch(
            fits[0],
            [functools.partial(rest, True), functools.partial(rest, False)],
            place, info, total, prices, columns, sums, mine, counts,
        )
    else:
        final, holder, counts = settled(place, info, total, prices, counts)
        fresh = 0.5 * mine.astype(f32) + 0.5 * sums[0] / counts[:, :1]
        refreshed = lax.all_gather(fresh.astype(centroids.dtype), "dp", axis=1, tiled=True)
    return final, best, holder, refreshed


def solution(mesh):
    placed = (P("dp", None), P("expert", None), P("expert"), P())
    return jax.shard_map(
        functools.partial(body, mesh.shape["dp"], mesh.shape["expert"]),
        mesh=mesh,
        in_specs=placed,
        out_specs=(P("expert"), P("dp"), P("expert"), P("expert", None)),
        check_vma=False,
    )
```

```python
import functools

import jax
import jax.numpy as jnp
from jax import lax
from jax.experimental import pallas as pl
from jax.experimental.pallas import tpu as pltpu
from jax.sharding import PartitionSpec as P

ROUNDS = 3

lowest = -1e30
far = 1073741824.0
VMEM = pl.BlockSpec(memory_space=pltpu.VMEM)
SMEM = pl.BlockSpec(memory_space=pltpu.SMEM)
ANY = pl.BlockSpec(memory_space=pl.ANY)


def room(mebibytes):
    return pltpu.CompilerParams(vmem_limit_bytes=mebibytes * 1024 * 1024)


def opening(chunks, place, tokens, centroids, prices, kept, sent, mine, largest, *refs):
    parcels, (tok, cen, acc, sem) = refs[:-4], refs[-4:]
    rows, cols = kept.shape[0], mine.shape[1]
    step = tok.shape[1] // chunks
    copies = []
    for i in range(chunks):
        part = pl.ds(i * step, step)
        copies.append((
            pltpu.make_async_copy(centroids.at[:, part], cen.at[:, part], sem.at[0, i]),
            pltpu.make_async_copy(tokens.at[:, part], tok.at[:, part], sem.at[1, i]),
        ))
    for pair in copies:
        pair[0].start()
        pair[1].start()
    for i, pair in enumerate(copies):
        pair[0].wait()
        pair[1].wait()
        part = slice(i * step, (i + 1) * step)
        product = lax.dot_general(
            tok[:, part], cen[:, part], (((1,), (1,)), ((), ())), preferred_element_type=jnp.float32
        )
        size = jnp.max(jnp.abs(tok[:, part]).reshape(-1, 16, step), axis=0)
        peak = size if i == 0 else jnp.maximum(peak, size)
        if i:
            acc[...] += product
        else:
            acc[...] = product
    peak = jnp.max(peak.astype(jnp.float32), axis=0, keepdims=True)
    largest[...] = jnp.broadcast_to(jnp.max(peak, axis=1, keepdims=True), largest.shape)
    for out, at in ((sent, 1), (kept, 0)):
        row = pl.multiple_of(place[at] * rows, rows)
        out[...] = acc[pl.ds(row, rows), :] * 0.015625 - prices[...]
    mine[...] = cen[:, pl.ds(pl.multiple_of(place[2] * cols, cols), cols)]
    for k, parcel in enumerate(parcels):
        parcel[...] = tok[:, pl.ds(pl.multiple_of(place[3 + k] * cols, cols), cols)]


def choose(values, eps):
    ids = lax.broadcasted_iota(jnp.int32, values.shape, 1).astype(jnp.float32)
    top = jnp.max(values, axis=1, keepdims=True)
    choice = jnp.min(jnp.where(values == top, ids, far), axis=1, keepdims=True)
    claims = ids == choice
    second = jnp.max(jnp.where(claims, lowest, values), axis=1, keepdims=True)
    bid = top - second + eps
    bids = jnp.where(claims, bid, -1.0)
    return choice, claims, bid, bids, jnp.max(bids, axis=0, keepdims=True)


def first_round(place, kept, theirs, epsilon, values, out):
    if theirs is None:
        values[...] = kept[...]
    else:
        own = kept.shape[1]
        swapped = place[0] != 0
        values[:, :own] = jnp.where(swapped, theirs[...], kept[...])
        values[:, own:] = jnp.where(swapped, kept[...], theirs[...])
    raised = choose(values[...], epsilon[0])[-1]
    out[...] = jnp.broadcast_to(raised[None], out.shape)


def first_round_whole(place, kept, epsilon, values, out):
    first_round(place, kept, None, epsilon, values, out)


def next_round(values, before, epsilon, bids, out, after):
    total = before[...] + jnp.maximum(jnp.max(bids[...], axis=0), 0.0)
    after[...] = total
    raised = choose(values[...] - total, epsilon[0])[-1]
    out[...] = jnp.broadcast_to(raised[None], out.shape)


def last_round(values, before, epsilon, bids, largest, out, after):
    rows, experts = values.shape
    total = before[...] + jnp.maximum(jnp.max(bids[...], axis=0), 0.0)
    after[...] = total
    choice, claims, bid, _, _ = choose(values[...] - total, epsilon[0])
    count = jnp.sum(claims.astype(jnp.float32), axis=0, keepdims=True)
    wide = (out.shape[2] - experts) // 2
    lane = lax.broadcasted_iota(jnp.int32, (rows, wide), 1)
    same = lane == lax.broadcasted_iota(jnp.int32, (rows, wide), 0)
    choices = jnp.sum(jnp.where(same, choice, 0.0), axis=0, keepdims=True)
    choices = jnp.where(lane[:1] == rows, largest[:, :1], choices)
    offered = jnp.sum(jnp.where(same, bid, 0.0), axis=0, keepdims=True)
    line = jnp.concatenate([count, choices, offered], axis=1)
    out[...] = jnp.broadcast_to(line[None], out.shape)


def pass_on(line, *refs):
    pass


def released(line, parcels):
    return pl.pallas_call(
        pass_on,
        out_shape=[jax.ShapeDtypeStruct(p.shape, p.dtype) for p in parcels],
        in_specs=[ANY] * (1 + len(parcels)),
        out_specs=[ANY] * len(parcels),
        input_output_aliases={1 + i: i for i in range(len(parcels))},
        compiler_params=room(4),
        cost_estimate=pl.CostEstimate(flops=1000000000, bytes_accessed=4096, transcendentals=0),
        name="released",
    )(line, *parcels)


def fill(line, value, out):
    out[...] = value[...]


def filled(line, value, flops):
    return pl.pallas_call(
        fill,
        out_shape=jax.ShapeDtypeStruct(value.shape, value.dtype),
        in_specs=[ANY, VMEM],
        out_specs=VMEM,
        compiler_params=room(4),
        cost_estimate=pl.CostEstimate(flops=flops, bytes_accessed=4096, transcendentals=0),
        name="filled",
    )(line, value)


def add_up(ne, rows, top, at, place, info, columns, total_out, short_out):
    height = total_out.shape[0]
    ids = place[0] + top + lax.broadcasted_iota(jnp.int32, (height, rows), 0)
    ids = ids.astype(jnp.float32)
    total = jnp.zeros(total_out.shape, jnp.float32)
    for k, features in enumerate(columns):
        for c in range(ne):
            chosen = info[place[2 + k] * ne + c, :, at : at + rows]
            hot = jnp.where(ids == chosen, 1.0, 0.0).astype(jnp.bfloat16)
            total += jnp.dot(
                hot, features[c * rows : (c + 1) * rows, :], preferred_element_type=jnp.float32
            )
    total_out[...] = total
    short_out[...] = total.astype(short_out.dtype)


def more_sums(ne, rows, top, at, place, info, *refs):
    add_up(ne, rows, top, at, place, info, refs[:-2], *refs[-2:])


def finish(ne, rows, outer, experts, place, info, *refs):
    columns, (best, counts_out, fits, *sums) = refs[:-6], refs[-5:]
    own = counts_out.shape[0]
    marks = [info[place[1] * ne + c, :, experts : experts + rows] for c in range(ne)]
    best[...] = jnp.concatenate(marks, axis=1).astype(jnp.int32).reshape(best.shape)
    add_up(ne, rows, 0, experts, place, info, columns, *sums)
    share = info.shape[0] // outer
    each = [jnp.sum(info[i * share : (i + 1) * share, :, :experts], axis=0) for i in range(outer)]
    largest = jnp.max(info[:, :, experts + rows : experts + rows + 1])
    fullest = jnp.max(functools.reduce(jnp.maximum, each))
    fits[0] = jnp.where(fullest * largest <= 256.0, 1, 0)
    counts = functools.reduce(jnp.add, each)
    expert_row = place[0] + lax.broadcasted_iota(jnp.int32, (own, experts), 0)
    lane = lax.broadcasted_iota(jnp.int32, (own, experts), 1)
    counts = jnp.sum(jnp.where(expert_row == lane, counts, 0.0), axis=1, keepdims=True)
    counts_out[...] = jnp.broadcast_to(jnp.maximum(counts, 1.0), counts_out.shape)


def settle(rows, experts, place, info, before, prices, counts, final, holder, same_counts):
    own = prices.shape[1]
    wide = (info.shape[2] - experts) // 2
    devices = info.shape[0]
    ids = (place[0] + lax.broadcasted_iota(jnp.int32, (own, rows), 0)).astype(jnp.float32)
    offset = lax.broadcasted_iota(jnp.int32, (own, rows), 1).astype(jnp.float32)

    def claimed(n):
        return ids == info[n, :, experts : experts + rows]

    def offered(n):
        return info[n, :, experts + wide : experts + wide + rows]

    def higher(n, top):
        return jnp.maximum(top, jnp.where(claimed(n), offered(n), -1.0))

    top = lax.fori_loop(0, devices, higher, jnp.full((own, rows), -1.0, jnp.float32), unroll=4)
    top = jnp.max(top, axis=1, keepdims=True)

    def earlier(n, first):
        token = (n * rows).astype(jnp.float32) + offset
        return jnp.minimum(first, jnp.where(claimed(n) & (offered(n) == top), token, far))

    first = lax.fori_loop(0, devices, earlier, jnp.full((own, rows), far, jnp.float32), unroll=4)
    first = jnp.min(first, axis=1, keepdims=True)
    same = lax.broadcasted_iota(jnp.int32, (own, own), 0) == lax.broadcasted_iota(jnp.int32, (own, own), 1)
    raised = jnp.sum(jnp.where(same, jnp.maximum(top, 0.0), 0.0), axis=0, keepdims=True)
    held = jnp.sum(jnp.where(same, jnp.where(top > 0, first, -1.0), 0.0), axis=0, keepdims=True)
    expert_row = place[0] + lax.broadcasted_iota(jnp.int32, (own, experts), 0)
    lane = lax.broadcasted_iota(jnp.int32, (own, experts), 1)
    so_far = jnp.sum(jnp.where(expert_row == lane, before[...], 0.0), axis=1, keepdims=True)
    so_far = jnp.sum(jnp.where(same, so_far, 0.0), axis=0, keepdims=True)
    final[...] = (prices[...] + so_far + raised).reshape(final.shape)
    holder[...] = held.astype(jnp.int32).reshape(holder.shape)


def blend(row, centroids, counts, *refs):
    sums, out = refs[:-1], refs[-1]
    rows, cols = out.shape
    total = functools.reduce(jnp.add, [s[...].astype(jnp.float32) for s in sums])
    old = centroids[row : row + rows, :].astype(jnp.float32)
    share = counts[row : row + rows, :1]
    out[...] = (0.5 * old + 0.5 * total / share).astype(out.dtype)


def assemble(plan, extras, base, *refs):
    pieces, out, sem = refs[: len(plan)], refs[-2 - extras], refs[-1]
    cols = pieces[0].shape[-1]
    copies = [
        pltpu.make_async_copy(refs[-2 - 2 * extras + i], refs[-1 - extras + i], sem.at[i])
        for i in range(extras)
    ]
    for piece, (row, slots) in zip(pieces, plan):
        for i, slot in enumerate(slots):
            col = pl.multiple_of(base[slot] * cols, cols)
            copies.append(
                pltpu.make_async_copy(
                    piece.at[i], out.at[pl.ds(row, piece.shape[1]), pl.ds(col, cols)], sem.at[len(copies)]
                )
            )
    for copy in copies:
        copy.start()
    for copy in copies:
        copy.wait()


PARTS = 2
TURNS = ((0, 1), (2, 1))


def spread_out(dp, inner, wide, sums, short, mine, counts, carried):
    bits = inner.bit_length() - 1
    member = lax.axis_index("dp") % inner
    core = lax.axis_index("expert")

    def move(value, masks):
        pairs = [(i * 2 + c, (i ^ masks[c]) * 2 + c) for i in range(dp) for c in range(2)]
        return lax.ppermute(value, ("dp", "expert"), pairs)

    parts = len(sums)
    cols = sums[0].shape[1]
    heights = [s.shape[0] for s in sums]
    tops = [sum(heights[:p]) for p in range(parts)]
    sent = sums if wide else short
    other = [move(s, (inner, inner)) for s in sent] if inner < dp else None
    held = []
    for p in range(parts):
        terms = [sums[p], other[p]] if other else [sums[p]]
        fresh = pl.pallas_call(
            functools.partial(blend, tops[p]),
            out_shape=jax.ShapeDtypeStruct((heights[p], cols), mine.dtype),
            in_specs=[VMEM] * (2 + len(terms)),
            out_specs=VMEM,
            compiler_params=room(4),
            name="blend",
        )(mine, counts, *terms)
        held.append([(fresh[None], [(0, 0)])])

    def join(values):
        return values[0] if len(values) == 1 else jnp.concatenate(values)

    late = [[] for _ in range(parts)]
    for stage in range(bits):
        for p in range(parts):
            masks = [1 << (stage + t) % bits for t in TURNS[p]]

            def onward(entries):
                where = [m for _, ms in entries for m in ms]
                value = move(join([v for v, _ in entries]), masks)
                return value, [(a ^ masks[0], b ^ masks[1]) for a, b in where]

            if stage < bits - 1 or stage < 2:
                held[p].append(onward(held[p]))
            else:
                late[p] = [onward(held[p][:-1]), onward(held[p][-1:])]
    def write(whole, groups, extras=()):
        pieces, plan, slots = [], [], []
        for p, group in enumerate(groups):
            for value, where in group:
                pieces.append(value)
                plan.append((tops[p], [len(slots) + i for i in range(len(where))]))
                slots += where
        base = jnp.stack([member ^ jnp.where(core == 0, a, b) for a, b in slots]).astype(jnp.int32)
        before = [] if whole is None else [whole]
        outs = pl.pallas_call(
            functools.partial(assemble, plan, len(extras)),
            out_shape=[jax.ShapeDtypeStruct((sum(heights), inner * cols), mine.dtype)]
            + [jax.ShapeDtypeStruct(e.shape, e.dtype) for e in extras],
            in_specs=[SMEM] + [VMEM] * len(pieces) + [ANY] * len(before) + [VMEM] * len(extras),
            out_specs=[ANY] + [pl.BlockSpec(memory_space=pltpu.HBM)] * len(extras),
            scratch_shapes=[pltpu.SemaphoreType.DMA((len(slots) + len(extras),))],
            input_output_aliases={1 + len(pieces): 0} if before else {},
            compiler_params=room(4),
            name="assemble",
        )(base, *pieces, *before, *extras)
        return outs if extras else outs[0]

    whole = write(None, held)
    for p in range(parts - 1):
        whole = write(whole, [late[p] if q == p else [] for q in range(parts)])
    return write(whole, [[]] * (parts - 1) + [late[-1]], carried)


def body(dp, ne, tokens, centroids, prices, epsilon):
    f32 = jnp.float32
    local_tokens, width = tokens.shape
    own = centroids.shape[0]
    experts = own * ne
    devices = dp * ne
    rows = local_tokens // ne
    cols = width // dp
    dp_at, expert_at = lax.axis_index("dp"), lax.axis_index("expert")
    everywhere = ("dp", "expert")
    outer = 2 if ne == 2 and dp % 16 == 0 and dp & (dp - 1) == 0 else 1
    inner = dp // outer
    cols = width // inner
    paired = outer == 2 and cols % 128 == 0 and own % 32 == 0
    swap = [(0, 1), (1, 0)]

    def shape(*sizes, dtype=f32):
        return jax.ShapeDtypeStruct(sizes, dtype)

    line, spread = shape(1, experts), shape(devices, 1, experts)
    at = jnp.stack([expert_at]).astype(jnp.int32)
    if paired:
        half = inner // 2
        chunks = 4
        masks = [(k, inner - 1 - k) for k in range(half)]
        theirs = [dp_at ^ jnp.where(expert_at == 0, *mask) for mask in masks]
        place = [expert_at, 1 - expert_at, dp_at % inner] + [t % inner for t in theirs]
        place = jnp.stack(place).astype(jnp.int32)
        kept, sent, mine, largest, *parcels = pl.pallas_call(
            functools.partial(opening, chunks),
            out_shape=[shape(rows, own)] * 2
            + [shape(own, cols, dtype=centroids.dtype), shape(1, 128)]
            + [shape(local_tokens, cols, dtype=tokens.dtype)] * half,
            in_specs=[SMEM, ANY, ANY, VMEM],
            out_specs=[VMEM] * (4 + half),
            scratch_shapes=[
                pltpu.VMEM(tokens.shape, tokens.dtype),
                pltpu.VMEM(centroids.shape, centroids.dtype),
                pltpu.VMEM((local_tokens, own), f32),
                pltpu.SemaphoreType.DMA((2, chunks)),
            ],
            compiler_params=room(52),
            name="opening",
        )(place, tokens, centroids, prices.reshape(1, own))
        received = lax.ppermute(sent, "expert", swap)
        values, bids = pl.pallas_call(
            first_round,
            out_shape=(shape(rows, experts), spread),
            in_specs=[SMEM, VMEM, VMEM, SMEM],
            out_specs=(VMEM, VMEM),
            compiler_params=room(4),
            name="first_round",
        )(at, kept, received, epsilon)
        columns = [None] * half

        def sent_on(k):
            pairs = [(i * 2 + c, (i ^ masks[k][c]) * 2 + c) for i in range(dp) for c in range(2)]
            columns[k] = lax.ppermute(parcels[k], everywhere, pairs)

        sources = theirs + [dp_at ^ jnp.where(expert_at == 0, *mask[::-1]) for mask in masks]
    else:
        parcels = tokens.reshape(local_tokens, dp, cols).transpose(1, 0, 2)
        columns = lax.all_to_all(parcels, "dp", 0, 0, tiled=True)
        columns = [columns.reshape(dp * local_tokens, cols)[i * local_tokens :][:local_tokens] for i in range(dp)]
        sources = list(range(dp))
        mine = lax.dynamic_slice_in_dim(centroids, dp_at * cols, cols, 1)
        largest = jnp.full((1, 128), jnp.max(jnp.abs(tokens)).astype(f32))
        part = lax.dot_general(
            tokens, centroids, (((1,), (1,)), ((), ())), preferred_element_type=f32
        ) * 0.015625 - prices
        part = lax.all_to_all(part, "expert", 0, 1, tiled=True)
        values, bids = pl.pallas_call(
            first_round_whole,
            out_shape=(shape(rows, experts), spread),
            in_specs=[SMEM, VMEM, SMEM],
            out_specs=(VMEM, VMEM),
            compiler_params=room(4),
            name="first_round",
        )(at, part, epsilon)

    total = jnp.zeros((1, experts), f32)
    waiting = list(range(half))[::-1] if paired else []
    for _ in range(ROUNDS - 2):
        for k in waiting[:-2]:
            sent_on(k)
        waiting = waiting[-2:]
        bids = lax.all_to_all(bids, everywhere, 0, 0, tiled=True)
        bids, total = pl.pallas_call(
            next_round,
            out_shape=(spread, line),
            in_specs=[VMEM, VMEM, SMEM, VMEM],
            out_specs=(VMEM, VMEM),
            compiler_params=room(4),
            name="next_round",
        )(values, total, epsilon, bids)
    if paired:
        parcels[: len(waiting)] = released(total, parcels[: len(waiting)])
    for k in waiting:
        sent_on(k)
    bids = lax.all_to_all(bids, everywhere, 0, 0, tiled=True)
    wide = (rows // 128 + 1) * 128
    largest = filled(total, largest, 8000000000)
    info, total = pl.pallas_call(
        last_round,
        out_shape=(shape(devices, 1, experts + 2 * wide), line),
        in_specs=[VMEM, VMEM, SMEM, VMEM, VMEM],
        out_specs=(VMEM, VMEM),
        compiler_params=room(8),
        name="last_round",
    )(values, total, epsilon, bids, largest)
    if paired:
        columns += [lax.ppermute(c, "expert", swap) for c in columns]
    info = lax.all_to_all(info, everywhere, 0, 0, tiled=True)

    timed = filled(total, largest, 8000000000)
    place = jnp.stack([expert_at * own, dp_at] + sources).astype(jnp.int32)
    low = own // 32 * 16 if own % 32 == 0 else own
    heights = [low, own - low] if paired else [own]

    def two(height):
        return (shape(height, cols), shape(height, cols, dtype=jnp.bfloat16))

    best, counts, fits, *sums = pl.pallas_call(
        functools.partial(finish, ne, rows, outer, experts),
        out_shape=(
            shape(local_tokens, dtype=jnp.int32),
            shape(own, 128),
            shape(1, dtype=jnp.int32),
        )
        + two(heights[0]),
        in_specs=[SMEM] + [VMEM] * (1 + len(columns)) + [ANY],
        out_specs=(VMEM, VMEM, SMEM, VMEM, VMEM),
        compiler_params=room(16),
        name="finish",
    )(place, info, *columns, timed)

    def settled(place, info, total, prices, counts):
        return pl.pallas_call(
            functools.partial(settle, rows, experts),
            out_shape=(shape(own), shape(own, dtype=jnp.int32), shape(own, 128)),
            in_specs=[SMEM, VMEM, VMEM, VMEM, ANY],
            out_specs=(VMEM, VMEM, ANY),
            input_output_aliases={4: 2},
            compiler_params=room(6),
            name="settle",
        )(place, info, total, prices, counts)

    prices = prices.reshape(1, own)
    if paired:

        def rest(wide, place, info, total, prices, columns, sums, mine, counts):
            more = pl.pallas_call(
                functools.partial(more_sums, ne, rows, heights[0], experts),
                out_shape=two(heights[1]),
                in_specs=[SMEM] + [VMEM] * (1 + len(columns)),
                out_specs=(VMEM, VMEM),
                compiler_params=room(8),
                name="more_sums",
            )(place, info, *columns)
            pairs = list(zip(sums, more))
            final, holder, counts = settled(place, info, total, prices, counts)
            pair = (final, holder)
            return spread_out(dp, inner, wide, pairs[0], pairs[1], mine, counts, pair)

        refreshed, final, holder = lax.switch(
            fits[0],
            [functools.partial(rest, True), functools.partial(rest, False)],
            place, info, total, prices, columns, sums, mine, counts,
        )
    else:
        final, holder, counts = settled(place, info, total, prices, counts)
        fresh = 0.5 * mine.astype(f32) + 0.5 * sums[0] / counts[:, :1]
        refreshed = lax.all_gather(fresh.astype(centroids.dtype), "dp", axis=1, tiled=True)
    return final, best, holder, refreshed


def solution(mesh):
    placed = (P("dp", None), P("expert", None), P("expert"), P())
    return jax.shard_map(
        functools.partial(body, mesh.shape["dp"], mesh.shape["expert"]),
        mesh=mesh,
        in_specs=placed,
        out_specs=(P("expert"), P("dp"), P("expert"), P("expert", None)),
        check_vma=False,
    )
```

```python
import functools

import jax
import jax.numpy as jnp
from jax import lax
from jax.experimental import pallas as pl
from jax.experimental.pallas import tpu as pltpu
from jax.sharding import PartitionSpec as P

ROUNDS = 3

lowest = -1e30
far = 1073741824.0
VMEM = pl.BlockSpec(memory_space=pltpu.VMEM)
SMEM = pl.BlockSpec(memory_space=pltpu.SMEM)
ANY = pl.BlockSpec(memory_space=pl.ANY)


def room(mebibytes):
    return pltpu.CompilerParams(vmem_limit_bytes=mebibytes * 1024 * 1024)


def opening(chunks, place, tokens, centroids, prices, kept, sent, mine, largest, *refs):
    parcels, (tok, cen, acc, sem) = refs[:-4], refs[-4:]
    rows, cols = kept.shape[0], mine.shape[1]
    step = tok.shape[1] // chunks
    copies = []
    for i in range(chunks):
        part = pl.ds(i * step, step)
        copies.append((
            pltpu.make_async_copy(centroids.at[:, part], cen.at[:, part], sem.at[0, i]),
            pltpu.make_async_copy(tokens.at[:, part], tok.at[:, part], sem.at[1, i]),
        ))
    for pair in copies:
        pair[0].start()
        pair[1].start()
    for i, pair in enumerate(copies):
        pair[0].wait()
        pair[1].wait()
        part = slice(i * step, (i + 1) * step)
        product = lax.dot_general(
            tok[:, part], cen[:, part], (((1,), (1,)), ((), ())), preferred_element_type=jnp.float32
        )
        size = jnp.max(jnp.abs(tok[:, part]).reshape(-1, 16, step), axis=0)
        peak = size if i == 0 else jnp.maximum(peak, size)
        if i:
            acc[...] += product
        else:
            acc[...] = product
    peak = jnp.max(peak.astype(jnp.float32), axis=0, keepdims=True)
    largest[...] = jnp.broadcast_to(jnp.max(peak, axis=1, keepdims=True), largest.shape)
    for out, at in ((sent, 1), (kept, 0)):
        row = pl.multiple_of(place[at] * rows, rows)
        out[...] = acc[pl.ds(row, rows), :] * 0.015625 - prices[...]
    mine[...] = cen[:, pl.ds(pl.multiple_of(place[2] * cols, cols), cols)]
    for k, parcel in enumerate(parcels):
        parcel[...] = tok[:, pl.ds(pl.multiple_of(place[3 + k] * cols, cols), cols)]


def choose(values, eps):
    ids = lax.broadcasted_iota(jnp.int32, values.shape, 1).astype(jnp.float32)
    top = jnp.max(values, axis=1, keepdims=True)
    choice = jnp.min(jnp.where(values == top, ids, far), axis=1, keepdims=True)
    claims = ids == choice
    second = jnp.max(jnp.where(claims, lowest, values), axis=1, keepdims=True)
    bid = top - second + eps
    bids = jnp.where(claims, bid, -1.0)
    return choice, claims, bid, bids, jnp.max(bids, axis=0, keepdims=True)


def first_round(place, kept, theirs, epsilon, values, out):
    if theirs is None:
        values[...] = kept[...]
    else:
        own = kept.shape[1]
        swapped = place[0] != 0
        values[:, :own] = jnp.where(swapped, theirs[...], kept[...])
        values[:, own:] = jnp.where(swapped, kept[...], theirs[...])
    raised = choose(values[...], epsilon[0])[-1]
    out[...] = jnp.broadcast_to(raised[None], out.shape)


def first_round_whole(place, kept, epsilon, values, out):
    first_round(place, kept, None, epsilon, values, out)


def next_round(values, before, epsilon, bids, out, after):
    total = before[...] + jnp.maximum(jnp.max(bids[...], axis=0), 0.0)
    after[...] = total
    raised = choose(values[...] - total, epsilon[0])[-1]
    out[...] = jnp.broadcast_to(raised[None], out.shape)


def last_round(values, before, epsilon, bids, largest, out, after):
    rows, experts = values.shape
    total = before[...] + jnp.maximum(jnp.max(bids[...], axis=0), 0.0)
    after[...] = total
    choice, claims, bid, _, _ = choose(values[...] - total, epsilon[0])
    count = jnp.sum(claims.astype(jnp.float32), axis=0, keepdims=True)
    wide = (out.shape[2] - experts) // 2
    lane = lax.broadcasted_iota(jnp.int32, (rows, wide), 1)
    same = lane == lax.broadcasted_iota(jnp.int32, (rows, wide), 0)
    choices = jnp.sum(jnp.where(same, choice, 0.0), axis=0, keepdims=True)
    choices = jnp.where(lane[:1] == rows, largest[:, :1], choices)
    offered = jnp.sum(jnp.where(same, bid, 0.0), axis=0, keepdims=True)
    line = jnp.concatenate([count, choices, offered], axis=1)
    out[...] = jnp.broadcast_to(line[None], out.shape)


def pass_on(line, *refs):
    pass


def released(line, parcels):
    return pl.pallas_call(
        pass_on,
        out_shape=[jax.ShapeDtypeStruct(p.shape, p.dtype) for p in parcels],
        in_specs=[ANY] * (1 + len(parcels)),
        out_specs=[ANY] * len(parcels),
        input_output_aliases={1 + i: i for i in range(len(parcels))},
        compiler_params=room(4),
        cost_estimate=pl.CostEstimate(flops=1000000000, bytes_accessed=4096, transcendentals=0),
        name="released",
    )(line, *parcels)


def fill(line, value, out):
    out[...] = value[...]


def filled(line, value, flops):
    return pl.pallas_call(
        fill,
        out_shape=jax.ShapeDtypeStruct(value.shape, value.dtype),
        in_specs=[ANY, VMEM],
        out_specs=VMEM,
        compiler_params=room(4),
        cost_estimate=pl.CostEstimate(flops=flops, bytes_accessed=4096, transcendentals=0),
        name="filled",
    )(line, value)


def add_up(ne, rows, top, at, place, info, columns, total_out, short_out):
    height = total_out.shape[0]
    ids = place[0] + top + lax.broadcasted_iota(jnp.int32, (height, rows), 0)
    ids = ids.astype(jnp.float32)
    total = jnp.zeros(total_out.shape, jnp.float32)
    for k, features in enumerate(columns):
        for c in range(ne):
            chosen = info[place[2 + k] * ne + c, :, at : at + rows]
            hot = jnp.where(ids == chosen, 1.0, 0.0).astype(jnp.bfloat16)
            total += jnp.dot(
                hot, features[c * rows : (c + 1) * rows, :], preferred_element_type=jnp.float32
            )
    total_out[...] = total
    short_out[...] = total.astype(short_out.dtype)


def finish(ne, rows, outer, experts, place, info, *refs):
    columns, (best, counts_out, fits, *sums) = refs[:-6], refs[-5:]
    own = counts_out.shape[0]
    marks = [info[place[1] * ne + c, :, experts : experts + rows] for c in range(ne)]
    best[...] = jnp.concatenate(marks, axis=1).astype(jnp.int32).reshape(best.shape)
    add_up(ne, rows, 0, experts, place, info, columns, *sums)
    share = info.shape[0] // outer
    each = [jnp.sum(info[i * share : (i + 1) * share, :, :experts], axis=0) for i in range(outer)]
    largest = jnp.max(info[:, :, experts + rows : experts + rows + 1])
    fullest = jnp.max(functools.reduce(jnp.maximum, each))
    fits[0] = jnp.where(fullest * largest <= 256.0, 1, 0)
    counts = functools.reduce(jnp.add, each)
    expert_row = place[0] + lax.broadcasted_iota(jnp.int32, (own, experts), 0)
    lane = lax.broadcasted_iota(jnp.int32, (own, experts), 1)
    counts = jnp.sum(jnp.where(expert_row == lane, counts, 0.0), axis=1, keepdims=True)
    counts_out[...] = jnp.broadcast_to(jnp.maximum(counts, 1.0), counts_out.shape)


def settle(rows, experts, place, info, before, prices, counts, final, holder, same_counts):
    own = prices.shape[1]
    wide = (info.shape[2] - experts) // 2
    devices = info.shape[0]
    ids = (place[0] + lax.broadcasted_iota(jnp.int32, (own, rows), 0)).astype(jnp.float32)
    offset = lax.broadcasted_iota(jnp.int32, (own, rows), 1).astype(jnp.float32)

    def claimed(n):
        return ids == info[n, :, experts : experts + rows]

    def offered(n):
        return info[n, :, experts + wide : experts + wide + rows]

    def higher(n, top):
        return jnp.maximum(top, jnp.where(claimed(n), offered(n), -1.0))

    top = lax.fori_loop(0, devices, higher, jnp.full((own, rows), -1.0, jnp.float32), unroll=4)
    top = jnp.max(top, axis=1, keepdims=True)

    def earlier(n, first):
        token = (n * rows).astype(jnp.float32) + offset
        return jnp.minimum(first, jnp.where(claimed(n) & (offered(n) == top), token, far))

    first = lax.fori_loop(0, devices, earlier, jnp.full((own, rows), far, jnp.float32), unroll=4)
    first = jnp.min(first, axis=1, keepdims=True)
    same = lax.broadcasted_iota(jnp.int32, (own, own), 0) == lax.broadcasted_iota(jnp.int32, (own, own), 1)
    raised = jnp.sum(jnp.where(same, jnp.maximum(top, 0.0), 0.0), axis=0, keepdims=True)
    held = jnp.sum(jnp.where(same, jnp.where(top > 0, first, -1.0), 0.0), axis=0, keepdims=True)
    expert_row = place[0] + lax.broadcasted_iota(jnp.int32, (own, experts), 0)
    lane = lax.broadcasted_iota(jnp.int32, (own, experts), 1)
    so_far = jnp.sum(jnp.where(expert_row == lane, before[...], 0.0), axis=1, keepdims=True)
    so_far = jnp.sum(jnp.where(same, so_far, 0.0), axis=0, keepdims=True)
    final[...] = (prices[...] + so_far + raised).reshape(final.shape)
    holder[...] = held.astype(jnp.int32).reshape(holder.shape)


def more_and_settle(ne, rows, top, experts, place, info, before, prices, *refs):
    columns, (total, short, final, holder) = refs[:-4], refs[-4:]
    add_up(ne, rows, top, experts, place, info, columns, total, short)
    settle(rows, experts, place, info, before, prices, None, final, holder, None)


def blend(row, centroids, counts, *refs):
    sums, out = refs[:-1], refs[-1]
    rows, cols = out.shape
    total = functools.reduce(jnp.add, [s[...].astype(jnp.float32) for s in sums])
    old = centroids[row : row + rows, :].astype(jnp.float32)
    share = counts[row : row + rows, :1]
    out[...] = (0.5 * old + 0.5 * total / share).astype(out.dtype)


def assemble(plan, extras, base, *refs):
    pieces, out, sem = refs[: len(plan)], refs[-2 - extras], refs[-1]
    cols = pieces[0].shape[-1]
    copies = [
        pltpu.make_async_copy(refs[-2 - 2 * extras + i], refs[-1 - extras + i], sem.at[i])
        for i in range(extras)
    ]
    for piece, (row, slots) in zip(pieces, plan):
        for i, slot in enumerate(slots):
            col = pl.multiple_of(base[slot] * cols, cols)
            copies.append(
                pltpu.make_async_copy(
                    piece.at[i], out.at[pl.ds(row, piece.shape[1]), pl.ds(col, cols)], sem.at[len(copies)]
                )
            )
    for copy in copies:
        copy.start()
    for copy in copies:
        copy.wait()


PARTS = 2
TURNS = ((0, 1), (2, 1))


def spread_out(dp, inner, wide, sums, short, mine, counts, carried):
    bits = inner.bit_length() - 1
    member = lax.axis_index("dp") % inner
    core = lax.axis_index("expert")

    def move(value, masks):
        pairs = [(i * 2 + c, (i ^ masks[c]) * 2 + c) for i in range(dp) for c in range(2)]
        return lax.ppermute(value, ("dp", "expert"), pairs)

    parts = len(sums)
    cols = sums[0].shape[1]
    heights = [s.shape[0] for s in sums]
    tops = [sum(heights[:p]) for p in range(parts)]
    sent = sums if wide else short
    other = [move(s, (inner, inner)) for s in sent] if inner < dp else None
    held = []
    for p in range(parts):
        terms = [sums[p], other[p]] if other else [sums[p]]
        fresh = pl.pallas_call(
            functools.partial(blend, tops[p]),
            out_shape=jax.ShapeDtypeStruct((heights[p], cols), mine.dtype),
            in_specs=[VMEM] * (2 + len(terms)),
            out_specs=VMEM,
            compiler_params=room(4),
            name="blend",
        )(mine, counts, *terms)
        held.append([(fresh[None], [(0, 0)])])

    def join(values):
        return values[0] if len(values) == 1 else jnp.concatenate(values)

    late = [[] for _ in range(parts)]
    for stage in range(bits):
        for p in range(parts):
            masks = [1 << (stage + t) % bits for t in TURNS[p]]

            def onward(entries):
                where = [m for _, ms in entries for m in ms]
                value = move(join([v for v, _ in entries]), masks)
                return value, [(a ^ masks[0], b ^ masks[1]) for a, b in where]

            if stage < bits - 1 or stage < 2:
                held[p].append(onward(held[p]))
            else:
                late[p] = [onward(held[p][:-1]), onward(held[p][-1:])]
    def write(whole, groups, extras=()):
        pieces, plan, slots = [], [], []
        for p, group in enumerate(groups):
            for value, where in group:
                pieces.append(value)
                plan.append((tops[p], [len(slots) + i for i in range(len(where))]))
                slots += where
        base = jnp.stack([member ^ jnp.where(core == 0, a, b) for a, b in slots]).astype(jnp.int32)
        before = [] if whole is None else [whole]
        outs = pl.pallas_call(
            functools.partial(assemble, plan, len(extras)),
            out_shape=[jax.ShapeDtypeStruct((sum(heights), inner * cols), mine.dtype)]
            + [jax.ShapeDtypeStruct(e.shape, e.dtype) for e in extras],
            in_specs=[SMEM] + [VMEM] * len(pieces) + [ANY] * len(before) + [VMEM] * len(extras),
            out_specs=[ANY] + [pl.BlockSpec(memory_space=pltpu.HBM)] * len(extras),
            scratch_shapes=[pltpu.SemaphoreType.DMA((len(slots) + len(extras),))],
            input_output_aliases={1 + len(pieces): 0} if before else {},
            compiler_params=room(4),
            name="assemble",
        )(base, *pieces, *before, *extras)
        return outs if extras else outs[0]

    whole = write(None, held)
    for p in range(parts - 1):
        whole = write(whole, [late[p] if q == p else [] for q in range(parts)])
    return write(whole, [[]] * (parts - 1) + [late[-1]], carried)


def body(dp, ne, tokens, centroids, prices, epsilon):
    f32 = jnp.float32
    local_tokens, width = tokens.shape
    own = centroids.shape[0]
    experts = own * ne
    devices = dp * ne
    rows = local_tokens // ne
    cols = width // dp
    dp_at, expert_at = lax.axis_index("dp"), lax.axis_index("expert")
    everywhere = ("dp", "expert")
    outer = 2 if ne == 2 and dp % 16 == 0 and dp & (dp - 1) == 0 else 1
    inner = dp // outer
    cols = width // inner
    paired = outer == 2 and cols % 128 == 0 and own % 32 == 0
    swap = [(0, 1), (1, 0)]

    def shape(*sizes, dtype=f32):
        return jax.ShapeDtypeStruct(sizes, dtype)

    line, spread = shape(1, experts), shape(devices, 1, experts)
    at = jnp.stack([expert_at]).astype(jnp.int32)
    if paired:
        half = inner // 2
        chunks = 4
        masks = [(k, inner - 1 - k) for k in range(half)]
        theirs = [dp_at ^ jnp.where(expert_at == 0, *mask) for mask in masks]
        place = [expert_at, 1 - expert_at, dp_at % inner] + [t % inner for t in theirs]
        place = jnp.stack(place).astype(jnp.int32)
        kept, sent, mine, largest, *parcels = pl.pallas_call(
            functools.partial(opening, chunks),
            out_shape=[shape(rows, own)] * 2
            + [shape(own, cols, dtype=centroids.dtype), shape(1, 128)]
            + [shape(local_tokens, cols, dtype=tokens.dtype)] * half,
            in_specs=[SMEM, ANY, ANY, VMEM],
            out_specs=[VMEM] * (4 + half),
            scratch_shapes=[
                pltpu.VMEM(tokens.shape, tokens.dtype),
                pltpu.VMEM(centroids.shape, centroids.dtype),
                pltpu.VMEM((local_tokens, own), f32),
                pltpu.SemaphoreType.DMA((2, chunks)),
            ],
            compiler_params=room(52),
            name="opening",
        )(place, tokens, centroids, prices.reshape(1, own))
        received = lax.ppermute(sent, "expert", swap)
        values, bids = pl.pallas_call(
            first_round,
            out_shape=(shape(rows, experts), spread),
            in_specs=[SMEM, VMEM, VMEM, SMEM],
            out_specs=(VMEM, VMEM),
            compiler_params=room(4),
            name="first_round",
        )(at, kept, received, epsilon)
        columns = [None] * half

        def sent_on(k):
            pairs = [(i * 2 + c, (i ^ masks[k][c]) * 2 + c) for i in range(dp) for c in range(2)]
            columns[k] = lax.ppermute(parcels[k], everywhere, pairs)

        sources = theirs + [dp_at ^ jnp.where(expert_at == 0, *mask[::-1]) for mask in masks]
    else:
        parcels = tokens.reshape(local_tokens, dp, cols).transpose(1, 0, 2)
        columns = lax.all_to_all(parcels, "dp", 0, 0, tiled=True)
        columns = [columns.reshape(dp * local_tokens, cols)[i * local_tokens :][:local_tokens] for i in range(dp)]
        sources = list(range(dp))
        mine = lax.dynamic_slice_in_dim(centroids, dp_at * cols, cols, 1)
        largest = jnp.full((1, 128), jnp.max(jnp.abs(tokens)).astype(f32))
        part = lax.dot_general(
            tokens, centroids, (((1,), (1,)), ((), ())), preferred_element_type=f32
        ) * 0.015625 - prices
        part = lax.all_to_all(part, "expert", 0, 1, tiled=True)
        values, bids = pl.pallas_call(
            first_round_whole,
            out_shape=(shape(rows, experts), spread),
            in_specs=[SMEM, VMEM, SMEM],
            out_specs=(VMEM, VMEM),
            compiler_params=room(4),
            name="first_round",
        )(at, part, epsilon)

    total = jnp.zeros((1, experts), f32)
    waiting = list(range(half))[::-1] if paired else []
    for _ in range(ROUNDS - 2):
        for k in waiting[:-2]:
            sent_on(k)
        waiting = waiting[-2:]
        bids = lax.all_to_all(bids, everywhere, 0, 0, tiled=True)
        bids, total = pl.pallas_call(
            next_round,
            out_shape=(spread, line),
            in_specs=[VMEM, VMEM, SMEM, VMEM],
            out_specs=(VMEM, VMEM),
            compiler_params=room(4),
            name="next_round",
        )(values, total, epsilon, bids)
    if paired:
        parcels[: len(waiting)] = released(total, parcels[: len(waiting)])
    for k in waiting:
        sent_on(k)
    bids = lax.all_to_all(bids, everywhere, 0, 0, tiled=True)
    wide = (rows // 128 + 1) * 128
    largest = filled(total, largest, 8000000000)
    info, total = pl.pallas_call(
        last_round,
        out_shape=(shape(devices, 1, experts + 2 * wide), line),
        in_specs=[VMEM, VMEM, SMEM, VMEM, VMEM],
        out_specs=(VMEM, VMEM),
        compiler_params=room(8),
        name="last_round",
    )(values, total, epsilon, bids, largest)
    if paired:
        columns += [lax.ppermute(c, "expert", swap) for c in columns]
    info = lax.all_to_all(info, everywhere, 0, 0, tiled=True)

    timed = filled(total, largest, 8000000000)
    place = jnp.stack([expert_at * own, dp_at] + sources).astype(jnp.int32)
    low = own // 32 * 16 if own % 32 == 0 else own
    heights = [low, own - low] if paired else [own]

    def two(height):
        return (shape(height, cols), shape(height, cols, dtype=jnp.bfloat16))

    best, counts, fits, *sums = pl.pallas_call(
        functools.partial(finish, ne, rows, outer, experts),
        out_shape=(
            shape(local_tokens, dtype=jnp.int32),
            shape(own, 128),
            shape(1, dtype=jnp.int32),
        )
        + two(heights[0]),
        in_specs=[SMEM] + [VMEM] * (1 + len(columns)) + [ANY],
        out_specs=(VMEM, VMEM, SMEM, VMEM, VMEM),
        compiler_params=room(16),
        name="finish",
    )(place, info, *columns, timed)

    def settled(place, info, total, prices, counts):
        return pl.pallas_call(
            functools.partial(settle, rows, experts),
            out_shape=(shape(own), shape(own, dtype=jnp.int32), shape(own, 128)),
            in_specs=[SMEM, VMEM, VMEM, VMEM, ANY],
            out_specs=(VMEM, VMEM, ANY),
            input_output_aliases={4: 2},
            compiler_params=room(6),
            name="settle",
        )(place, info, total, prices, counts)

    prices = prices.reshape(1, own)
    if paired:

        def rest(wide, place, info, total, prices, columns, sums, mine, counts):
            *more, final, holder = pl.pallas_call(
                functools.partial(more_and_settle, ne, rows, heights[0], experts),
                out_shape=two(heights[1]) + (shape(own), shape(own, dtype=jnp.int32)),
                in_specs=[SMEM] + [VMEM] * (3 + len(columns)),
                out_specs=(VMEM,) * 4,
                compiler_params=room(8),
                name="more_sums",
            )(place, info, total, prices, *columns)
            pairs = list(zip(sums, more))
            pair = (final, holder)
            return spread_out(dp, inner, wide, pairs[0], pairs[1], mine, counts, pair)

        refreshed, final, holder = lax.switch(
            fits[0],
            [functools.partial(rest, True), functools.partial(rest, False)],
            place, info, total, prices, columns, sums, mine, counts,
        )
    else:
        final, holder, counts = settled(place, info, total, prices, counts)
        fresh = 0.5 * mine.astype(f32) + 0.5 * sums[0] / counts[:, :1]
        refreshed = lax.all_gather(fresh.astype(centroids.dtype), "dp", axis=1, tiled=True)
    return final, best, holder, refreshed


def solution(mesh):
    placed = (P("dp", None), P("expert", None), P("expert"), P())
    return jax.shard_map(
        functools.partial(body, mesh.shape["dp"], mesh.shape["expert"]),
        mesh=mesh,
        in_specs=placed,
        out_specs=(P("expert"), P("dp"), P("expert"), P("expert", None)),
        check_vma=False,
    )
```

```python
import functools

import jax
import jax.numpy as jnp
from jax import lax
from jax.experimental import pallas as pl
from jax.experimental.pallas import tpu as pltpu
from jax.sharding import PartitionSpec as P

ROUNDS = 3

lowest = -1e30
far = 1073741824.0
VMEM = pl.BlockSpec(memory_space=pltpu.VMEM)
SMEM = pl.BlockSpec(memory_space=pltpu.SMEM)
ANY = pl.BlockSpec(memory_space=pl.ANY)


def room(mebibytes):
    return pltpu.CompilerParams(vmem_limit_bytes=mebibytes * 1024 * 1024)


def opening(chunks, place, tokens, centroids, prices, kept, sent, mine, largest, *refs):
    parcels, (tok, cen, acc, sem) = refs[:-4], refs[-4:]
    rows, cols = kept.shape[0], mine.shape[1]
    step = tok.shape[1] // chunks
    copies = []
    for i in range(chunks):
        part = pl.ds(i * step, step)
        copies.append((
            pltpu.make_async_copy(centroids.at[:, part], cen.at[:, part], sem.at[0, i]),
            pltpu.make_async_copy(tokens.at[:, part], tok.at[:, part], sem.at[1, i]),
        ))
    for pair in copies:
        pair[0].start()
        pair[1].start()
    for i, pair in enumerate(copies):
        pair[0].wait()
        pair[1].wait()
        part = slice(i * step, (i + 1) * step)
        product = lax.dot_general(
            tok[:, part], cen[:, part], (((1,), (1,)), ((), ())), preferred_element_type=jnp.float32
        )
        size = jnp.max(jnp.abs(tok[:, part]).reshape(-1, 16, step), axis=0)
        peak = size if i == 0 else jnp.maximum(peak, size)
        if i:
            acc[...] += product
        else:
            acc[...] = product
    peak = jnp.max(peak.astype(jnp.float32), axis=0, keepdims=True)
    largest[...] = jnp.broadcast_to(jnp.max(peak, axis=1, keepdims=True), largest.shape)
    for out, at in ((sent, 1), (kept, 0)):
        row = pl.multiple_of(place[at] * rows, rows)
        out[...] = acc[pl.ds(row, rows), :] * 0.015625 - prices[...]
    mine[...] = cen[:, pl.ds(pl.multiple_of(place[2] * cols, cols), cols)]
    for k, parcel in enumerate(parcels):
        parcel[...] = tok[:, pl.ds(pl.multiple_of(place[3 + k] * cols, cols), cols)]


def choose(values, eps):
    ids = lax.broadcasted_iota(jnp.int32, values.shape, 1).astype(jnp.float32)
    top = jnp.max(values, axis=1, keepdims=True)
    choice = jnp.min(jnp.where(values == top, ids, far), axis=1, keepdims=True)
    claims = ids == choice
    second = jnp.max(jnp.where(claims, lowest, values), axis=1, keepdims=True)
    bid = top - second + eps
    bids = jnp.where(claims, bid, -1.0)
    return choice, claims, bid, bids, jnp.max(bids, axis=0, keepdims=True)


def first_round(place, kept, theirs, epsilon, values, out):
    if theirs is None:
        values[...] = kept[...]
    else:
        own = kept.shape[1]
        swapped = place[0] != 0
        values[:, :own] = jnp.where(swapped, theirs[...], kept[...])
        values[:, own:] = jnp.where(swapped, kept[...], theirs[...])
    raised = choose(values[...], epsilon[0])[-1]
    out[...] = jnp.broadcast_to(raised[None], out.shape)


def first_round_whole(place, kept, epsilon, values, out):
    first_round(place, kept, None, epsilon, values, out)


def next_round(values, before, epsilon, bids, out, after):
    total = before[...] + jnp.maximum(jnp.max(bids[...], axis=0), 0.0)
    after[...] = total
    raised = choose(values[...] - total, epsilon[0])[-1]
    out[...] = jnp.broadcast_to(raised[None], out.shape)


def last_round(values, before, epsilon, bids, largest, out, after):
    rows, experts = values.shape
    total = before[...] + jnp.maximum(jnp.max(bids[...], axis=0), 0.0)
    after[...] = total
    choice, claims, bid, _, _ = choose(values[...] - total, epsilon[0])
    count = jnp.sum(claims.astype(jnp.float32), axis=0, keepdims=True)
    wide = (out.shape[2] - experts) // 2
    lane = lax.broadcasted_iota(jnp.int32, (rows, wide), 1)
    same = lane == lax.broadcasted_iota(jnp.int32, (rows, wide), 0)
    choices = jnp.sum(jnp.where(same, choice, 0.0), axis=0, keepdims=True)
    choices = jnp.where(lane[:1] == rows, largest[:, :1], choices)
    offered = jnp.sum(jnp.where(same, bid, 0.0), axis=0, keepdims=True)
    line = jnp.concatenate([count, choices, offered], axis=1)
    out[...] = jnp.broadcast_to(line[None], out.shape)


def pass_on(line, *refs):
    pass


def released(line, parcels):
    return pl.pallas_call(
        pass_on,
        out_shape=[jax.ShapeDtypeStruct(p.shape, p.dtype) for p in parcels],
        in_specs=[ANY] * (1 + len(parcels)),
        out_specs=[ANY] * len(parcels),
        input_output_aliases={1 + i: i for i in range(len(parcels))},
        compiler_params=room(4),
        cost_estimate=pl.CostEstimate(flops=1000000000, bytes_accessed=4096, transcendentals=0),
        name="released",
    )(line, *parcels)


def fill(line, value, out):
    out[...] = value[...]


def filled(line, value, flops):
    return pl.pallas_call(
        fill,
        out_shape=jax.ShapeDtypeStruct(value.shape, value.dtype),
        in_specs=[ANY, VMEM],
        out_specs=VMEM,
        compiler_params=room(4),
        cost_estimate=pl.CostEstimate(flops=flops, bytes_accessed=4096, transcendentals=0),
        name="filled",
    )(line, value)


def add_up(ne, rows, top, at, place, info, columns, total_out, short_out):
    height = total_out.shape[0]
    ids = place[0] + top + lax.broadcasted_iota(jnp.int32, (height, rows), 0)
    ids = ids.astype(jnp.float32)
    total = jnp.zeros(total_out.shape, jnp.float32)
    for k, features in enumerate(columns):
        for c in range(ne):
            chosen = info[place[2 + k] * ne + c, :, at : at + rows]
            hot = jnp.where(ids == chosen, 1.0, 0.0).astype(jnp.bfloat16)
            total += jnp.dot(
                hot, features[c * rows : (c + 1) * rows, :], preferred_element_type=jnp.float32
            )
    total_out[...] = total
    short_out[...] = total.astype(short_out.dtype)


def more_sums(ne, rows, top, at, place, info, *refs):
    add_up(ne, rows, top, at, place, info, refs[:-2], *refs[-2:])


def finish(ne, rows, outer, experts, place, info, *refs):
    columns, (best, counts_out, fits, *sums) = refs[:-6], refs[-5:]
    own = counts_out.shape[0]
    marks = [info[place[1] * ne + c, :, experts : experts + rows] for c in range(ne)]
    best[...] = jnp.concatenate(marks, axis=1).astype(jnp.int32).reshape(best.shape)
    add_up(ne, rows, 0, experts, place, info, columns, *sums)
    share = info.shape[0] // outer
    each = [jnp.sum(info[i * share : (i + 1) * share, :, :experts], axis=0) for i in range(outer)]
    largest = jnp.max(info[:, :, experts + rows : experts + rows + 1])
    fullest = jnp.max(functools.reduce(jnp.maximum, each))
    fits[0] = jnp.where(fullest * largest <= 256.0, 1, 0)
    counts = functools.reduce(jnp.add, each)
    expert_row = place[0] + lax.broadcasted_iota(jnp.int32, (own, experts), 0)
    lane = lax.broadcasted_iota(jnp.int32, (own, experts), 1)
    counts = jnp.sum(jnp.where(expert_row == lane, counts, 0.0), axis=1, keepdims=True)
    counts_out[...] = jnp.broadcast_to(jnp.maximum(counts, 1.0), counts_out.shape)


def settle(rows, experts, place, info, before, prices, counts, final, holder, same_counts):
    own = prices.shape[1]
    wide = (info.shape[2] - experts) // 2
    devices = info.shape[0]
    ids = (place[0] + lax.broadcasted_iota(jnp.int32, (own, rows), 0)).astype(jnp.float32)
    offset = lax.broadcasted_iota(jnp.int32, (own, rows), 1).astype(jnp.float32)

    def claimed(n):
        return ids == info[n, :, experts : experts + rows]

    def offered(n):
        return info[n, :, experts + wide : experts + wide + rows]

    def higher(n, top):
        return jnp.maximum(top, jnp.where(claimed(n), offered(n), -1.0))

    top = lax.fori_loop(0, devices, higher, jnp.full((own, rows), -1.0, jnp.float32), unroll=4)
    top = jnp.max(top, axis=1, keepdims=True)

    def earlier(n, first):
        token = (n * rows).astype(jnp.float32) + offset
        return jnp.minimum(first, jnp.where(claimed(n) & (offered(n) == top), token, far))

    first = lax.fori_loop(0, devices, earlier, jnp.full((own, rows), far, jnp.float32), unroll=4)
    first = jnp.min(first, axis=1, keepdims=True)
    same = lax.broadcasted_iota(jnp.int32, (own, own), 0) == lax.broadcasted_iota(jnp.int32, (own, own), 1)
    raised = jnp.sum(jnp.where(same, jnp.maximum(top, 0.0), 0.0), axis=0, keepdims=True)
    held = jnp.sum(jnp.where(same, jnp.where(top > 0, first, -1.0), 0.0), axis=0, keepdims=True)
    expert_row = place[0] + lax.broadcasted_iota(jnp.int32, (own, experts), 0)
    lane = lax.broadcasted_iota(jnp.int32, (own, experts), 1)
    so_far = jnp.sum(jnp.where(expert_row == lane, before[...], 0.0), axis=1, keepdims=True)
    so_far = jnp.sum(jnp.where(same, so_far, 0.0), axis=0, keepdims=True)
    final[...] = (prices[...] + so_far + raised).reshape(final.shape)
    holder[...] = held.astype(jnp.int32).reshape(holder.shape)


def blend(row, centroids, counts, *refs):
    sums, out = refs[:-1], refs[-1]
    rows, cols = out.shape
    total = functools.reduce(jnp.add, [s[...].astype(jnp.float32) for s in sums])
    old = centroids[row : row + rows, :].astype(jnp.float32)
    share = counts[row : row + rows, :1]
    out[...] = (0.5 * old + 0.5 * total / share).astype(out.dtype)


def assemble(plan, extras, base, *refs):
    pieces, out, sem = refs[: len(plan)], refs[-2 - extras], refs[-1]
    cols = pieces[0].shape[-1]
    copies = [
        pltpu.make_async_copy(refs[-2 - 2 * extras + i], refs[-1 - extras + i], sem.at[i])
        for i in range(extras)
    ]
    for piece, (row, slots) in zip(pieces, plan):
        for i, slot in enumerate(slots):
            col = pl.multiple_of(base[slot] * cols, cols)
            copies.append(
                pltpu.make_async_copy(
                    piece.at[i], out.at[pl.ds(row, piece.shape[1]), pl.ds(col, cols)], sem.at[len(copies)]
                )
            )
    for copy in copies:
        copy.start()
    for copy in copies:
        copy.wait()


PARTS = 2
TURNS = ((0, 1), (0, 2))


def spread_out(dp, inner, wide, sums, short, mine, counts, carried):
    bits = inner.bit_length() - 1
    member = lax.axis_index("dp") % inner
    core = lax.axis_index("expert")

    def move(value, masks):
        pairs = [(i * 2 + c, (i ^ masks[c]) * 2 + c) for i in range(dp) for c in range(2)]
        return lax.ppermute(value, ("dp", "expert"), pairs)

    parts = len(sums)
    cols = sums[0].shape[1]
    heights = [s.shape[0] for s in sums]
    tops = [sum(heights[:p]) for p in range(parts)]
    sent = sums if wide else short
    other = [move(s, (inner, inner)) for s in sent] if inner < dp else None
    held = []
    for p in range(parts):
        terms = [sums[p], other[p]] if other else [sums[p]]
        fresh = pl.pallas_call(
            functools.partial(blend, tops[p]),
            out_shape=jax.ShapeDtypeStruct((heights[p], cols), mine.dtype),
            in_specs=[VMEM] * (2 + len(terms)),
            out_specs=VMEM,
            compiler_params=room(4),
            name="blend",
        )(mine, counts, *terms)
        held.append([(fresh[None], [(0, 0)])])

    def join(values):
        return values[0] if len(values) == 1 else jnp.concatenate(values)

    late = [[] for _ in range(parts)]
    for stage in range(bits):
        for p in range(parts):
            masks = [1 << (stage + t) % bits for t in TURNS[p]]

            def onward(entries):
                where = [m for _, ms in entries for m in ms]
                value = move(join([v for v, _ in entries]), masks)
                return value, [(a ^ masks[0], b ^ masks[1]) for a, b in where]

            if stage < bits - 1 or stage < 2:
                held[p].append(onward(held[p]))
            else:
                late[p] = [onward(held[p][:-1]), onward(held[p][-1:])]
    def write(whole, groups, extras=()):
        pieces, plan, slots = [], [], []
        for p, group in enumerate(groups):
            for value, where in group:
                pieces.append(value)
                plan.append((tops[p], [len(slots) + i for i in range(len(where))]))
                slots += where
        base = jnp.stack([member ^ jnp.where(core == 0, a, b) for a, b in slots]).astype(jnp.int32)
        before = [] if whole is None else [whole]
        outs = pl.pallas_call(
            functools.partial(assemble, plan, len(extras)),
            out_shape=[jax.ShapeDtypeStruct((sum(heights), inner * cols), mine.dtype)]
            + [jax.ShapeDtypeStruct(e.shape, e.dtype) for e in extras],
            in_specs=[SMEM] + [VMEM] * len(pieces) + [ANY] * len(before) + [VMEM] * len(extras),
            out_specs=[ANY] + [pl.BlockSpec(memory_space=pltpu.HBM)] * len(extras),
            scratch_shapes=[pltpu.SemaphoreType.DMA((len(slots) + len(extras),))],
            input_output_aliases={1 + len(pieces): 0} if before else {},
            compiler_params=room(4),
            name="assemble",
        )(base, *pieces, *before, *extras)
        return outs if extras else outs[0]

    whole = write(None, held)
    for p in range(parts - 1):
        whole = write(whole, [late[p] if q == p else [] for q in range(parts)])
    return write(whole, [[]] * (parts - 1) + [late[-1]], carried)


def body(dp, ne, tokens, centroids, prices, epsilon):
    f32 = jnp.float32
    local_tokens, width = tokens.shape
    own = centroids.shape[0]
    experts = own * ne
    devices = dp * ne
    rows = local_tokens // ne
    cols = width // dp
    dp_at, expert_at = lax.axis_index("dp"), lax.axis_index("expert")
    everywhere = ("dp", "expert")
    outer = 2 if ne == 2 and dp % 16 == 0 and dp & (dp - 1) == 0 else 1
    inner = dp // outer
    cols = width // inner
    paired = outer == 2 and cols % 128 == 0 and own % 32 == 0
    swap = [(0, 1), (1, 0)]

    def shape(*sizes, dtype=f32):
        return jax.ShapeDtypeStruct(sizes, dtype)

    line, spread = shape(1, experts), shape(devices, 1, experts)
    at = jnp.stack([expert_at]).astype(jnp.int32)
    if paired:
        half = inner // 2
        chunks = 4
        masks = [(k, inner - 1 - k) for k in range(half)]
        theirs = [dp_at ^ jnp.where(expert_at == 0, *mask) for mask in masks]
        place = [expert_at, 1 - expert_at, dp_at % inner] + [t % inner for t in theirs]
        place = jnp.stack(place).astype(jnp.int32)
        kept, sent, mine, largest, *parcels = pl.pallas_call(
            functools.partial(opening, chunks),
            out_shape=[shape(rows, own)] * 2
            + [shape(own, cols, dtype=centroids.dtype), shape(1, 128)]
            + [shape(local_tokens, cols, dtype=tokens.dtype)] * half,
            in_specs=[SMEM, ANY, ANY, VMEM],
            out_specs=[VMEM] * (4 + half),
            scratch_shapes=[
                pltpu.VMEM(tokens.shape, tokens.dtype),
                pltpu.VMEM(centroids.shape, centroids.dtype),
                pltpu.VMEM((local_tokens, own), f32),
                pltpu.SemaphoreType.DMA((2, chunks)),
            ],
            compiler_params=room(52),
            name="opening",
        )(place, tokens, centroids, prices.reshape(1, own))
        received = lax.ppermute(sent, "expert", swap)
        values, bids = pl.pallas_call(
            first_round,
            out_shape=(shape(rows, experts), spread),
            in_specs=[SMEM, VMEM, VMEM, SMEM],
            out_specs=(VMEM, VMEM),
            compiler_params=room(4),
            name="first_round",
        )(at, kept, received, epsilon)
        columns = [None] * half

        def sent_on(k):
            pairs = [(i * 2 + c, (i ^ masks[k][c]) * 2 + c) for i in range(dp) for c in range(2)]
            columns[k] = lax.ppermute(parcels[k], everywhere, pairs)

        sources = theirs + [dp_at ^ jnp.where(expert_at == 0, *mask[::-1]) for mask in masks]
    else:
        parcels = tokens.reshape(local_tokens, dp, cols).transpose(1, 0, 2)
        columns = lax.all_to_all(parcels, "dp", 0, 0, tiled=True)
        columns = [columns.reshape(dp * local_tokens, cols)[i * local_tokens :][:local_tokens] for i in range(dp)]
        sources = list(range(dp))
        mine = lax.dynamic_slice_in_dim(centroids, dp_at * cols, cols, 1)
        largest = jnp.full((1, 128), jnp.max(jnp.abs(tokens)).astype(f32))
        part = lax.dot_general(
            tokens, centroids, (((1,), (1,)), ((), ())), preferred_element_type=f32
        ) * 0.015625 - prices
        part = lax.all_to_all(part, "expert", 0, 1, tiled=True)
        values, bids = pl.pallas_call(
            first_round_whole,
            out_shape=(shape(rows, experts), spread),
            in_specs=[SMEM, VMEM, SMEM],
            out_specs=(VMEM, VMEM),
            compiler_params=room(4),
            name="first_round",
        )(at, part, epsilon)

    total = jnp.zeros((1, experts), f32)
    waiting = list(range(half))[::-1] if paired else []
    for _ in range(ROUNDS - 2):
        for k in waiting[:-2]:
            sent_on(k)
        waiting = waiting[-2:]
        bids = lax.all_to_all(bids, everywhere, 0, 0, tiled=True)
        bids, total = pl.pallas_call(
            next_round,
            out_shape=(spread, line),
            in_specs=[VMEM, VMEM, SMEM, VMEM],
            out_specs=(VMEM, VMEM),
            compiler_params=room(4),
            name="next_round",
        )(values, total, epsilon, bids)
    if paired:
        parcels[: len(waiting)] = released(total, parcels[: len(waiting)])
    for k in waiting:
        sent_on(k)
    bids = lax.all_to_all(bids, everywhere, 0, 0, tiled=True)
    wide = (rows // 128 + 1) * 128
    largest = filled(total, largest, 8000000000)
    info, total = pl.pallas_call(
        last_round,
        out_shape=(shape(devices, 1, experts + 2 * wide), line),
        in_specs=[VMEM, VMEM, SMEM, VMEM, VMEM],
        out_specs=(VMEM, VMEM),
        compiler_params=room(8),
        name="last_round",
    )(values, total, epsilon, bids, largest)
    if paired:
        columns += [lax.ppermute(c, "expert", swap) for c in columns]
    info = lax.all_to_all(info, everywhere, 0, 0, tiled=True)

    timed = filled(total, largest, 8000000000)
    place = jnp.stack([expert_at * own, dp_at] + sources).astype(jnp.int32)
    low = own // 32 * 16 if own % 32 == 0 else own
    heights = [low, own - low] if paired else [own]

    def two(height):
        return (shape(height, cols), shape(height, cols, dtype=jnp.bfloat16))

    best, counts, fits, *sums = pl.pallas_call(
        functools.partial(finish, ne, rows, outer, experts),
        out_shape=(
            shape(local_tokens, dtype=jnp.int32),
            shape(own, 128),
            shape(1, dtype=jnp.int32),
        )
        + two(heights[0]),
        in_specs=[SMEM] + [VMEM] * (1 + len(columns)) + [ANY],
        out_specs=(VMEM, VMEM, SMEM, VMEM, VMEM),
        compiler_params=room(16),
        name="finish",
    )(place, info, *columns, timed)

    def settled(place, info, total, prices, counts):
        return pl.pallas_call(
            functools.partial(settle, rows, experts),
            out_shape=(shape(own), shape(own, dtype=jnp.int32), shape(own, 128)),
            in_specs=[SMEM, VMEM, VMEM, VMEM, ANY],
            out_specs=(VMEM, VMEM, ANY),
            input_output_aliases={4: 2},
            compiler_params=room(6),
            name="settle",
        )(place, info, total, prices, counts)

    prices = prices.reshape(1, own)
    if paired:

        def rest(wide, place, info, total, prices, columns, sums, mine, counts):
            more = pl.pallas_call(
                functools.partial(more_sums, ne, rows, heights[0], experts),
                out_shape=two(heights[1]),
                in_specs=[SMEM] + [VMEM] * (1 + len(columns)),
                out_specs=(VMEM, VMEM),
                compiler_params=room(8),
                name="more_sums",
            )(place, info, *columns)
            pairs = list(zip(sums, more))
            final, holder, counts = settled(place, info, total, prices, counts)
            pair = (final, holder)
            return spread_out(dp, inner, wide, pairs[0], pairs[1], mine, counts, pair)

        refreshed, final, holder = lax.switch(
            fits[0],
            [functools.partial(rest, True), functools.partial(rest, False)],
            place, info, total, prices, columns, sums, mine, counts,
        )
    else:
        final, holder, counts = settled(place, info, total, prices, counts)
        fresh = 0.5 * mine.astype(f32) + 0.5 * sums[0] / counts[:, :1]
        refreshed = lax.all_gather(fresh.astype(centroids.dtype), "dp", axis=1, tiled=True)
    return final, best, holder, refreshed


def solution(mesh):
    placed = (P("dp", None), P("expert", None), P("expert"), P())
    return jax.shard_map(
        functools.partial(body, mesh.shape["dp"], mesh.shape["expert"]),
        mesh=mesh,
        in_specs=placed,
        out_specs=(P("expert"), P("dp"), P("expert"), P("expert", None)),
        check_vma=False,
    )
```
